512 devices in a mesh: dp: 64 (over z, y), tensor: 8 (over x, core).
Axes of the slice: x: 4, y: 4, z: 16, core: 2. Of those that a mesh axis runs over, the one named last changes fastest.
Arguments:
- post_deter: bfloat16 [16384, 4096], P('dp', 'tensor'), may hold values from -1 to 1
- post_sample: int32 [16384, 32], P('dp'), may hold values from 0 to 31
- samples: int32 [2, 16384, 32], P(None, 'dp'), may hold values from 0 to 31
- actions: int32 [2, 16384], P(None, 'dp'), may hold values from 0 to 17
- counts: int32 [256], P('dp'), may hold values from 1 to 64, 8192 in all
- w_stoch: bfloat16 [1024, 1024], P(None, 'tensor'), may hold values from -1 to 1
- w_action: bfloat16 [18, 1024], P(None, 'tensor'), may hold values from -6 to 6
- w_gate: bfloat16 [1024, 12288], P('dp', 'tensor'), may hold values from -0.1875 to 0.1875
- w_rec: bfloat16 [8, 512, 1536], P('tensor'), may hold values from -0.25 to 0.25
- w_prior_in: bfloat16 [4096, 1024], P('tensor'), may hold values from -0.09375 to 0.09375
- w_prior_out: bfloat16 [1024, 1024], P(None, 'tensor'), may hold values from -8 to 8
Outputs:
- deter_out: bfloat16 [16384, 4096], P('dp', 'tensor')
- log_prob: float32 [2, 16384], P(None, 'dp')
The draws below stay inside these ranges and needn't reach their ends.
Inputs may be any that keep to these rules, and one draw needn't show every extreme that they name: Every sequence has at least one valid start; the counts of all sequences sum to 8192 and the largest is 64.
All inputs are finite; a program needn't handle non-finite values. No bound on the sum of `counts` on one device may be relied on, other than what follows from the above.
Results may differ from the reference program's by a relative error of at most 0.0051.
Values may be sent and summed in bfloat16 or wider, within the bound.
No kernel may reach another device: no remote copies, remote signals or barrier semaphores. Data moves between devices by JAX's collectives and lax.ppermute only.
A program may use at most 64 MiB of HBM per device.

```python
import math
import jax
import jax.numpy as jnp
import numpy as np
from jax import lax

DETER = 4096
BLOCKS = 8
BW = 512
STOCH = 32
CLASSES = 32
LAT = 1024
UNITS = 1024
ACTIONS = 18
STEPS = 64
SEQ_DEV = 4
IMAG = 2
STARTS_DEV = 256
SEQS = 256
STARTS = 16384
N_DP = 64


def draw_w_prior_out(key, part):
    key = jax.random.fold_in(key, 7)
    first, second = jax.random.split(key)
    base = jax.random.normal(first, (UNITS, LAT), jnp.float32) * UNITS ** (-0.5)
    column = jnp.exp(jax.random.uniform(second, (1, LAT), jnp.float32, 0.0, math.log(10.0)))
    return jnp.clip(base * column, -8.0, 8.0).astype(jnp.bfloat16)


def place_ends(values, stream_key, least, largest):
    longest = values.shape.index(max(values.shape))
    spots = []
    for shift in (0, 1):
        where = [jax.random.randint(jax.random.fold_in(stream_key, axis), (), 0, length) for axis, length in enumerate(values.shape)]
        where[longest] = (where[longest] + shift) % values.shape[longest]
        spots.append(tuple(where))
    return values.at[spots[0]].set(least).at[spots[1]].set(largest)


def steps_of(rng, dims, cuts, least, largest):
    def one(position, shards_of):
        draws = jax.random.uniform(jax.random.fold_in(jax.random.fold_in(rng, 6), position), (shards_of,), jnp.float32, least / len(cuts), largest / len(cuts))
        return jnp.repeat(jnp.exp(draws), dims[position] // shards_of).reshape((-1,) + (1,) * (len(dims) - position - 1))

    level = one(*cuts[0])
    for cut in cuts[1:]:
        level = level * one(*cut)
    return level


def profile(number_of, total, limit, lean):
    portions = [(1 << 20) // math.isqrt(grade ** lean) + 1 for grade in range(2, number_of + 1)]
    rest, holding = total - limit - (number_of - 1), [1] * (number_of - 1)
    while rest > 0:
        movable = [i for i in range(number_of - 1) if holding[i] < limit]
        mass, remaining = sum([portions[i] for i in movable]), rest
        for i in movable:
            addition = min(limit - holding[i], max(1, remaining * portions[i] // mass), rest)
            holding[i] = holding[i] + addition
            rest = rest - addition
    return np.array([limit] + holding)


def uneven(stream_key, count, total, bound, lean):
    if count == 2:
        one = jax.random.randint(stream_key, (), max(1, total - bound), min(bound, total - 1) + 1)
        return jnp.stack([one, total - one])
    sizes = jnp.asarray(profile(count, total, bound, lean), jnp.int32)
    twos = (count - 1) // 2
    giver, receiver = sizes[1:1 + 2 * twos:2], sizes[2:2 + 2 * twos:2]
    margin = jnp.minimum(giver - 1, bound - receiver)
    passed = jax.random.randint(jax.random.fold_in(stream_key, 1), (twos,), 0, 1 << 20) % (margin + 1)
    sizes = sizes.at[1:1 + 2 * twos:2].set(giver - passed).at[2:2 + 2 * twos:2].set(receiver + passed)
    return sizes[jax.random.permutation(jax.random.fold_in(stream_key, 2), count)]


def scatter_about(stream_key, shape, width, reach, cuts=(), held_as=jnp.bfloat16):
    entries = width * jax.random.normal(stream_key, shape, jnp.float32)
    if cuts:
        entries = entries * steps_of(stream_key, shape, cuts, -0.22, 0.18)
    return jnp.clip(entries, -reach, reach).astype(held_as)


def setup_inputs(seed: int = 0) -> dict:
    key_list = jax.random.split(jax.random.key(seed), 12)
    post_deter = jnp.clip(jax.random.uniform(key_list[0], (STARTS, DETER), jnp.float32, -1.0, 1.0) * steps_of(key_list[0], (STARTS, DETER), ((0, 64), (1, 8)), -0.4, 0.0), -1.0, 1.0).astype(jnp.bfloat16)
    post_sample = place_ends(jax.random.randint(key_list[1], (STARTS, STOCH), 0, CLASSES), jax.random.fold_in(key_list[1], 1), 0, CLASSES - 1).astype(jnp.int32)
    samples = place_ends(jax.random.randint(key_list[2], (IMAG, STARTS, STOCH), 0, CLASSES), jax.random.fold_in(key_list[2], 1), 0, CLASSES - 1).astype(jnp.int32)
    actions = place_ends(jax.random.randint(key_list[3], (IMAG, STARTS), 0, ACTIONS), jax.random.fold_in(key_list[3], 1), 0, ACTIONS - 1).astype(jnp.int32)
    counts = uneven(key_list[4], SEQS, SEQS * STEPS // 2, STEPS, 2).astype(jnp.int32)
    w_stoch = scatter_about(key_list[5], (LAT, UNITS), STOCH ** -0.5, 1.0, ((1, 8),))
    w_action = scatter_about(key_list[6], (ACTIONS, UNITS), 1 ** -0.5, 6.0, ((1, 8),))
    w_gate = scatter_about(key_list[7], (UNITS, 3 * DETER), UNITS ** -0.5, 0.1875, ((0, 64), (1, 8)))
    w_rec = scatter_about(key_list[8], (BLOCKS, BW, 3 * BW), BW ** -0.5, 0.25, ((0, 8),))
    w_prior_in = scatter_about(key_list[9], (DETER, UNITS), DETER ** -0.5, 0.09375, ((0, 8),))
    w_prior_out = draw_w_prior_out(jax.random.fold_in(key_list[11], 71), 0)
    return {"post_deter": post_deter, "post_sample": post_sample, "samples": samples, "actions": actions, "counts": counts, "w_stoch": w_stoch, "w_action": w_action, "w_gate": w_gate, "w_rec": w_rec, "w_prior_in": w_prior_in, "w_prior_out": w_prior_out}


epsilon = 1e-06

def rms_silu(values):
    scale = lax.rsqrt(lax.optimization_barrier(jnp.mean(values * values, axis=1, keepdims=True)) + epsilon)
    return jax.nn.silu(values * scale).astype(jnp.bfloat16)

def imagine_block(packed, w_stoch, w_action, w_gate, w_rec, w_prior_in, w_prior_out):
    deter, latent, samples, actions, counts = packed
    row_count = deter.shape[0]
    positions = jnp.arange(STEPS, dtype=jnp.int32)
    valid_mask = (positions[None, :] < counts[:, None]).reshape(row_count)
    class_ids = jnp.arange(CLASSES, dtype=jnp.int32)
    action_ids = jnp.arange(ACTIONS, dtype=jnp.int32)
    rec_float = w_rec.astype(jnp.float32)
    log_list = []
    for imag_step in range(IMAG):
        latent_hot = (latent[:, :, None] == class_ids).reshape(row_count, LAT).astype(jnp.bfloat16)
        action_hot = (actions[imag_step][:, None] == action_ids).astype(jnp.bfloat16)
        embed_pre = jnp.dot(latent_hot, w_stoch, preferred_element_type=jnp.float32)
        embed_pre = embed_pre + jnp.dot(action_hot, w_action, preferred_element_type=jnp.float32)
        features = rms_silu(embed_pre)
        gate_sum = jnp.dot(features, w_gate, preferred_element_type=jnp.float32).reshape(row_count, BLOCKS, 3 * BW)
        deter_blocks = deter.reshape(row_count, BLOCKS, BW).astype(jnp.float32)
        gate_sum = gate_sum + jnp.einsum('rbk,bkn->rbn', deter_blocks, rec_float)
        reset_gate = jax.nn.sigmoid(gate_sum[..., :BW])
        candidate = jnp.tanh(reset_gate * gate_sum[..., BW:2 * BW])
        update = jax.nn.sigmoid(gate_sum[..., 2 * BW:] - 1.0)
        fresh = update * candidate + (1.0 - update) * deter_blocks
        deter = fresh.reshape(row_count, DETER).astype(jnp.bfloat16)
        prior_pre = jnp.dot(deter, w_prior_in, preferred_element_type=jnp.float32)
        prior_hidden = rms_silu(prior_pre)
        logits = jnp.dot(prior_hidden, w_prior_out, preferred_element_type=jnp.float32).reshape(row_count, STOCH, CLASSES)
        softmax_probs = jax.nn.softmax(logits, axis=-1)
        mixture = 0.99 * softmax_probs + 0.01 / CLASSES
        chosen = lax.optimization_barrier(jnp.sum(jnp.where(samples[imag_step][:, :, None] == class_ids, mixture, 0.0), axis=-1))
        log_terms = lax.optimization_barrier(jnp.sum(jnp.log(chosen), axis=1))
        log_list.append(jnp.where(valid_mask, log_terms, 0.0))
        latent = samples[imag_step]
    deter_out = jnp.where(valid_mask[:, None], deter, jnp.zeros_like(deter))
    return (deter_out, jnp.stack(log_list))

def reference(post_deter, post_sample, samples, actions, counts, w_stoch, w_action, w_gate, w_rec, w_prior_in, w_prior_out):
    packed = (post_deter.reshape(N_DP, STARTS_DEV, DETER), post_sample.reshape(N_DP, STARTS_DEV, STOCH), samples.reshape(IMAG, N_DP, STARTS_DEV, STOCH).transpose(1, 0, 2, 3), actions.reshape(IMAG, N_DP, STARTS_DEV).transpose(1, 0, 2), counts.reshape(N_DP, SEQ_DEV))

    def one_block(item):
        return imagine_block(item, w_stoch, w_action, w_gate, w_rec, w_prior_in, w_prior_out)
    deter_all, log_all = lax.map(one_block, packed)
    deter_out = deter_all.reshape(STARTS, DETER)
    log_prob = log_all.transpose(1, 0, 2).reshape(IMAG, STARTS)
    return (deter_out, log_prob)
```

```python
import functools

import jax
import jax.numpy as jnp
from jax import lax
from jax.experimental import pallas as pl
from jax.experimental.pallas import tpu as pltpu
from jax.sharding import PartitionSpec as P

STOCH = 32
CLASSES = 32
LAT = STOCH * CLASSES
ACTIONS = 18
STEPS = 64
IMAG = 2
UNITS = 1024
NY = 4
NX = 4
NC = 2
LANES = 128
EPS = 1e-06
MIB = 1024 * 1024


def y_groups(n_dp):
    return [[start + y for y in range(NY)] for start in range(0, n_dp, NY)]


def z_groups(n_dp):
    return [list(range(y, n_dp, NY)) for y in range(NY)]


def x_groups():
    return [list(range(core, NX * NC, NC)) for core in range(NC)]


def spread_to(value, axis, groups, count):
    copies = jnp.broadcast_to(value[None], (count,) + value.shape)
    return lax.all_to_all(copies, axis, 0, 0, axis_index_groups=groups)


def core_swap(value):
    perm = [(i, i ^ 1) for i in range(NX * NC)]
    return lax.ppermute(value, "tensor", perm)


def features_kernel(core_ref, pack_ref, spread_ref, target_ref, mine_ref, other_ref, out_ref, w_ref):
    @pl.when(pl.program_id(0) == 0)
    def _():
        core = core_ref[0]
        for x in range(NX):
            base = x * NC * LANES
            w_ref[:, pl.ds(pl.multiple_of(base + core * LANES, LANES), LANES)] = mine_ref[x]
            w_ref[:, pl.ds(pl.multiple_of(base + (1 - core) * LANES, LANES), LANES)] = other_ref[x]

    spread = jnp.dot(pack_ref[...], spread_ref[...], preferred_element_type=jnp.float32)
    hot = jnp.where(spread == target_ref[...], 1.0, 0.0).astype(jnp.bfloat16)
    pre = jnp.dot(hot, w_ref[...], preferred_element_type=jnp.float32)
    scale = lax.rsqrt(jnp.mean(pre * pre, axis=1, keepdims=True) + EPS)
    normed = pre * scale
    out_ref[...] = (normed * jax.nn.sigmoid(normed)).astype(jnp.bfloat16)


def features_call(step, core, pack, mine, other):
    rows = pack.shape[1]
    width = mine.shape[1]
    lane = jnp.arange(width, dtype=jnp.int32)
    is_lat = lane < LAT
    target = jnp.where(is_lat, lane % CLASSES, lane - LAT).astype(jnp.float32)[None, :]
    source = jnp.where(is_lat, step * STOCH + lane // CLASSES, IMAG * STOCH + step)
    spread = (jnp.arange(LANES, dtype=jnp.int32)[:, None] == source[None, :]).astype(jnp.bfloat16)
    return pl.pallas_call(
        features_kernel,
        grid=(NY,),
        in_specs=[
            pl.BlockSpec(memory_space=pltpu.SMEM),
            pl.BlockSpec((None, rows, LANES), lambda b: (b, 0, 0)),
            pl.BlockSpec((LANES, width), lambda b: (0, 0)),
            pl.BlockSpec((1, width), lambda b: (0, 0)),
            pl.BlockSpec((NX, width, LANES), lambda b: (0, 0, 0)),
            pl.BlockSpec((NX, width, LANES), lambda b: (0, 0, 0)),
        ],
        out_specs=pl.BlockSpec((None, rows, UNITS), lambda b: (b, 0, 0)),
        out_shape=jax.ShapeDtypeStruct((NY, rows, UNITS), jnp.bfloat16),
        scratch_shapes=[pltpu.VMEM((width, UNITS), jnp.bfloat16)],
        compiler_params=pltpu.CompilerParams(vmem_limit_bytes=32 * MIB),
        cost_estimate=pl.CostEstimate(
            flops=2 * NY * rows * width * (UNITS + LANES),
            bytes_accessed=NY * rows * UNITS * 2 + width * UNITS * 2,
            transcendentals=NY * rows * UNITS,
        ),
        name="features",
    )(core, pack, spread, target, mine, other)


def gru_kernel(deter_ref, w_rec_ref, w_in_ref, f_ref, new_ref, prior_ref):
    bw = deter_ref.shape[1]
    part = bw // NY
    rec = jnp.dot(deter_ref[...], w_rec_ref[...], preferred_element_type=jnp.float32)
    for q in range(NY):

        def gate(which):
            mine = f_ref[q, :, which * part : (which + 1) * part].astype(jnp.float32)
            return rec[:, which * bw + q * part : which * bw + (q + 1) * part] + mine

        reset = jax.nn.sigmoid(gate(0))
        candidate = jnp.tanh(reset * gate(1))
        update = jax.nn.sigmoid(gate(2) - 1.0)
        old = deter_ref[:, q * part : (q + 1) * part].astype(jnp.float32)
        fresh = update * candidate + (1.0 - update) * old
        new_ref[:, q * part : (q + 1) * part] = fresh.astype(jnp.bfloat16)
    prior_ref[...] = jnp.dot(new_ref[...], w_in_ref[...], preferred_element_type=jnp.float32).astype(jnp.bfloat16)


def gru_call(deter, w_rec, w_in, sums):
    rows, bw = deter.shape
    vmem = pl.BlockSpec(memory_space=pltpu.VMEM)
    return pl.pallas_call(
        gru_kernel,
        in_specs=[vmem] * 4,
        out_specs=[vmem, vmem],
        out_shape=[
            jax.ShapeDtypeStruct((rows, bw), jnp.bfloat16),
            jax.ShapeDtypeStruct((rows, w_in.shape[1]), jnp.bfloat16),
        ],
        compiler_params=pltpu.CompilerParams(vmem_limit_bytes=32 * MIB),
        cost_estimate=pl.CostEstimate(
            flops=2 * rows * bw * (3 * bw + w_in.shape[1]),
            bytes_accessed=2 * (w_rec.size + w_in.size) + 12 * rows * bw,
            transcendentals=3 * rows * bw,
        ),
        name="gru",
    )(deter, w_rec, w_in, sums)


def tail_kernel(p0_ref, p1_ref, w_out_ref, picked_ref, var_ref, mask_ref, log_ref):
    def hidden_of(ref):
        pre = ref[0].astype(jnp.float32)
        for i in range(1, ref.shape[0]):
            pre = pre + ref[i].astype(jnp.float32)
        normed = pre * lax.rsqrt(jnp.mean(pre * pre, axis=1, keepdims=True) + EPS)
        return (normed * jax.nn.sigmoid(normed)).astype(jnp.bfloat16)

    hidden = jnp.concatenate([hidden_of(p0_ref), hidden_of(p1_ref)], axis=0)
    rows = hidden.shape[0]
    cls = lax.broadcasted_iota(jnp.int32, (rows, LANES), 1) % CLASSES

    def within(value, combine):
        step = 1
        while step < CLASSES:
            ahead = pltpu.roll(value, step, 1)
            wrapped = pltpu.roll(value, LANES - CLASSES + step, 1)
            value = combine(value, jnp.where(cls >= step, ahead, wrapped))
            step *= 2
        return value

    total = jnp.zeros((rows, LANES), jnp.float32)
    for j in range(w_out_ref.shape[0]):
        logits = jnp.dot(hidden, w_out_ref[j], preferred_element_type=jnp.float32)
        powers = jnp.exp(logits - within(logits, jnp.maximum))
        probs = 0.99 * (powers / within(powers, jnp.add)) + 0.01 / CLASSES
        want = jnp.dot(picked_ref[...], var_ref[:, j * LANES : (j + 1) * LANES], preferred_element_type=jnp.float32)
        total = total + jnp.where(cls.astype(jnp.float32) == want, jnp.log(probs), 0.0)
    summed = jnp.where(mask_ref[...] > 0, jnp.sum(total, axis=1, keepdims=True), 0.0)
    diagonal = lax.broadcasted_iota(jnp.int32, (rows, rows), 0) == lax.broadcasted_iota(jnp.int32, (rows, rows), 1)
    log_ref[...] = jnp.sum(jnp.where(diagonal, summed, 0.0), axis=0, keepdims=True)


def tail_call(parts, w_out, picked, mask):
    rows = picked.shape[0]
    lane = jnp.arange(LAT, dtype=jnp.int32)
    var_of = (jnp.arange(STOCH, dtype=jnp.int32)[:, None] == lane[None, :] // CLASSES).astype(jnp.bfloat16)
    vmem = pl.BlockSpec(memory_space=pltpu.VMEM)
    return pl.pallas_call(
        tail_kernel,
        in_specs=[vmem] * 6,
        out_specs=vmem,
        out_shape=jax.ShapeDtypeStruct((1, rows), jnp.float32),
        compiler_params=pltpu.CompilerParams(vmem_limit_bytes=32 * MIB),
        cost_estimate=pl.CostEstimate(
            flops=2 * rows * UNITS * LAT, bytes_accessed=4 * w_out.size, transcendentals=4 * rows * LAT
        ),
        name="tail",
    )(parts[0], parts[1], w_out, picked, var_of, mask)


def body(
    post_deter,
    post_sample,
    samples,
    actions,
    counts,
    w_stoch,
    w_action,
    w_gate,
    w_rec,
    w_prior_in,
    w_prior_out,
    n_dp,
):
    rows = post_deter.shape[0]
    bw = w_rec.shape[1]
    part = bw // NY
    depth = w_gate.shape[0]
    tensor_n = NX * NC
    share = rows // tensor_n
    me = lax.axis_index("tensor")
    core = (me % NC).reshape(1).astype(jnp.int32)

    quarters = w_gate.reshape(depth * 3, NY, part).transpose(1, 0, 2)
    columns = [post_sample, samples[0]] + [actions[k][:, None] for k in range(IMAG)]
    pack = jnp.concatenate(columns, axis=1).astype(jnp.bfloat16)
    pack = jnp.pad(pack, ((0, 0), (0, LANES - pack.shape[1])))
    sent = jnp.concatenate([quarters, jnp.broadcast_to(pack[None], (NY,) + pack.shape)], axis=1)
    came = lax.all_to_all(sent, "dp", 0, 0, axis_index_groups=y_groups(n_dp))
    pack = came[:, depth * 3 :]
    held = came[:, : depth * 3].reshape(NY * depth, 3 * part)
    gate = lax.all_gather(held, "dp", axis=0, tiled=True, axis_index_groups=z_groups(n_dp))

    action_rows = jnp.pad(w_action, ((0, LANES - ACTIONS), (0, 0)))
    embed, _ = lax.optimization_barrier((jnp.concatenate([w_stoch, action_rows], axis=0), came))
    mine = spread_to(embed, "tensor", x_groups(), NX)
    other = core_swap(mine)

    w_out_late, _ = lax.optimization_barrier((w_prior_out, gate))
    w_out = lax.all_gather(w_out_late, "tensor", axis=0)

    positions = jnp.arange(STEPS, dtype=jnp.int32)
    valid_mask = (positions[None, :] < counts[:, None]).reshape(rows)
    my_mask = lax.dynamic_slice_in_dim(valid_mask, me * share, share, 0).astype(jnp.float32)
    my_mask = jnp.concatenate([my_mask] * IMAG)[:, None]
    picked = lax.dynamic_slice_in_dim(samples, me * share, share, 1)
    picked = picked.reshape(IMAG * share, STOCH).astype(jnp.bfloat16)

    sums = []
    for k in range(IMAG):
        features = features_call(k, core, pack, mine, other)
        total = jnp.dot(features.reshape(NY * rows, UNITS), gate, preferred_element_type=jnp.float32)
        total = total.astype(jnp.bfloat16).reshape(NY, rows, 3 * part)
        sums.append(lax.all_to_all(total, "dp", 0, 0, axis_index_groups=y_groups(n_dp)))

    deter = post_deter
    parts = []
    for k in range(IMAG):
        deter, partial = gru_call(deter, w_rec[0], w_prior_in, sums[k])
        parts.append(lax.all_to_all(partial.reshape(tensor_n, share, UNITS), "tensor", 0, 0))
    logs = tail_call(parts, w_out, picked, my_mask)
    logs = spread_to(logs.reshape(IMAG, share), "tensor", None, tensor_n)
    log_prob = logs.transpose(1, 0, 2).reshape(IMAG, rows)
    deter_out = jnp.where(valid_mask[:, None], deter, jnp.zeros_like(deter))
    return (deter_out, log_prob)


def solution(mesh):
    in_specs = (
        P("dp", "tensor"),
        P("dp", None),
        P(None, "dp", None),
        P(None, "dp"),
        P("dp"),
        P(None, "tensor"),
        P(None, "tensor"),
        P("dp", "tensor"),
        P("tensor", None, None),
        P("tensor", None),
        P(None, "tensor"),
    )
    out_specs = (P("dp", "tensor"), P(None, "dp"))
    whole = functools.partial(body, n_dp=mesh.shape["dp"])
    return jax.shard_map(whole, mesh=mesh, in_specs=in_specs, out_specs=out_specs, check_vma=False)
```

```python
import functools

import jax
import jax.numpy as jnp
from jax import lax
from jax.experimental import pallas as pl
from jax.experimental.pallas import tpu as pltpu
from jax.sharding import PartitionSpec as P

STOCH = 32
CLASSES = 32
LAT = STOCH * CLASSES
ACTIONS = 18
STEPS = 64
IMAG = 2
UNITS = 1024
NY = 4
NX = 4
NC = 2
LANES = 128
EPS = 1e-06
MIB = 1024 * 1024


def y_groups(n_dp):
    return [[start + y for y in range(NY)] for start in range(0, n_dp, NY)]


def y_shift(value, step, n_dp):
    perm = [(i, i // NY * NY + (i % NY + step) % NY) for i in range(n_dp)]
    return lax.ppermute(value, "dp", perm)


def x_shift(value, step):
    count = NX * NC
    perm = [(i, (i + step * NC) % count) for i in range(count)]
    return lax.ppermute(value, "tensor", perm)


def core_swap(value):
    perm = [(i, i ^ 1) for i in range(NX * NC)]
    return lax.ppermute(value, "tensor", perm)


def tensor_gather(value):
    mine = jnp.stack([value] + [x_shift(value, step) for step in range(1, NX)])
    return mine, core_swap(mine)


def split_kernel(w_ref, out_ref):
    part = w_ref.shape[1] // 3 // NY
    for y in range(NY):
        for which in range(3):
            columns = w_ref[:, (which * NY + y) * part : (which * NY + y + 1) * part]
            for z in range(out_ref.shape[0]):
                out_ref[z, y, :, which * part : (which + 1) * part] = columns


def split_call(w_gate, n_z):
    depth, width = w_gate.shape
    vmem = pl.BlockSpec(memory_space=pltpu.VMEM)
    return pl.pallas_call(
        split_kernel,
        in_specs=[vmem],
        out_specs=vmem,
        out_shape=jax.ShapeDtypeStruct((n_z, NY, depth, width // NY), w_gate.dtype),
        compiler_params=pltpu.CompilerParams(vmem_limit_bytes=16 * MIB),
        cost_estimate=pl.CostEstimate(flops=0, bytes_accessed=2 * n_z * depth * width, transcendentals=0),
        name="split",
    )(w_gate)


def features_kernel(me_ref, pack_ref, spread_ref, target_ref, mine_ref, other_ref, out_ref, w_ref):
    @pl.when(pl.program_id(0) == 0)
    def _():
        x, core = me_ref[0], me_ref[1]
        for i in range(NX):
            base = lax.rem(x + NX - i, NX) * NC
            w_ref[:, pl.ds(pl.multiple_of((base + core) * LANES, LANES), LANES)] = mine_ref[i]
            w_ref[:, pl.ds(pl.multiple_of((base + 1 - core) * LANES, LANES), LANES)] = other_ref[i]

    for k in range(IMAG):
        spread = jnp.dot(pack_ref[...], spread_ref[k], preferred_element_type=jnp.float32)
        hot = jnp.where(spread == target_ref[...], 1.0, 0.0).astype(jnp.bfloat16)
        pre = jnp.dot(hot, w_ref[...], preferred_element_type=jnp.float32)
        scale = lax.rsqrt(jnp.mean(pre * pre, axis=1, keepdims=True) + EPS)
        normed = pre * scale
        out_ref[k] = (normed * jax.nn.sigmoid(normed)).astype(jnp.bfloat16)


def features_call(place, pack, mine, other):
    rows = pack.shape[1]
    width = mine.shape[1]
    lane = jnp.arange(width, dtype=jnp.int32)
    is_lat = lane < LAT
    target = jnp.where(is_lat, lane % CLASSES, lane - LAT).astype(jnp.float32)[None, :]
    step = jnp.arange(IMAG, dtype=jnp.int32)[:, None]
    source = jnp.where(is_lat[None, :], step * STOCH + lane[None, :] // CLASSES, IMAG * STOCH + step)
    spread = (jnp.arange(LANES, dtype=jnp.int32)[None, :, None] == source[:, None, :]).astype(jnp.bfloat16)
    return pl.pallas_call(
        features_kernel,
        grid=(NY,),
        in_specs=[
            pl.BlockSpec(memory_space=pltpu.SMEM),
            pl.BlockSpec((None, rows, LANES), lambda b: (b, 0, 0)),
            pl.BlockSpec((IMAG, LANES, width), lambda b: (0, 0, 0)),
            pl.BlockSpec((1, width), lambda b: (0, 0)),
            pl.BlockSpec((NX, width, LANES), lambda b: (0, 0, 0)),
            pl.BlockSpec((NX, width, LANES), lambda b: (0, 0, 0)),
        ],
        out_specs=pl.BlockSpec((IMAG, None, rows, UNITS), lambda b: (0, b, 0, 0)),
        out_shape=jax.ShapeDtypeStruct((IMAG, NY, rows, UNITS), jnp.bfloat16),
        scratch_shapes=[pltpu.VMEM((width, UNITS), jnp.bfloat16)],
        compiler_params=pltpu.CompilerParams(vmem_limit_bytes=32 * MIB),
        cost_estimate=pl.CostEstimate(
            flops=2 * IMAG * NY * rows * width * (UNITS + LANES),
            bytes_accessed=IMAG * NY * rows * UNITS * 2 + width * UNITS * 2,
            transcendentals=IMAG * NY * rows * UNITS,
        ),
        name="features",
    )(place, pack, spread, target, mine, other)


def gate_kernel(features_ref, gate_ref, out_ref):
    for k in range(IMAG):
        out_ref[k] = jnp.dot(features_ref[k], gate_ref[...], preferred_element_type=jnp.float32).astype(jnp.bfloat16)


def gate_call(features, gate):
    rows = features.shape[2]
    width = gate.shape[1]
    return pl.pallas_call(
        gate_kernel,
        grid=(NY,),
        in_specs=[
            pl.BlockSpec((IMAG, None, rows, UNITS), lambda b: (0, b, 0, 0)),
            pl.BlockSpec((UNITS, width), lambda b: (0, 0)),
        ],
        out_specs=pl.BlockSpec((None, IMAG, rows, width), lambda b: (b, 0, 0, 0)),
        out_shape=jax.ShapeDtypeStruct((NY, IMAG, rows, width), jnp.bfloat16),
        compiler_params=pltpu.CompilerParams(vmem_limit_bytes=32 * MIB),
        cost_estimate=pl.CostEstimate(
            flops=2 * IMAG * NY * rows * UNITS * width,
            bytes_accessed=IMAG * NY * rows * (UNITS + width) * 2 + UNITS * width * 2,
            transcendentals=0,
        ),
        name="gate",
    )(features, gate)


def gru_kernel(deter_ref, w_rec_ref, w_in_ref, f_ref, new_ref, prior_ref, mid_ref):
    rows, bw = deter_ref.shape
    part = bw // NY
    for k in range(IMAG):
        old_ref = deter_ref if k == 0 else mid_ref
        next_ref = new_ref if k == IMAG - 1 else mid_ref
        old = old_ref[...]
        rec = jnp.dot(old, w_rec_ref[...], preferred_element_type=jnp.float32)
        for q in range(NY):

            def gate(which):
                mine = f_ref[q, k, :, which * part : (which + 1) * part].astype(jnp.float32)
                return rec[:, which * bw + q * part : which * bw + (q + 1) * part] + mine

            reset = jax.nn.sigmoid(gate(0))
            candidate = jnp.tanh(reset * gate(1))
            update = jax.nn.sigmoid(gate(2) - 1.0)
            before = old[:, q * part : (q + 1) * part].astype(jnp.float32)
            fresh = update * candidate + (1.0 - update) * before
            next_ref[:, q * part : (q + 1) * part] = fresh.astype(jnp.bfloat16)
        prior = jnp.dot(next_ref[...], w_in_ref[...], preferred_element_type=jnp.float32).astype(jnp.bfloat16)
        share = prior_ref.shape[2]
        for j in range(prior_ref.shape[0]):
            prior_ref[j, k] = prior[j * share : (j + 1) * share]


def gru_call(deter, w_rec, w_in, sums, tensor_n):
    rows, bw = deter.shape
    vmem = pl.BlockSpec(memory_space=pltpu.VMEM)
    return pl.pallas_call(
        gru_kernel,
        in_specs=[vmem] * 4,
        out_specs=[vmem, vmem],
        out_shape=[
            jax.ShapeDtypeStruct((rows, bw), jnp.bfloat16),
            jax.ShapeDtypeStruct((tensor_n, IMAG, rows // tensor_n, w_in.shape[1]), jnp.bfloat16),
        ],
        scratch_shapes=[pltpu.VMEM((rows, bw), jnp.bfloat16)],
        compiler_params=pltpu.CompilerParams(vmem_limit_bytes=32 * MIB),
        cost_estimate=pl.CostEstimate(
            flops=2 * IMAG * rows * bw * (3 * bw + w_in.shape[1]),
            bytes_accessed=2 * (w_rec.size + w_in.size) + 24 * rows * bw,
            transcendentals=6 * rows * bw,
        ),
        name="gru",
    )(deter, w_rec, w_in, sums)


def tail_kernel(me_ref, parts_ref, mine_ref, other_ref, picked_ref, var_ref, mask_ref, log_ref):
    pre = parts_ref[0].astype(jnp.float32)
    for i in range(1, parts_ref.shape[0]):
        pre = pre + parts_ref[i].astype(jnp.float32)
    normed = pre * lax.rsqrt(jnp.mean(pre * pre, axis=1, keepdims=True) + EPS)
    hidden = (normed * jax.nn.sigmoid(normed)).astype(jnp.bfloat16)
    rows = hidden.shape[0]
    cls = lax.broadcasted_iota(jnp.int32, (rows, LANES), 1) % CLASSES

    def within(value, combine):
        step = 1
        while step < CLASSES:
            ahead = pltpu.roll(value, step, 1)
            wrapped = pltpu.roll(value, LANES - CLASSES + step, 1)
            value = combine(value, jnp.where(cls >= step, ahead, wrapped))
            step *= 2
        return value

    total = jnp.zeros((rows, LANES), jnp.float32)
    x, core = me_ref[0], me_ref[1]
    for i in range(NX * NC):
        w_ref = mine_ref if i % NC == 0 else other_ref
        piece = lax.rem(x + NX - i // NC, NX) * NC + (core if i % NC == 0 else 1 - core)
        here = pl.ds(pl.multiple_of(piece * LANES, LANES), LANES)
        logits = jnp.dot(hidden, w_ref[i // NC], preferred_element_type=jnp.float32)
        powers = jnp.exp(logits - within(logits, jnp.maximum))
        probs = 0.99 * (powers / within(powers, jnp.add)) + 0.01 / CLASSES
        want = jnp.dot(picked_ref[...], var_ref[:, here], preferred_element_type=jnp.float32)
        total = total + jnp.where(cls.astype(jnp.float32) == want, jnp.log(probs), 0.0)
    summed = jnp.where(mask_ref[...] > 0, jnp.sum(total, axis=1, keepdims=True), 0.0)
    lanes = lax.broadcasted_iota(jnp.int32, (rows, LANES), 1)
    diagonal = lax.broadcasted_iota(jnp.int32, (rows, LANES), 0) == lanes
    line = jnp.sum(jnp.where(diagonal, summed, 0.0), axis=0, keepdims=True)
    log_ref[...] = jnp.broadcast_to(line[None], log_ref.shape)


def tail_call(place, parts, mine, other, picked, mask):
    tensor_n, rows = parts.shape[:2]
    lane = jnp.arange(LAT, dtype=jnp.int32)
    var_of = (jnp.arange(STOCH, dtype=jnp.int32)[:, None] == lane[None, :] // CLASSES).astype(jnp.bfloat16)
    vmem = pl.BlockSpec(memory_space=pltpu.VMEM)
    return pl.pallas_call(
        tail_kernel,
        in_specs=[pl.BlockSpec(memory_space=pltpu.SMEM)] + [vmem] * 6,
        out_specs=vmem,
        out_shape=jax.ShapeDtypeStruct((tensor_n, 8, LANES), jnp.float32),
        compiler_params=pltpu.CompilerParams(vmem_limit_bytes=32 * MIB),
        cost_estimate=pl.CostEstimate(
            flops=2 * rows * UNITS * LAT, bytes_accessed=8 * mine.size, transcendentals=4 * rows * LAT
        ),
        name="tail",
    )(place, parts, mine, other, picked, var_of, mask)


def body(
    post_deter,
    post_sample,
    samples,
    actions,
    counts,
    w_stoch,
    w_action,
    w_gate,
    w_rec,
    w_prior_in,
    w_prior_out,
    n_dp,
):
    rows = post_deter.shape[0]
    depth = w_gate.shape[0]
    tensor_n = NX * NC
    share = rows // tensor_n
    me = lax.axis_index("tensor")
    place = jnp.stack([me // NC, me % NC]).astype(jnp.int32)

    sent = split_call(w_gate, n_dp // NY)
    gate = lax.all_to_all(sent.reshape(n_dp, depth, -1), "dp", 0, 0).reshape(n_dp * depth, -1)

    action_rows = jnp.pad(w_action, ((0, LANES - ACTIONS), (0, 0)))
    mine, other = tensor_gather(jnp.concatenate([w_stoch, action_rows], axis=0))

    columns = [post_sample, samples[0]] + [actions[k][:, None] for k in range(IMAG)]
    pack = jnp.concatenate(columns, axis=1).astype(jnp.bfloat16)
    pack = jnp.pad(pack, ((0, 0), (0, LANES - pack.shape[1])))
    pack = jnp.stack([pack] + [y_shift(pack, b, n_dp) for b in range(1, NY)])
    y = lax.axis_index("dp") % NY
    pack = jnp.stack([lax.dynamic_index_in_dim(pack, (y - b + NY) % NY, 0, keepdims=False) for b in range(NY)])

    features = features_call(place, pack, mine, other)
    sums = lax.all_to_all(gate_call(features, gate), "dp", 0, 0, axis_index_groups=y_groups(n_dp))

    w_out_late, _ = lax.optimization_barrier((w_prior_out, features))
    out_mine, out_other = tensor_gather(w_out_late)

    positions = jnp.arange(STEPS, dtype=jnp.int32)
    valid_mask = (positions[None, :] < counts[:, None]).reshape(rows)
    my_mask = lax.dynamic_slice_in_dim(valid_mask, me * share, share, 0).astype(jnp.float32)
    my_mask = jnp.concatenate([my_mask] * IMAG)[:, None]
    picked = lax.dynamic_slice_in_dim(samples, me * share, share, 1)
    picked = picked.reshape(IMAG * share, STOCH).astype(jnp.bfloat16)

    deter, partial = gru_call(post_deter, w_rec[0], w_prior_in, sums, tensor_n)
    parts = lax.all_to_all(partial.reshape(tensor_n, IMAG * share, UNITS), "tensor", 0, 0)
    logs = tail_call(place, parts, out_mine, out_other, picked, my_mask)
    logs = lax.all_to_all(logs, "tensor", 0, 0)[:, 0, : IMAG * share]
    log_prob = logs.reshape(tensor_n, IMAG, share).transpose(1, 0, 2).reshape(IMAG, rows)
    deter_out = jnp.where(valid_mask[:, None], deter, jnp.zeros_like(deter))
    return (deter_out, log_prob)


def solution(mesh):
    in_specs = (
        P("dp", "tensor"),
        P("dp", None),
        P(None, "dp", None),
        P(None, "dp"),
        P("dp"),
        P(None, "tensor"),
        P(None, "tensor"),
        P("dp", "tensor"),
        P("tensor", None, None),
        P("tensor", None),
        P(None, "tensor"),
    )
    out_specs = (P("dp", "tensor"), P(None, "dp"))
    whole = functools.partial(body, n_dp=mesh.shape["dp"])
    return jax.shard_map(whole, mesh=mesh, in_specs=in_specs, out_specs=out_specs, check_vma=False)
```

```python
import functools

import jax
import jax.numpy as jnp
from jax import lax
from jax.experimental import pallas as pl
from jax.experimental.pallas import tpu as pltpu
from jax.sharding import PartitionSpec as P

STOCH = 32
CLASSES = 32
LAT = STOCH * CLASSES
ACTIONS = 18
STEPS = 64
IMAG = 2
UNITS = 1024
NY = 4
NX = 4
NC = 2
NEAR = 4
LANES = 128
EPS = 1e-06
MIB = 1024 * 1024
GRANT = 60 * MIB


def y_groups(n_dp):
    return [[start + y for y in range(NY)] for start in range(0, n_dp, NY)]


def far_groups(n_dp):
    n_far = n_dp // NY // NEAR
    return [[(far * NEAR + near) * NY + y for far in range(n_far) for y in range(NY)] for near in range(NEAR)]


def near_groups(n_dp):
    n_far = n_dp // NY // NEAR
    return [[(far * NEAR + near) * NY + y for near in range(NEAR)] for far in range(n_far) for y in range(NY)]


def x_groups():
    return [list(range(core, NX * NC, NC)) for core in range(NC)]


def y_shift(value, step, n_dp):
    perm = [(i, i // NY * NY + (i % NY + step) % NY) for i in range(n_dp)]
    return lax.ppermute(value, "dp", perm)


def x_shift(value, step):
    count = NX * NC
    perm = [(i, (i + step * NC) % count) for i in range(count)]
    return lax.ppermute(value, "tensor", perm)


def core_swap(value):
    perm = [(i, i ^ 1) for i in range(NX * NC)]
    return lax.ppermute(value, "tensor", perm)


def x_gather(value):
    return jnp.stack([value] + [x_shift(value, step) for step in range(1, NX)])


def silu(value):
    half = 0.5 * value
    return half + half * jnp.tanh(half)


def sigmoid(value):
    return 0.5 + 0.5 * jnp.tanh(0.5 * value)


def split_kernel(w_ref, out_ref):
    part = w_ref.shape[1] // 3 // NY
    for y in range(NY):
        for which in range(3):
            columns = w_ref[:, (which * NY + y) * part : (which * NY + y + 1) * part]
            for z in range(out_ref.shape[0]):
                out_ref[z, y, :, which * part : (which + 1) * part] = columns


def split_call(w_gate, n_z):
    depth, width = w_gate.shape
    vmem = pl.BlockSpec(memory_space=pltpu.VMEM)
    return pl.pallas_call(
        split_kernel,
        in_specs=[vmem],
        out_specs=vmem,
        out_shape=jax.ShapeDtypeStruct((n_z, NY, depth, width // NY), w_gate.dtype),
        compiler_params=pltpu.CompilerParams(vmem_limit_bytes=16 * MIB),
        cost_estimate=pl.CostEstimate(flops=0, bytes_accessed=2 * n_z * depth * width, transcendentals=0),
        name="split",
    )(w_gate)


def features_kernel(me_ref, pack_ref, spread_ref, target_ref, mine_ref, other_ref, out_ref, w_ref):
    @pl.when(pl.program_id(0) == 0)
    def _():
        x, core = me_ref[0], me_ref[1]
        for i in range(NX):
            base = lax.rem(x + NX - i, NX) * NC
            w_ref[:, pl.ds(pl.multiple_of((base + core) * LANES, LANES), LANES)] = mine_ref[i]
            w_ref[:, pl.ds(pl.multiple_of((base + 1 - core) * LANES, LANES), LANES)] = other_ref[i]

    for k in range(IMAG):
        spread = jnp.dot(pack_ref[...], spread_ref[k], preferred_element_type=jnp.float32)
        hot = jnp.where(spread == target_ref[...], 1.0, 0.0).astype(jnp.bfloat16)
        pre = jnp.dot(hot, w_ref[...], preferred_element_type=jnp.float32)
        scale = lax.rsqrt(jnp.mean(pre * pre, axis=1, keepdims=True) + EPS)
        normed = pre * scale
        out_ref[k] = silu(normed).astype(jnp.bfloat16)


def features_call(place, pack, mine, other):
    rows = pack.shape[1]
    width = mine.shape[1]
    lane = jnp.arange(width, dtype=jnp.int32)
    is_lat = lane < LAT
    target = jnp.where(is_lat, lane % CLASSES, lane - LAT).astype(jnp.float32)[None, :]
    step = jnp.arange(IMAG, dtype=jnp.int32)[:, None]
    source = jnp.where(is_lat[None, :], step * STOCH + lane[None, :] // CLASSES, IMAG * STOCH + step)
    spread = (jnp.arange(LANES, dtype=jnp.int32)[None, :, None] == source[:, None, :]).astype(jnp.bfloat16)
    return pl.pallas_call(
        features_kernel,
        grid=(NY,),
        in_specs=[
            pl.BlockSpec(memory_space=pltpu.SMEM),
            pl.BlockSpec((None, rows, LANES), lambda b: (b, 0, 0)),
            pl.BlockSpec((IMAG, LANES, width), lambda b: (0, 0, 0)),
            pl.BlockSpec((1, width), lambda b: (0, 0)),
            pl.BlockSpec((NX, width, LANES), lambda b: (0, 0, 0)),
            pl.BlockSpec((NX, width, LANES), lambda b: (0, 0, 0)),
        ],
        out_specs=pl.BlockSpec((IMAG, None, rows, UNITS), lambda b: (0, b, 0, 0)),
        out_shape=pltpu.HBM((IMAG, NY, rows, UNITS), jnp.bfloat16),
        scratch_shapes=[pltpu.VMEM((width, UNITS), jnp.bfloat16)],
        compiler_params=pltpu.CompilerParams(vmem_limit_bytes=32 * MIB),
        cost_estimate=pl.CostEstimate(
            flops=2 * IMAG * NY * rows * width * (UNITS + LANES),
            bytes_accessed=IMAG * NY * rows * UNITS * 2 + width * UNITS * 2,
            transcendentals=IMAG * NY * rows * UNITS,
        ),
        name="features",
    )(place, pack, spread, target, mine, other)


def gate_kernel(n_far, features_ref, gate_ref, out_ref, w_ref):
    near, held = gate_ref.shape[:2]
    depth = held // n_far

    @pl.when(pl.program_id(0) == 0)
    def _():
        for i in range(near):
            for far in range(n_far):
                w_ref[(far * near + i) * depth : (far * near + i + 1) * depth] = gate_ref[i, far * depth : (far + 1) * depth]

    for k in range(IMAG):
        out_ref[k] = jnp.dot(features_ref[k], w_ref[...], preferred_element_type=jnp.float32).astype(jnp.bfloat16)


def gate_call(features, gate, n_far):
    rows = features.shape[2]
    width = gate.shape[2]
    return pl.pallas_call(
        functools.partial(gate_kernel, n_far),
        grid=(NY,),
        in_specs=[
            pl.BlockSpec((IMAG, None, rows, UNITS), lambda b: (0, b, 0, 0)),
            pl.BlockSpec(gate.shape, lambda b: (0, 0, 0)),
        ],
        out_specs=pl.BlockSpec((None, IMAG, rows, width), lambda b: (b, 0, 0, 0)),
        out_shape=pltpu.HBM((NY, IMAG, rows, width), jnp.bfloat16),
        scratch_shapes=[pltpu.VMEM((UNITS, width), jnp.bfloat16)],
        compiler_params=pltpu.CompilerParams(vmem_limit_bytes=GRANT),
        cost_estimate=pl.CostEstimate(
            flops=2 * IMAG * NY * rows * UNITS * width,
            bytes_accessed=IMAG * NY * rows * (UNITS + width) * 2 + UNITS * width * 2,
            transcendentals=0,
        ),
        name="gate",
    )(features, gate)


def gru_kernel(
    core_ref,
    deter_hbm,
    w_rec_hbm,
    w_in_hbm,
    f_hbm,
    new_ref,
    keep_ref,
    send_ref,
    deter_ref,
    w_rec_ref,
    w_in_ref,
    f_ref,
    mid_ref,
    prior_ref,
    sems,
):
    rows, bw = deter_ref.shape
    part = bw // NY
    half = bw // 2
    core = core_ref[1]
    pairs = [(deter_hbm, deter_ref)]
    pairs += [(w_rec_hbm.at[pl.ds(i * half, half)], w_rec_ref.at[pl.ds(i * half, half)]) for i in range(2)]
    pairs += [(f_hbm.at[:, k], f_ref.at[:, k]) for k in range(IMAG)]
    pairs += [(w_in_hbm, w_in_ref)]
    copies = [pltpu.make_async_copy(src, dst, sems.at[i]) for i, (src, dst) in enumerate(pairs)]
    for copy in copies:
        copy.start()
    copies[0].wait()
    for k in range(IMAG):
        old_ref = deter_ref if k == 0 else mid_ref
        next_ref = new_ref if k == IMAG - 1 else mid_ref
        old = old_ref[...]
        rec = None
        for i in range(2):
            if k == 0:
                copies[1 + i].wait()
            term = jnp.dot(
                old[:, i * half : (i + 1) * half],
                w_rec_ref[i * half : (i + 1) * half],
                preferred_element_type=jnp.float32,
            )
            rec = term if rec is None else rec + term
        copies[3 + k].wait()
        for q in range(NY):

            def gate(which):
                mine = f_ref[q, k, :, which * part : (which + 1) * part].astype(jnp.float32)
                return rec[:, which * bw + q * part : which * bw + (q + 1) * part] + mine

            reset = sigmoid(gate(0))
            candidate = jnp.tanh(reset * gate(1))
            update = sigmoid(gate(2) - 1.0)
            before = old[:, q * part : (q + 1) * part].astype(jnp.float32)
            fresh = update * candidate + (1.0 - update) * before
            next_ref[:, q * part : (q + 1) * part] = fresh.astype(jnp.bfloat16)
        if k == 0:
            copies[3 + IMAG].wait()
        prior_ref[...] = jnp.dot(next_ref[...], w_in_ref[...], preferred_element_type=jnp.float32)
        share = keep_ref.shape[2]
        for x in range(NX):
            for out_ref, owner in ((keep_ref, core), (send_ref, 1 - core)):
                here = pl.ds(pl.multiple_of((x * NC + owner) * share, share), share)
                out_ref[x, k] = prior_ref[here].astype(jnp.bfloat16)


def gru_call(place, deter, w_rec, w_in, sums):
    rows, bw = deter.shape
    width = w_in.shape[1]
    vmem = pl.BlockSpec(memory_space=pltpu.VMEM)
    hbm = pl.BlockSpec(memory_space=pl.ANY)
    prior = jax.ShapeDtypeStruct((NX, IMAG, rows // (NX * NC), width), jnp.bfloat16)
    return pl.pallas_call(
        gru_kernel,
        in_specs=[pl.BlockSpec(memory_space=pltpu.SMEM)] + [hbm] * 4,
        out_specs=[vmem, vmem, vmem],
        out_shape=[jax.ShapeDtypeStruct((rows, bw), jnp.bfloat16), prior, prior],
        scratch_shapes=[
            pltpu.VMEM(deter.shape, jnp.bfloat16),
            pltpu.VMEM(w_rec.shape, jnp.bfloat16),
            pltpu.VMEM(w_in.shape, jnp.bfloat16),
            pltpu.VMEM(sums.shape, jnp.bfloat16),
            pltpu.VMEM((rows, bw), jnp.bfloat16),
            pltpu.VMEM((rows, width), jnp.float32),
            pltpu.SemaphoreType.DMA((4 + IMAG,)),
        ],
        compiler_params=pltpu.CompilerParams(vmem_limit_bytes=GRANT),
        cost_estimate=pl.CostEstimate(
            flops=2 * IMAG * rows * bw * (3 * bw + width),
            bytes_accessed=2 * (w_rec.size + w_in.size) + 24 * rows * bw,
            transcendentals=6 * rows * bw,
        ),
        name="gru",
    )(place, deter, w_rec, w_in, sums)


def tail_kernel(me_ref, parts_ref, mine_ref, other_ref, picked_ref, var_ref, mask_ref, log_ref):
    pre = parts_ref[0].astype(jnp.float32)
    for i in range(1, parts_ref.shape[0]):
        pre = pre + parts_ref[i].astype(jnp.float32)
    normed = pre * lax.rsqrt(jnp.mean(pre * pre, axis=1, keepdims=True) + EPS)
    hidden = silu(normed).astype(jnp.bfloat16)
    rows = hidden.shape[0]
    cls = lax.broadcasted_iota(jnp.int32, (rows, LANES), 1) % CLASSES

    def within(value, combine):
        step = 1
        while step < CLASSES:
            ahead = pltpu.roll(value, step, 1)
            wrapped = pltpu.roll(value, LANES - CLASSES + step, 1)
            value = combine(value, jnp.where(cls >= step, ahead, wrapped))
            step *= 2
        return value

    total = jnp.zeros((rows, LANES), jnp.float32)
    x, core = me_ref[0], me_ref[1]
    for i in range(NX * NC):
        w_ref = mine_ref if i % NC == 0 else other_ref
        piece = lax.rem(x + NX - i // NC, NX) * NC + (core if i % NC == 0 else 1 - core)
        here = pl.ds(pl.multiple_of(piece * LANES, LANES), LANES)
        logits = jnp.dot(hidden, w_ref[i // NC], preferred_element_type=jnp.float32)
        powers = jnp.exp(logits - within(logits, jnp.maximum))
        probs = 0.99 * (powers / within(powers, jnp.add)) + 0.01 / CLASSES
        want = jnp.dot(picked_ref[...], var_ref[:, here], preferred_element_type=jnp.float32)
        total = total + jnp.where(cls.astype(jnp.float32) == want, jnp.log(probs), 0.0)
    summed = jnp.where(mask_ref[...] > 0, jnp.sum(total, axis=1, keepdims=True), 0.0)
    lanes = lax.broadcasted_iota(jnp.int32, (rows, LANES), 1)
    diagonal = lax.broadcasted_iota(jnp.int32, (rows, LANES), 0) == lanes
    line = jnp.sum(jnp.where(diagonal, summed, 0.0), axis=0, keepdims=True)
    log_ref[...] = jnp.broadcast_to(line[None], log_ref.shape)


def tail_call(place, parts, mine, other, picked, mask):
    rows = parts.shape[1]
    lane = jnp.arange(LAT, dtype=jnp.int32)
    var_of = (jnp.arange(STOCH, dtype=jnp.int32)[:, None] == lane[None, :] // CLASSES).astype(jnp.bfloat16)
    vmem = pl.BlockSpec(memory_space=pltpu.VMEM)
    return pl.pallas_call(
        tail_kernel,
        in_specs=[pl.BlockSpec(memory_space=pltpu.SMEM)] + [vmem] * 6,
        out_specs=vmem,
        out_shape=jax.ShapeDtypeStruct((NX * NC, 8, LANES), jnp.float32),
        compiler_params=pltpu.CompilerParams(vmem_limit_bytes=32 * MIB),
        cost_estimate=pl.CostEstimate(
            flops=2 * rows * UNITS * LAT, bytes_accessed=8 * mine.size, transcendentals=4 * rows * LAT
        ),
        name="tail",
    )(place, parts, mine, other, picked, var_of, mask)


def body(
    post_deter,
    post_sample,
    samples,
    actions,
    counts,
    w_stoch,
    w_action,
    w_gate,
    w_rec,
    w_prior_in,
    w_prior_out,
    n_dp,
):
    rows = post_deter.shape[0]
    depth = w_gate.shape[0]
    tensor_n = NX * NC
    share = rows // tensor_n
    me = lax.axis_index("tensor")
    place = jnp.stack([me // NC, me % NC]).astype(jnp.int32)

    n_far = n_dp // NY // NEAR
    sent = split_call(w_gate, n_far).reshape(n_far * NY, depth, -1)
    held = lax.all_to_all(sent, "dp", 0, 0, axis_index_groups=far_groups(n_dp)).reshape(n_far * NY * depth, -1)
    gate = jnp.broadcast_to(held[None], (NEAR,) + held.shape)
    gate = lax.all_to_all(gate, "dp", 0, 0, axis_index_groups=near_groups(n_dp))

    action_rows = jnp.pad(w_action, ((0, LANES - ACTIONS), (0, 0)))
    mine = x_gather(jnp.concatenate([w_stoch, action_rows], axis=0))
    other = core_swap(mine)

    first_latent, first_samples, late_actions, _ = lax.optimization_barrier((post_sample, samples[0], actions, held))
    columns = [first_latent, first_samples] + [late_actions[k][:, None] for k in range(IMAG)]
    pack = jnp.concatenate(columns, axis=1).astype(jnp.bfloat16)
    pack = jnp.pad(pack, ((0, 0), (0, LANES - pack.shape[1])))
    pack = jnp.stack([pack] + [y_shift(pack, b, n_dp) for b in range(1, NY)])
    y = lax.axis_index("dp") % NY
    pack = jnp.stack([lax.dynamic_index_in_dim(pack, (y - b + NY) % NY, 0, keepdims=False) for b in range(NY)])

    features = features_call(place, pack, mine, other)
    sums = lax.all_to_all(gate_call(features, gate, n_far), "dp", 0, 0, axis_index_groups=y_groups(n_dp))

    w_out_late, _ = lax.optimization_barrier((w_prior_out, features))
    out_mine = x_gather(w_out_late)

    positions = jnp.arange(STEPS, dtype=jnp.int32)
    valid_mask = (positions[None, :] < counts[:, None]).reshape(rows)
    my_mask = lax.dynamic_slice_in_dim(valid_mask, me * share, share, 0).astype(jnp.float32)
    my_mask = jnp.concatenate([my_mask] * IMAG)[:, None]
    picked = lax.dynamic_slice_in_dim(samples, me * share, share, 1)
    picked = picked.reshape(IMAG * share, STOCH).astype(jnp.bfloat16)

    deter, keep, send = gru_call(place, post_deter, w_rec[0], w_prior_in, sums)
    pair = (keep.astype(jnp.float32) + core_swap(send).astype(jnp.float32)).astype(jnp.bfloat16)
    parts = lax.all_to_all(pair.reshape(NX, IMAG * share, UNITS), "tensor", 0, 0, axis_index_groups=x_groups())
    out_mine, _ = lax.optimization_barrier((out_mine, pair))
    out_other = core_swap(out_mine)
    logs = tail_call(place, parts, out_mine, out_other, picked, my_mask)
    logs = lax.all_to_all(logs, "tensor", 0, 0)[:, 0, : IMAG * share]
    log_prob = logs.reshape(tensor_n, IMAG, share).transpose(1, 0, 2).reshape(IMAG, rows)
    deter_out = jnp.where(valid_mask[:, None], deter, jnp.zeros_like(deter))
    return (deter_out, log_prob)


def solution(mesh):
    in_specs = (
        P("dp", "tensor"),
        P("dp", None),
        P(None, "dp", None),
        P(None, "dp"),
        P("dp"),
        P(None, "tensor"),
        P(None, "tensor"),
        P("dp", "tensor"),
        P("tensor", None, None),
        P("tensor", None),
        P(None, "tensor"),
    )
    out_specs = (P("dp", "tensor"), P(None, "dp"))
    whole = functools.partial(body, n_dp=mesh.shape["dp"])
    return jax.shard_map(whole, mesh=mesh, in_specs=in_specs, out_specs=out_specs, check_vma=False)
```

```python
import functools

import jax
import jax.numpy as jnp
from jax import lax
from jax.experimental import pallas as pl
from jax.experimental.pallas import tpu as pltpu
from jax.sharding import PartitionSpec as P

STOCH = 32
CLASSES = 32
LAT = STOCH * CLASSES
ACTIONS = 18
STEPS = 64
IMAG = 2
UNITS = 1024
NY = 4
NX = 4
NC = 2
NEAR = 4
LANES = 128
CODES = 80
EPS = 1e-06
MIB = 1024 * 1024


def y_groups(n_dp):
    return [[start + y for y in range(NY)] for start in range(0, n_dp, NY)]


def far_groups(n_dp):
    n_far = n_dp // NY // NEAR
    return [[(far * NEAR + near) * NY + y for far in range(n_far)] for near in range(NEAR) for y in range(NY)]


def y_shift(value, step, n_dp):
    perm = [(i, i // NY * NY + (i % NY + step) % NY) for i in range(n_dp)]
    return lax.ppermute(value, "dp", perm)


def z_shift(value, step, n_dp):
    return lax.ppermute(value, "dp", [(i, (i + step * NY) % n_dp) for i in range(n_dp)])


def x_shift(value, step):
    count = NX * NC
    perm = [(i, (i + step * NC) % count) for i in range(count)]
    return lax.ppermute(value, "tensor", perm)


def core_swap(value):
    perm = [(i, i ^ 1) for i in range(NX * NC)]
    return lax.ppermute(value, "tensor", perm)


def x_gather(value):
    return jnp.stack([value] + [x_shift(value, step) for step in range(1, NX)])


def silu(value):
    half = 0.5 * value
    return half + half * jnp.tanh(half)


def sigmoid(value):
    return 0.5 + 0.5 * jnp.tanh(0.5 * value)


def prep_kernel(w_ref, latent_ref, samples_ref, actions_ref, out_ref):
    depth = w_ref.shape[0]
    part = w_ref.shape[1] // 3 // NY
    rows = out_ref.shape[2]
    line = lax.broadcasted_iota(jnp.int32, (CODES - IMAG * STOCH, rows), 0)
    acts = jnp.zeros((CODES - IMAG * STOCH, rows), jnp.float32)
    for k in range(IMAG):
        acts = jnp.where(line == k, actions_ref[k : k + 1].astype(jnp.float32), acts)
    codes = [latent_ref[...].astype(jnp.float32), samples_ref[0].astype(jnp.float32), acts]
    codes = jnp.concatenate(codes, axis=0).astype(jnp.bfloat16)
    for y in range(NY):
        for which in range(3):
            columns = w_ref[:, (which * NY + y) * part : (which * NY + y + 1) * part]
            out_ref[y, which // 2 * depth : (which // 2 + 1) * depth, which % 2 * part : (which % 2 + 1) * part] = columns
        out_ref[y, depth : 2 * depth, part:] = jnp.zeros((depth, rows - part), jnp.bfloat16)
        out_ref[y, 2 * depth :] = codes


def prep_call(w_gate, latent, samples, actions):
    depth = w_gate.shape[0]
    rows = latent.shape[1]
    vmem = pl.BlockSpec(memory_space=pltpu.VMEM)
    return pl.pallas_call(
        prep_kernel,
        in_specs=[vmem] * 4,
        out_specs=vmem,
        out_shape=jax.ShapeDtypeStruct((NY, 2 * depth + CODES, rows), jnp.bfloat16),
        compiler_params=pltpu.CompilerParams(vmem_limit_bytes=16 * MIB),
        cost_estimate=pl.CostEstimate(flops=0, bytes_accessed=NY * rows * 512, transcendentals=0),
        name="prep",
    )(w_gate, latent, samples, actions)


def copies_kernel(came_ref, out_ref):
    depth = out_ref.shape[1] // NY
    part = out_ref.shape[2] // 3
    for y in range(NY):
        for far in range(out_ref.shape[0]):
            here = slice(y * depth, (y + 1) * depth)
            out_ref[far, here, : 2 * part] = came_ref[y, :depth, : 2 * part]
            out_ref[far, here, 2 * part :] = came_ref[y, depth : 2 * depth, :part]


def copies_call(came, n_far, depth, width):
    vmem = pl.BlockSpec(memory_space=pltpu.VMEM)
    return pl.pallas_call(
        copies_kernel,
        in_specs=[vmem],
        out_specs=vmem,
        out_shape=jax.ShapeDtypeStruct((n_far, NY * depth, width), jnp.bfloat16),
        compiler_params=pltpu.CompilerParams(vmem_limit_bytes=16 * MIB),
        cost_estimate=pl.CostEstimate(flops=0, bytes_accessed=4 * n_far * depth * width, transcendentals=0),
        name="copies",
    )(came)


def features_kernel(place_ref, came_ref, spread_ref, target_ref, mine_ref, other_ref, out0_ref, out1_ref, w_ref):
    x, core, y = place_ref[0], place_ref[1], place_ref[2]
    width = w_ref.shape[0]
    rows = out0_ref.shape[0]

    @pl.when(pl.program_id(0) == 0)
    def _():
        for i in range(NX):
            base = lax.rem(x + NX - i, NX) * NC
            w_ref[:, pl.ds(pl.multiple_of((base + core) * LANES, LANES), LANES)] = mine_ref[i]
            w_ref[:, pl.ds(pl.multiple_of((base + 1 - core) * LANES, LANES), LANES)] = other_ref[i]

    codes = came_ref[lax.rem(y + pl.program_id(0), NY)][came_ref.shape[1] - CODES :]
    spread = lax.dot_general(codes, spread_ref[...], (((0,), (0,)), ((), ())), preferred_element_type=jnp.float32)
    spread = jnp.concatenate([spread[:, :width], spread[:, width:]], axis=0)
    hot = jnp.where(spread == target_ref[...], 1.0, 0.0).astype(jnp.bfloat16)
    pre = jnp.dot(hot, w_ref[...], preferred_element_type=jnp.float32)
    scale = lax.rsqrt(jnp.mean(pre * pre, axis=1, keepdims=True) + EPS)
    features = silu(pre * scale).astype(jnp.bfloat16)
    out0_ref[...] = features[:rows]
    out1_ref[...] = features[rows:]


def features_call(place, came, mine, other):
    rows = came.shape[2]
    width = mine.shape[1]
    lane = jnp.arange(width, dtype=jnp.int32)
    is_lat = lane < LAT
    target = jnp.where(is_lat, lane % CLASSES, lane - LAT).astype(jnp.float32)[None, :]
    source = [jnp.where(is_lat, k * STOCH + lane // CLASSES, IMAG * STOCH + k) for k in range(IMAG)]
    source = jnp.concatenate(source)
    spread = (jnp.arange(CODES, dtype=jnp.int32)[:, None] == source[None, :]).astype(jnp.bfloat16)
    out = pltpu.HBM((NY, rows, UNITS), jnp.bfloat16)
    return pl.pallas_call(
        features_kernel,
        grid=(NY,),
        in_specs=[
            pl.BlockSpec(memory_space=pltpu.SMEM),
            pl.BlockSpec(came.shape, lambda b: (0, 0, 0)),
            pl.BlockSpec(spread.shape, lambda b: (0, 0)),
            pl.BlockSpec((1, width), lambda b: (0, 0)),
            pl.BlockSpec((NX, width, LANES), lambda b: (0, 0, 0)),
            pl.BlockSpec((NX, width, LANES), lambda b: (0, 0, 0)),
        ],
        out_specs=[pl.BlockSpec((None, rows, UNITS), lambda b: (b, 0, 0))] * IMAG,
        out_shape=[out] * IMAG,
        scratch_shapes=[pltpu.VMEM((width, UNITS), jnp.bfloat16)],
        compiler_params=pltpu.CompilerParams(vmem_limit_bytes=32 * MIB),
        cost_estimate=pl.CostEstimate(
            flops=2 * IMAG * NY * rows * width * (UNITS + LANES),
            bytes_accessed=IMAG * NY * rows * UNITS * 2 + width * UNITS * 2,
            transcendentals=IMAG * NY * rows * UNITS,
        ),
        name="features",
    )(place, came, spread, target, mine, other)


def gate_kernel(n_far, place_ref, features_ref, g0_ref, g1_ref, g2_ref, g3_ref, o0_ref, o1_ref, o2_ref, o3_ref, w_ref):
    outs = (o0_ref, o1_ref, o2_ref, o3_ref)
    depth = g0_ref.shape[0] // n_far
    near = place_ref[3]
    each, rows = features_ref.shape[:2]

    @pl.when(pl.program_id(0) == 0)
    def _():
        for i, g_ref in enumerate((g0_ref, g1_ref, g2_ref, g3_ref)):
            from_near = lax.rem(near + NEAR - i, NEAR)
            for far in range(n_far):
                start = pl.multiple_of((far * NEAR + from_near) * depth, depth)
                w_ref[pl.ds(start, depth)] = g_ref[far * depth : (far + 1) * depth]

    flat = features_ref[...].reshape(each * rows, UNITS)
    total = jnp.dot(flat, w_ref[...], preferred_element_type=jnp.float32).astype(jnp.bfloat16)
    for step in range(NY // each):

        @pl.when(pl.program_id(0) == step)
        def _():
            for i in range(each):
                outs[step * each + i][...] = total[i * rows : (i + 1) * rows]


def gate_call(place, features, held, n_far):
    rows = features.shape[1]
    width = held[0].shape[1]
    each = 2
    whole = pl.BlockSpec(held[0].shape, lambda b: (0, 0))
    return pl.pallas_call(
        functools.partial(gate_kernel, n_far),
        grid=(NY // each,),
        in_specs=[
            pl.BlockSpec(memory_space=pltpu.SMEM),
            pl.BlockSpec((each, rows, UNITS), lambda b: (b, 0, 0)),
        ]
        + [whole] * NEAR,
        out_specs=[pl.BlockSpec((rows, width), lambda b: (0, 0))] * NY,
        out_shape=[jax.ShapeDtypeStruct((rows, width), jnp.bfloat16)] * NY,
        scratch_shapes=[pltpu.VMEM((UNITS, width), jnp.bfloat16)],
        compiler_params=pltpu.CompilerParams(vmem_limit_bytes=24 * MIB),
        cost_estimate=pl.CostEstimate(
            flops=2 * NY * rows * UNITS * width,
            bytes_accessed=NY * rows * (UNITS + width) * 2 + UNITS * width * 2,
            transcendentals=0,
        ),
        name="gate",
    )(place, features, *held)


def gru_kernel(place_ref, deter_ref, w_rec_ref, w_in_ref, f0_ref, f1_ref, f2_ref, f3_ref, new_ref, prior_ref, rec_ref):
    y = place_ref[2]
    bw = deter_ref.shape[1]
    part = bw // NY
    rec_ref[...] = jnp.dot(deter_ref[...], w_rec_ref[...], preferred_element_type=jnp.float32)
    for i, f_ref in enumerate((f0_ref, f1_ref, f2_ref, f3_ref)):
        off = pl.multiple_of(lax.rem(y + NY - i, NY) * part, part)

        def gate(which):
            mine = f_ref[:, which * part : (which + 1) * part].astype(jnp.float32)
            return rec_ref[:, pl.ds(pl.multiple_of(which * bw + off, part), part)] + mine

        reset = sigmoid(gate(0))
        candidate = jnp.tanh(reset * gate(1))
        update = sigmoid(gate(2) - 1.0)
        old = deter_ref[:, pl.ds(off, part)].astype(jnp.float32)
        fresh = update * candidate + (1.0 - update) * old
        new_ref[:, pl.ds(off, part)] = fresh.astype(jnp.bfloat16)
    prior_ref[...] = jnp.dot(new_ref[...], w_in_ref[...], preferred_element_type=jnp.float32).astype(jnp.bfloat16)


def gru_call(place, deter, w_rec, w_in, sums):
    rows, bw = deter.shape
    vmem = pl.BlockSpec(memory_space=pltpu.VMEM)
    return pl.pallas_call(
        gru_kernel,
        in_specs=[pl.BlockSpec(memory_space=pltpu.SMEM)] + [vmem] * 7,
        out_specs=[vmem, vmem],
        out_shape=[
            jax.ShapeDtypeStruct((rows, bw), jnp.bfloat16),
            jax.ShapeDtypeStruct((rows, w_in.shape[1]), jnp.bfloat16),
        ],
        scratch_shapes=[pltpu.VMEM((rows, 3 * bw), jnp.float32)],
        compiler_params=pltpu.CompilerParams(vmem_limit_bytes=24 * MIB),
        cost_estimate=pl.CostEstimate(
            flops=2 * rows * bw * (3 * bw + w_in.shape[1]),
            bytes_accessed=2 * (w_rec.size + w_in.size) + 12 * rows * bw,
            transcendentals=3 * rows * bw,
        ),
        name="gru",
    )(place, deter, w_rec, w_in, *sums)


def tail_kernel(step, place_ref, parts_ref, mine_ref, other_ref, picked_ref, var_ref, mask_ref, prev_ref, log_ref):
    pre = parts_ref[0].astype(jnp.float32)
    for i in range(1, parts_ref.shape[0]):
        pre = pre + parts_ref[i].astype(jnp.float32)
    normed = pre * lax.rsqrt(jnp.mean(pre * pre, axis=1, keepdims=True) + EPS)
    hidden = silu(normed).astype(jnp.bfloat16)
    rows = hidden.shape[0]
    cls = lax.broadcasted_iota(jnp.int32, (rows, LANES), 1) % CLASSES

    def within(value, combine):
        step = 1
        while step < CLASSES:
            ahead = pltpu.roll(value, step, 1)
            wrapped = pltpu.roll(value, LANES - CLASSES + step, 1)
            value = combine(value, jnp.where(cls >= step, ahead, wrapped))
            step *= 2
        return value

    total = jnp.zeros((rows, LANES), jnp.float32)
    x, core = place_ref[0], place_ref[1]
    for i in range(NX * NC):
        w_ref = mine_ref if i % NC == 0 else other_ref
        piece = lax.rem(x + NX - i // NC, NX) * NC + (core if i % NC == 0 else 1 - core)
        here = pl.ds(pl.multiple_of(piece * LANES, LANES), LANES)
        logits = jnp.dot(hidden, w_ref[i // NC], preferred_element_type=jnp.float32)
        powers = jnp.exp(logits - within(logits, jnp.maximum))
        probs = 0.99 * (powers / within(powers, jnp.add)) + 0.01 / CLASSES
        want = jnp.dot(picked_ref[...], var_ref[:, here], preferred_element_type=jnp.float32)
        total = total + jnp.where(cls.astype(jnp.float32) == want, jnp.log(probs), 0.0)
    summed = jnp.where(mask_ref[...] > 0, jnp.sum(total, axis=1, keepdims=True), 0.0)
    lanes = lax.broadcasted_iota(jnp.int32, (rows, LANES), 1)
    diagonal = lax.broadcasted_iota(jnp.int32, (rows, LANES), 0) == lanes
    line = jnp.sum(jnp.where(diagonal, summed, 0.0), axis=0, keepdims=True)
    here = lax.broadcasted_iota(jnp.int32, log_ref.shape, 1) == step
    log_ref[...] = jnp.where(here, line[None], prev_ref[...])


def tail_call(step, place, parts, mine, other, picked, mask, prev):
    rows = parts.shape[1]
    lane = jnp.arange(LAT, dtype=jnp.int32)
    var_of = (jnp.arange(STOCH, dtype=jnp.int32)[:, None] == lane[None, :] // CLASSES).astype(jnp.bfloat16)
    vmem = pl.BlockSpec(memory_space=pltpu.VMEM)
    return pl.pallas_call(
        functools.partial(tail_kernel, step),
        in_specs=[pl.BlockSpec(memory_space=pltpu.SMEM)] + [vmem] * 7,
        out_specs=vmem,
        out_shape=jax.ShapeDtypeStruct(prev.shape, jnp.float32),
        compiler_params=pltpu.CompilerParams(vmem_limit_bytes=24 * MIB),
        cost_estimate=pl.CostEstimate(
            flops=2 * rows * UNITS * LAT, bytes_accessed=8 * mine.size, transcendentals=4 * rows * LAT
        ),
        name="tail",
    )(place, parts, mine, other, picked, var_of, mask, prev)


def body(
    post_deter,
    post_sample,
    samples,
    actions,
    counts,
    w_stoch,
    w_action,
    w_gate,
    w_rec,
    w_prior_in,
    w_prior_out,
    n_dp,
):
    rows = post_deter.shape[0]
    depth = w_gate.shape[0]
    tensor_n = NX * NC
    share = rows // tensor_n
    n_far = n_dp // NY // NEAR
    me, dp_index = lax.axis_index("tensor"), lax.axis_index("dp")
    place = jnp.stack([me // NC, me % NC, dp_index % NY, dp_index // NY % NEAR]).astype(jnp.int32)

    sent = prep_call(w_gate, post_sample.T, samples.transpose(0, 2, 1), actions)
    came = lax.all_to_all(sent, "dp", 0, 0, axis_index_groups=y_groups(n_dp))
    held = copies_call(came, n_far, depth, w_gate.shape[1] // NY)
    held = lax.all_to_all(held, "dp", 0, 0, axis_index_groups=far_groups(n_dp)).reshape(n_far * NY * depth, -1)
    held = [held] + [z_shift(held, step, n_dp) for step in range(1, NEAR)]

    action_rows = jnp.pad(w_action, ((0, LANES - ACTIONS), (0, 0)))
    mine = x_gather(jnp.concatenate([w_stoch, action_rows], axis=0))
    other = core_swap(mine)
    features = features_call(place, came, mine, other)

    out_mine = x_gather(w_prior_out)
    out_other = core_swap(out_mine)

    positions = jnp.arange(STEPS, dtype=jnp.int32)
    valid_mask = (positions[None, :] < counts[:, None]).reshape(rows)
    my_mask = lax.dynamic_slice_in_dim(valid_mask, me * share, share, 0).astype(jnp.float32)[:, None]
    picked = lax.dynamic_slice_in_dim(samples, me * share, share, 1).astype(jnp.bfloat16)

    sums = []
    for k in range(IMAG):
        pieces = gate_call(place, features[k], held, n_far)
        sums.append([pieces[0]] + [y_shift(pieces[i], i, n_dp) for i in range(1, NY)])

    deter = post_deter
    logs = jnp.zeros((tensor_n, 8, LANES), jnp.float32)
    for k in range(IMAG):
        deter, partial = gru_call(place, deter, w_rec[0], w_prior_in, sums[k])
        parts = lax.all_to_all(partial.reshape(tensor_n, share, UNITS), "tensor", 0, 0)
        logs = tail_call(k, place, parts, out_mine, out_other, picked[k], my_mask, logs)
    logs = lax.all_to_all(logs, "tensor", 0, 0)[:, :IMAG, :share]
    log_prob = logs.transpose(1, 0, 2).reshape(IMAG, rows)
    deter_out = jnp.where(valid_mask[:, None], deter, jnp.zeros_like(deter))
    return (deter_out, log_prob)


def solution(mesh):
    in_specs = (
        P("dp", "tensor"),
        P("dp", None),
        P(None, "dp", None),
        P(None, "dp"),
        P("dp"),
        P(None, "tensor"),
        P(None, "tensor"),
        P("dp", "tensor"),
        P("tensor", None, None),
        P("tensor", None),
        P(None, "tensor"),
    )
    out_specs = (P("dp", "tensor"), P(None, "dp"))
    whole = functools.partial(body, n_dp=mesh.shape["dp"])
    return jax.shard_map(whole, mesh=mesh, in_specs=in_specs, out_specs=out_specs, check_vma=False)
```

```python
import functools

import jax
import jax.numpy as jnp
from jax import lax
from jax.experimental import pallas as pl
from jax.experimental.pallas import tpu as pltpu
from jax.sharding import PartitionSpec as P

STOCH = 32
CLASSES = 32
LAT = STOCH * CLASSES
ACTIONS = 18
STEPS = 64
IMAG = 2
UNITS = 1024
NY = 4
NX = 4
NC = 2
LANES = 128
CODES = 80
EPS = 1e-06
MIB = 1024 * 1024


def y_groups(n_dp):
    return [[start + y for y in range(NY)] for start in range(0, n_dp, NY)]


def z_groups(n_dp):
    return [list(range(y, n_dp, NY)) for y in range(NY)]


def x_shift(value, step):
    count = NX * NC
    perm = [(i, (i + step * NC) % count) for i in range(count)]
    return lax.ppermute(value, "tensor", perm)


def core_swap(value):
    perm = [(i, i ^ 1) for i in range(NX * NC)]
    return lax.ppermute(value, "tensor", perm)


def tensor_gather(value):
    mine = jnp.stack([value] + [x_shift(value, step) for step in range(1, NX)])
    return mine, core_swap(mine)


def silu(value):
    half = 0.5 * value
    return half + half * jnp.tanh(half)


def sigmoid(value):
    return 0.5 + 0.5 * jnp.tanh(0.5 * value)


def prep_kernel(w_ref, latent_ref, samples_ref, actions_ref, out_ref):
    depth = w_ref.shape[0]
    part = w_ref.shape[1] // 3 // NY
    rows = out_ref.shape[2]
    line = lax.broadcasted_iota(jnp.int32, (CODES - IMAG * STOCH, rows), 0)
    acts = jnp.zeros((CODES - IMAG * STOCH, rows), jnp.float32)
    for k in range(IMAG):
        acts = jnp.where(line == k, actions_ref[k : k + 1].astype(jnp.float32), acts)
    codes = [latent_ref[...].astype(jnp.float32), samples_ref[0].astype(jnp.float32), acts]
    codes = jnp.concatenate(codes, axis=0).astype(jnp.bfloat16)
    for y in range(NY):
        for which in range(3):
            columns = w_ref[:, (which * NY + y) * part : (which * NY + y + 1) * part]
            out_ref[y, which // 2 * depth : (which // 2 + 1) * depth, which % 2 * part : (which % 2 + 1) * part] = columns
        out_ref[y, depth : 2 * depth, part:] = jnp.zeros((depth, rows - part), jnp.bfloat16)
        out_ref[y, 2 * depth :] = codes


def prep_call(w_gate, latent, samples, actions):
    depth = w_gate.shape[0]
    rows = latent.shape[1]
    vmem = pl.BlockSpec(memory_space=pltpu.VMEM)
    return pl.pallas_call(
        prep_kernel,
        in_specs=[vmem] * 4,
        out_specs=vmem,
        out_shape=jax.ShapeDtypeStruct((NY, 2 * depth + CODES, rows), jnp.bfloat16),
        compiler_params=pltpu.CompilerParams(vmem_limit_bytes=60 * MIB),
        cost_estimate=pl.CostEstimate(flops=0, bytes_accessed=NY * rows * 512, transcendentals=0),
        name="prep",
    )(w_gate, latent, samples, actions)


def copies_kernel(came_ref, out_ref):
    depth = out_ref.shape[1] // NY
    part = out_ref.shape[2] // 3
    for y in range(NY):
        for z in range(out_ref.shape[0]):
            here = slice(y * depth, (y + 1) * depth)
            out_ref[z, here, : 2 * part] = came_ref[y, :depth, : 2 * part]
            out_ref[z, here, 2 * part :] = came_ref[y, depth : 2 * depth, :part]


def copies_call(came, n_z, depth, width):
    vmem = pl.BlockSpec(memory_space=pltpu.VMEM)
    return pl.pallas_call(
        copies_kernel,
        in_specs=[vmem],
        out_specs=vmem,
        out_shape=jax.ShapeDtypeStruct((n_z, NY * depth, width), jnp.bfloat16),
        compiler_params=pltpu.CompilerParams(vmem_limit_bytes=60 * MIB),
        cost_estimate=pl.CostEstimate(flops=0, bytes_accessed=4 * n_z * depth * width, transcendentals=0),
        name="copies",
    )(came)


def features_kernel(place_ref, came_ref, spread_ref, target_ref, mine_ref, other_ref, out_ref, w_ref):
    x, core = place_ref[0], place_ref[1]
    width = w_ref.shape[0]
    rows = out_ref.shape[1]

    @pl.when(pl.program_id(0) == 0)
    def _():
        for i in range(NX):
            base = lax.rem(x + NX - i, NX) * NC
            w_ref[:, pl.ds(pl.multiple_of((base + core) * LANES, LANES), LANES)] = mine_ref[i]
            w_ref[:, pl.ds(pl.multiple_of((base + 1 - core) * LANES, LANES), LANES)] = other_ref[i]

    codes = came_ref[came_ref.shape[0] - CODES :]
    spread = lax.dot_general(codes, spread_ref[...], (((0,), (0,)), ((), ())), preferred_element_type=jnp.float32)
    spread = jnp.concatenate([spread[:, :width], spread[:, width:]], axis=0)
    hot = jnp.where(spread == target_ref[...], 1.0, 0.0).astype(jnp.bfloat16)
    pre = jnp.dot(hot, w_ref[...], preferred_element_type=jnp.float32)
    scale = lax.rsqrt(jnp.mean(pre * pre, axis=1, keepdims=True) + EPS)
    features = silu(pre * scale).astype(jnp.bfloat16)
    for k in range(IMAG):
        out_ref[k] = features[k * rows : (k + 1) * rows]


def features_call(place, came, mine, other):
    rows = came.shape[2]
    width = mine.shape[1]
    lane = jnp.arange(width, dtype=jnp.int32)
    is_lat = lane < LAT
    target = jnp.where(is_lat, lane % CLASSES, lane - LAT).astype(jnp.float32)[None, :]
    source = [jnp.where(is_lat, k * STOCH + lane // CLASSES, IMAG * STOCH + k) for k in range(IMAG)]
    source = jnp.concatenate(source)
    spread = (jnp.arange(CODES, dtype=jnp.int32)[:, None] == source[None, :]).astype(jnp.bfloat16)
    return pl.pallas_call(
        features_kernel,
        grid=(NY,),
        in_specs=[
            pl.BlockSpec(memory_space=pltpu.SMEM),
            pl.BlockSpec((None,) + came.shape[1:], lambda b: (b, 0, 0)),
            pl.BlockSpec(spread.shape, lambda b: (0, 0)),
            pl.BlockSpec((1, width), lambda b: (0, 0)),
            pl.BlockSpec((NX, width, LANES), lambda b: (0, 0, 0)),
            pl.BlockSpec((NX, width, LANES), lambda b: (0, 0, 0)),
        ],
        out_specs=pl.BlockSpec((IMAG, None, rows, UNITS), lambda b: (0, b, 0, 0)),
        out_shape=pltpu.HBM((IMAG, NY, rows, UNITS), jnp.bfloat16),
        scratch_shapes=[pltpu.VMEM((width, UNITS), jnp.bfloat16)],
        compiler_params=pltpu.CompilerParams(vmem_limit_bytes=32 * MIB),
        cost_estimate=pl.CostEstimate(
            flops=2 * IMAG * NY * rows * width * (UNITS + LANES),
            bytes_accessed=IMAG * NY * rows * UNITS * 2 + width * UNITS * 2,
            transcendentals=IMAG * NY * rows * UNITS,
        ),
        name="features",
    )(place, came, spread, target, mine, other)


def gate_kernel(features_ref, gate_ref, out_ref):
    for k in range(IMAG):
        out_ref[k] = jnp.dot(features_ref[k], gate_ref[...], preferred_element_type=jnp.float32).astype(jnp.bfloat16)


def gate_call(features, gate):
    rows = features.shape[2]
    width = gate.shape[1]
    return pl.pallas_call(
        gate_kernel,
        grid=(NY,),
        in_specs=[
            pl.BlockSpec((IMAG, None, rows, UNITS), lambda b: (0, b, 0, 0)),
            pl.BlockSpec((UNITS, width), lambda b: (0, 0)),
        ],
        out_specs=pl.BlockSpec((None, IMAG, rows, width), lambda b: (b, 0, 0, 0)),
        out_shape=jax.ShapeDtypeStruct((NY, IMAG, rows, width), jnp.bfloat16),
        compiler_params=pltpu.CompilerParams(vmem_limit_bytes=32 * MIB),
        cost_estimate=pl.CostEstimate(
            flops=2 * IMAG * NY * rows * UNITS * width,
            bytes_accessed=IMAG * NY * rows * (UNITS + width) * 2 + UNITS * width * 2,
            transcendentals=0,
        ),
        name="gate",
    )(features, gate)


def gru_kernel(deter_ref, w_rec_ref, w_in_ref, f_ref, new_ref, prior_ref, mid_ref):
    rows, bw = deter_ref.shape
    part = bw // NY
    for k in range(IMAG):
        old_ref = deter_ref if k == 0 else mid_ref
        next_ref = new_ref if k == IMAG - 1 else mid_ref
        old = old_ref[...]
        rec = jnp.dot(old, w_rec_ref[...], preferred_element_type=jnp.float32)
        for q in range(NY):

            def gate(which):
                mine = f_ref[q, k, :, which * part : (which + 1) * part].astype(jnp.float32)
                return rec[:, which * bw + q * part : which * bw + (q + 1) * part] + mine

            reset = sigmoid(gate(0))
            candidate = jnp.tanh(reset * gate(1))
            update = sigmoid(gate(2) - 1.0)
            before = old[:, q * part : (q + 1) * part].astype(jnp.float32)
            fresh = update * candidate + (1.0 - update) * before
            next_ref[:, q * part : (q + 1) * part] = fresh.astype(jnp.bfloat16)
        prior = jnp.dot(next_ref[...], w_in_ref[...], preferred_element_type=jnp.float32).astype(jnp.bfloat16)
        share = prior_ref.shape[2]
        for j in range(prior_ref.shape[0]):
            prior_ref[j, k] = prior[j * share : (j + 1) * share]


def gru_call(deter, w_rec, w_in, sums, tensor_n):
    rows, bw = deter.shape
    vmem = pl.BlockSpec(memory_space=pltpu.VMEM)
    return pl.pallas_call(
        gru_kernel,
        in_specs=[vmem] * 4,
        out_specs=[vmem, vmem],
        out_shape=[
            jax.ShapeDtypeStruct((rows, bw), jnp.bfloat16),
            jax.ShapeDtypeStruct((tensor_n, IMAG, rows // tensor_n, w_in.shape[1]), jnp.bfloat16),
        ],
        scratch_shapes=[pltpu.VMEM((rows, bw), jnp.bfloat16)],
        compiler_params=pltpu.CompilerParams(vmem_limit_bytes=32 * MIB),
        cost_estimate=pl.CostEstimate(
            flops=2 * IMAG * rows * bw * (3 * bw + w_in.shape[1]),
            bytes_accessed=2 * (w_rec.size + w_in.size) + 24 * rows * bw,
            transcendentals=6 * rows * bw,
        ),
        name="gru",
    )(deter, w_rec, w_in, sums)


def tail_kernel(me_ref, parts_ref, mine_ref, other_ref, picked_ref, var_ref, mask_ref, log_ref):
    pre = parts_ref[0].astype(jnp.float32)
    for i in range(1, parts_ref.shape[0]):
        pre = pre + parts_ref[i].astype(jnp.float32)
    normed = pre * lax.rsqrt(jnp.mean(pre * pre, axis=1, keepdims=True) + EPS)
    hidden = (silu(normed)).astype(jnp.bfloat16)
    rows = hidden.shape[0]
    cls = lax.broadcasted_iota(jnp.int32, (rows, LANES), 1) % CLASSES

    def within(value, combine):
        step = 1
        while step < CLASSES:
            ahead = pltpu.roll(value, step, 1)
            wrapped = pltpu.roll(value, LANES - CLASSES + step, 1)
            value = combine(value, jnp.where(cls >= step, ahead, wrapped))
            step *= 2
        return value

    total = jnp.zeros((rows, LANES), jnp.float32)
    x, core = me_ref[0], me_ref[1]
    for i in range(NX * NC):
        w_ref = mine_ref if i % NC == 0 else other_ref
        piece = lax.rem(x + NX - i // NC, NX) * NC + (core if i % NC == 0 else 1 - core)
        here = pl.ds(pl.multiple_of(piece * LANES, LANES), LANES)
        logits = jnp.dot(hidden, w_ref[i // NC], preferred_element_type=jnp.float32)
        powers = jnp.exp(logits - within(logits, jnp.maximum))
        probs = 0.99 * (powers / within(powers, jnp.add)) + 0.01 / CLASSES
        want = jnp.dot(picked_ref[...], var_ref[:, here], preferred_element_type=jnp.float32)
        total = total + jnp.where(cls.astype(jnp.float32) == want, jnp.log(probs), 0.0)
    summed = jnp.where(mask_ref[...] > 0, jnp.sum(total, axis=1, keepdims=True), 0.0)
    lanes = lax.broadcasted_iota(jnp.int32, (rows, LANES), 1)
    diagonal = lax.broadcasted_iota(jnp.int32, (rows, LANES), 0) == lanes
    line = jnp.sum(jnp.where(diagonal, summed, 0.0), axis=0, keepdims=True)
    log_ref[...] = jnp.broadcast_to(line[None], log_ref.shape)


def tail_call(place, parts, mine, other, picked, mask):
    tensor_n, rows = parts.shape[:2]
    lane = jnp.arange(LAT, dtype=jnp.int32)
    var_of = (jnp.arange(STOCH, dtype=jnp.int32)[:, None] == lane[None, :] // CLASSES).astype(jnp.bfloat16)
    vmem = pl.BlockSpec(memory_space=pltpu.VMEM)
    return pl.pallas_call(
        tail_kernel,
        in_specs=[pl.BlockSpec(memory_space=pltpu.SMEM)] + [vmem] * 6,
        out_specs=vmem,
        out_shape=jax.ShapeDtypeStruct((tensor_n, 8, LANES), jnp.float32),
        compiler_params=pltpu.CompilerParams(vmem_limit_bytes=32 * MIB),
        cost_estimate=pl.CostEstimate(
            flops=2 * rows * UNITS * LAT, bytes_accessed=8 * mine.size, transcendentals=4 * rows * LAT
        ),
        name="tail",
    )(place, parts, mine, other, picked, var_of, mask)


def body(
    post_deter,
    post_sample,
    samples,
    actions,
    counts,
    w_stoch,
    w_action,
    w_gate,
    w_rec,
    w_prior_in,
    w_prior_out,
    n_dp,
):
    rows = post_deter.shape[0]
    depth = w_gate.shape[0]
    tensor_n = NX * NC
    share = rows // tensor_n
    me = lax.axis_index("tensor")
    place = jnp.stack([me // NC, me % NC]).astype(jnp.int32)

    sent = prep_call(w_gate, post_sample.T, samples.transpose(0, 2, 1), actions)
    came = lax.all_to_all(sent, "dp", 0, 0, axis_index_groups=y_groups(n_dp))
    held = copies_call(came, n_dp // NY, depth, w_gate.shape[1] // NY)
    gate = lax.all_to_all(held, "dp", 0, 0, axis_index_groups=z_groups(n_dp)).reshape(n_dp * depth, -1)

    action_rows = jnp.pad(w_action, ((0, LANES - ACTIONS), (0, 0)))
    mine, other = tensor_gather(jnp.concatenate([w_stoch, action_rows], axis=0))

    features = features_call(place, came, mine, other)
    sums = lax.all_to_all(gate_call(features, gate), "dp", 0, 0, axis_index_groups=y_groups(n_dp))

    w_out_late, _ = lax.optimization_barrier((w_prior_out, features))
    out_mine, out_other = tensor_gather(w_out_late)

    positions = jnp.arange(STEPS, dtype=jnp.int32)
    valid_mask = (positions[None, :] < counts[:, None]).reshape(rows)
    my_mask = lax.dynamic_slice_in_dim(valid_mask, me * share, share, 0).astype(jnp.float32)
    my_mask = jnp.concatenate([my_mask] * IMAG)[:, None]
    picked = lax.dynamic_slice_in_dim(samples, me * share, share, 1)
    picked = picked.reshape(IMAG * share, STOCH).astype(jnp.bfloat16)

    deter, partial = gru_call(post_deter, w_rec[0], w_prior_in, sums, tensor_n)
    parts = lax.all_to_all(partial.reshape(tensor_n, IMAG * share, UNITS), "tensor", 0, 0)
    logs = tail_call(place, parts, out_mine, out_other, picked, my_mask)
    logs = lax.all_to_all(logs, "tensor", 0, 0)[:, 0, : IMAG * share]
    log_prob = logs.reshape(tensor_n, IMAG, share).transpose(1, 0, 2).reshape(IMAG, rows)
    deter_out = jnp.where(valid_mask[:, None], deter, jnp.zeros_like(deter))
    return (deter_out, log_prob)


def solution(mesh):
    in_specs = (
        P("dp", "tensor"),
        P("dp", None),
        P(None, "dp", None),
        P(None, "dp"),
        P("dp"),
        P(None, "tensor"),
        P(None, "tensor"),
        P("dp", "tensor"),
        P("tensor", None, None),
        P("tensor", None),
        P(None, "tensor"),
    )
    out_specs = (P("dp", "tensor"), P(None, "dp"))
    whole = functools.partial(body, n_dp=mesh.shape["dp"])
    return jax.shard_map(whole, mesh=mesh, in_specs=in_specs, out_specs=out_specs, check_vma=False)
```

```python
import functools

import jax
import jax.numpy as jnp
from jax import lax
from jax.experimental import pallas as pl
from jax.experimental.pallas import tpu as pltpu
from jax.sharding import PartitionSpec as P

STOCH = 32
CLASSES = 32
LAT = STOCH * CLASSES
ACTIONS = 18
STEPS = 64
IMAG = 2
UNITS = 1024
NY = 4
NX = 4
NC = 2
LANES = 128
EMBED = LAT + LANES
NEAR = 4
CODES = 80
EPS = 1e-06
MIB = 1024 * 1024
FEATURES_WEIGHT = 12


def y_groups(n_dp):
    return [[start + y for y in range(NY)] for start in range(0, n_dp, NY)]


def far_groups(n_dp):
    n_far = n_dp // NY // NEAR
    return [[(far * NEAR + near) * NY + y for far in range(n_far) for y in range(NY)] for near in range(NEAR)]


def near_groups(n_dp):
    n_far = n_dp // NY // NEAR
    return [[(far * NEAR + near) * NY + y for near in range(NEAR)] for far in range(n_far) for y in range(NY)]


def diagonal_gather(value, n_dp):
    places = [(z, y, x, core) for z in range(n_dp // NY) for y in range(NY) for x in range(NX) for core in range(NC)]

    def index(z, y, x, core):
        return ((z * NY + y) * NX + x) * NC + core

    pieces = [value]
    for step in range(1, NX):
        perm = [(index(*p), index(p[0], (p[1] + step) % NY, (p[2] + step) % NX, p[3])) for p in places]
        pieces.append(lax.ppermute(value, ("dp", "tensor"), perm))
    return jnp.stack(pieces)


def x_gather(value):
    pieces = [value]
    for step in range(1, NX):
        perm = [(i, (i + step * NC) % (NX * NC)) for i in range(NX * NC)]
        pieces.append(lax.ppermute(value, "tensor", perm))
    return jnp.stack(pieces)


def core_swap(value):
    perm = [(i, i ^ 1) for i in range(NX * NC)]
    return lax.ppermute(value, "tensor", perm)


def silu(value):
    half = 0.5 * value
    return half + half * jnp.tanh(half)


def sigmoid(value):
    return 0.5 + 0.5 * jnp.tanh(0.5 * value)


def split_kernel(w_ref, out_ref):
    part = w_ref.shape[1] // 3 // NY
    for y in range(NY):
        for which in range(3):
            columns = w_ref[:, (which * NY + y) * part : (which * NY + y + 1) * part]
            for z in range(out_ref.shape[0]):
                out_ref[z, y, :, which * part : (which + 1) * part] = columns


def split_call(w_gate, n_z):
    depth, width = w_gate.shape
    vmem = pl.BlockSpec(memory_space=pltpu.VMEM)
    return pl.pallas_call(
        split_kernel,
        in_specs=[vmem],
        out_specs=vmem,
        out_shape=jax.ShapeDtypeStruct((n_z, NY, depth, width // NY), w_gate.dtype),
        compiler_params=pltpu.CompilerParams(vmem_limit_bytes=60 * MIB),
        cost_estimate=pl.CostEstimate(flops=0, bytes_accessed=2 * n_z * depth * width, transcendentals=0),
        name="split",
    )(w_gate)


def prep_kernel(w_stoch_ref, w_action_ref, latent_ref, samples_ref, actions_ref, out_ref):
    rows = latent_ref.shape[1]
    out_ref[:LAT] = w_stoch_ref[...]
    out_ref[LAT:EMBED] = jnp.zeros((EMBED - LAT, LANES), jnp.bfloat16)
    out_ref[LAT : LAT + ACTIONS] = w_action_ref[...]
    line = lax.broadcasted_iota(jnp.int32, (CODES - IMAG * STOCH, rows), 0)
    acts = jnp.zeros((CODES - IMAG * STOCH, rows), jnp.float32)
    for k in range(IMAG):
        acts = jnp.where(line == k, actions_ref[k : k + 1].astype(jnp.float32), acts)
    codes = [latent_ref[...].astype(jnp.float32), samples_ref[0].astype(jnp.float32), acts]
    codes = jnp.concatenate(codes, axis=0).astype(jnp.bfloat16)
    for i in range(rows // LANES):
        out_ref[EMBED + i * CODES : EMBED + (i + 1) * CODES] = codes[:, i * LANES : (i + 1) * LANES]


def prep_call(w_stoch, w_action, latent, samples, actions):
    rows = latent.shape[1]
    vmem = pl.BlockSpec(memory_space=pltpu.VMEM)
    return pl.pallas_call(
        prep_kernel,
        in_specs=[vmem] * 5,
        out_specs=vmem,
        out_shape=jax.ShapeDtypeStruct((EMBED + rows // LANES * CODES, LANES), jnp.bfloat16),
        compiler_params=pltpu.CompilerParams(vmem_limit_bytes=60 * MIB),
        cost_estimate=pl.CostEstimate(flops=0, bytes_accessed=2 * EMBED * LANES * 2, transcendentals=0),
        name="prep",
    )(w_stoch, w_action, latent, samples, actions)


def features_kernel(place_ref, spread_ref, target_ref, mine_ref, other_ref, out_ref, w_ref):
    x, core, y = place_ref[0], place_ref[1], place_ref[2]
    rows = out_ref.shape[1]

    @pl.when(pl.program_id(0) == 0)
    def _():
        for i in range(NX):
            base = lax.rem(x + NX - i, NX) * NC
            w_ref[:, pl.ds(pl.multiple_of((base + core) * LANES, LANES), LANES)] = mine_ref[i, :EMBED]
            w_ref[:, pl.ds(pl.multiple_of((base + 1 - core) * LANES, LANES), LANES)] = other_ref[i, :EMBED]

    source = lax.rem(y + NY - pl.program_id(0), NY)
    spread = []
    for k in range(IMAG):
        for half in range(rows // LANES):
            codes = mine_ref[source, EMBED + half * CODES : EMBED + (half + 1) * CODES]
            wide = spread_ref[:, k * EMBED : (k + 1) * EMBED]
            spread.append(
                lax.dot_general(codes, wide, (((0,), (0,)), ((), ())), preferred_element_type=jnp.float32)
            )
    spread = jnp.concatenate(spread, axis=0)
    hot = jnp.where(spread == target_ref[...], 1.0, 0.0).astype(jnp.bfloat16)
    pre = jnp.dot(hot, w_ref[...], preferred_element_type=jnp.float32)
    scale = lax.rsqrt(jnp.mean(pre * pre, axis=1, keepdims=True) + EPS)
    features = silu(pre * scale).astype(jnp.bfloat16)
    for k in range(IMAG):
        out_ref[k] = features[k * rows : (k + 1) * rows]


def features_call(rows, place, mine, other):
    lane = jnp.arange(EMBED, dtype=jnp.int32)
    is_lat = lane < LAT
    target = jnp.where(is_lat, lane % CLASSES, lane - LAT).astype(jnp.float32)[None, :]
    source = [jnp.where(is_lat, k * STOCH + lane // CLASSES, IMAG * STOCH + k) for k in range(IMAG)]
    source = jnp.concatenate(source)
    spread = (jnp.arange(CODES, dtype=jnp.int32)[:, None] == source[None, :]).astype(jnp.bfloat16)
    return pl.pallas_call(
        features_kernel,
        grid=(NY,),
        in_specs=[
            pl.BlockSpec(memory_space=pltpu.SMEM),
            pl.BlockSpec(spread.shape, lambda b: (0, 0)),
            pl.BlockSpec((1, EMBED), lambda b: (0, 0)),
            pl.BlockSpec(mine.shape, lambda b: (0, 0, 0)),
            pl.BlockSpec(other.shape, lambda b: (0, 0, 0)),
        ],
        out_specs=pl.BlockSpec((IMAG, None, rows, UNITS), lambda b: (0, b, 0, 0)),
        out_shape=pltpu.HBM((IMAG, NY, rows, UNITS), jnp.bfloat16),
        scratch_shapes=[pltpu.VMEM((EMBED, UNITS), jnp.bfloat16)],
        compiler_params=pltpu.CompilerParams(vmem_limit_bytes=32 * MIB),
        cost_estimate=pl.CostEstimate(
            flops=FEATURES_WEIGHT * IMAG * NY * rows * EMBED * (UNITS + LANES) // 5,
            bytes_accessed=IMAG * NY * rows * UNITS * 2 + EMBED * UNITS * 2,
            transcendentals=IMAG * NY * rows * UNITS,
        ),
        name="features",
    )(place, spread, target, mine, other)


def gate_kernel(n_far, features_ref, gate_ref, out_ref, w_ref):
    near, held = gate_ref.shape[:2]
    depth = held // n_far

    @pl.when(pl.program_id(0) == 0)
    def _():
        for i in range(near):
            for far in range(n_far):
                w_ref[(far * near + i) * depth : (far * near + i + 1) * depth] = gate_ref[i, far * depth : (far + 1) * depth]

    for k in range(IMAG):
        out_ref[k] = jnp.dot(features_ref[k], w_ref[...], preferred_element_type=jnp.float32).astype(jnp.bfloat16)


def gate_call(features, gate, n_far):
    rows = features.shape[2]
    width = gate.shape[2]
    return pl.pallas_call(
        functools.partial(gate_kernel, n_far),
        grid=(NY,),
        in_specs=[
            pl.BlockSpec((IMAG, None, rows, UNITS), lambda b: (0, b, 0, 0)),
            pl.BlockSpec(gate.shape, lambda b: (0, 0, 0)),
        ],
        out_specs=pl.BlockSpec((None, IMAG, rows, width), lambda b: (b, 0, 0, 0)),
        out_shape=jax.ShapeDtypeStruct((NY, IMAG, rows, width), jnp.bfloat16),
        scratch_shapes=[pltpu.VMEM((UNITS, width), jnp.bfloat16)],
        compiler_params=pltpu.CompilerParams(vmem_limit_bytes=32 * MIB),
        cost_estimate=pl.CostEstimate(
            flops=2 * IMAG * NY * rows * UNITS * width,
            bytes_accessed=IMAG * NY * rows * (UNITS + width) * 2 + UNITS * width * 2,
            transcendentals=0,
        ),
        name="gate",
    )(features, gate)


def gru_kernel(
    deter_hbm, w_rec_hbm, w_in_hbm, f_hbm, new_ref, prior_hbm, deter_ref, w_rec_ref, w_in_ref, f_ref, mid_ref, prior_ref, sems
):
    rows, bw = deter_ref.shape
    part = bw // NY
    pairs = [(deter_hbm, deter_ref), (w_rec_hbm, w_rec_ref)]
    pairs += [(f_hbm.at[:, k], f_ref.at[:, k]) for k in range(IMAG)]
    pairs += [(w_in_hbm, w_in_ref)]
    pairs += [(prior_ref.at[:, k], prior_hbm.at[:, k]) for k in range(IMAG)]
    copies = [pltpu.make_async_copy(src, dst, sems.at[i]) for i, (src, dst) in enumerate(pairs)]
    for copy in copies[: 3 + IMAG]:
        copy.start()
    copies[0].wait()
    copies[1].wait()
    for k in range(IMAG):
        old_ref = deter_ref if k == 0 else mid_ref
        next_ref = new_ref if k == IMAG - 1 else mid_ref
        old = old_ref[...]
        rec = jnp.dot(old, w_rec_ref[...], preferred_element_type=jnp.float32)
        copies[2 + k].wait()
        for q in range(NY):

            def gate(which):
                mine = f_ref[q, k, :, which * part : (which + 1) * part].astype(jnp.float32)
                return rec[:, which * bw + q * part : which * bw + (q + 1) * part] + mine

            reset = sigmoid(gate(0))
            candidate = jnp.tanh(reset * gate(1))
            update = sigmoid(gate(2) - 1.0)
            before = old[:, q * part : (q + 1) * part].astype(jnp.float32)
            fresh = update * candidate + (1.0 - update) * before
            next_ref[:, q * part : (q + 1) * part] = fresh.astype(jnp.bfloat16)
        if k == 0:
            copies[2 + IMAG].wait()
        prior = jnp.dot(next_ref[...], w_in_ref[...], preferred_element_type=jnp.float32).astype(jnp.bfloat16)
        share = prior_ref.shape[2]
        for j in range(prior_ref.shape[0]):
            prior_ref[j, k] = prior[j * share : (j + 1) * share]
        copies[3 + IMAG + k].start()
    for k in range(IMAG):
        copies[3 + IMAG + k].wait()


def gru_call(deter, w_rec, w_in, sums, tensor_n):
    rows, bw = deter.shape
    hbm = pl.BlockSpec(memory_space=pl.ANY)
    prior = (tensor_n, IMAG, rows // tensor_n, w_in.shape[1])
    return pl.pallas_call(
        gru_kernel,
        in_specs=[hbm] * 4,
        out_specs=[pl.BlockSpec(memory_space=pltpu.VMEM), hbm],
        out_shape=[jax.ShapeDtypeStruct((rows, bw), jnp.bfloat16), jax.ShapeDtypeStruct(prior, jnp.bfloat16)],
        scratch_shapes=[
            pltpu.VMEM(deter.shape, jnp.bfloat16),
            pltpu.VMEM(w_rec.shape, jnp.bfloat16),
            pltpu.VMEM(w_in.shape, jnp.bfloat16),
            pltpu.VMEM(sums.shape, jnp.bfloat16),
            pltpu.VMEM((rows, bw), jnp.bfloat16),
            pltpu.VMEM(prior, jnp.bfloat16),
            pltpu.SemaphoreType.DMA((3 + 2 * IMAG,)),
        ],
        compiler_params=pltpu.CompilerParams(vmem_limit_bytes=60 * MIB),
        cost_estimate=pl.CostEstimate(
            flops=2 * IMAG * rows * bw * (3 * bw + w_in.shape[1]),
            bytes_accessed=2 * (w_rec.size + w_in.size) + 24 * rows * bw,
            transcendentals=6 * rows * bw,
        ),
        name="gru",
    )(deter, w_rec, w_in, sums)


def assemble_kernel(place_ref, mine_ref, other_ref, out_ref):
    x, core = place_ref[0], place_ref[1]
    for i in range(NX):
        base = lax.rem(x + NX - i, NX) * NC
        out_ref[:, pl.ds(pl.multiple_of((base + core) * LANES, LANES), LANES)] = mine_ref[i]
        out_ref[:, pl.ds(pl.multiple_of((base + 1 - core) * LANES, LANES), LANES)] = other_ref[i]


def assemble_call(place, mine, other):
    vmem = pl.BlockSpec(memory_space=pltpu.VMEM)
    return pl.pallas_call(
        assemble_kernel,
        in_specs=[pl.BlockSpec(memory_space=pltpu.SMEM), vmem, vmem],
        out_specs=vmem,
        out_shape=jax.ShapeDtypeStruct((mine.shape[1], NX * NC * LANES), jnp.bfloat16),
        compiler_params=pltpu.CompilerParams(vmem_limit_bytes=16 * MIB),
        cost_estimate=pl.CostEstimate(flops=0, bytes_accessed=8 * mine.size, transcendentals=0),
        name="assemble",
    )(place, mine, other)


def tail_kernel(parts_ref, w_out_ref, picked_ref, var_ref, mask_ref, log_ref):
    pre = parts_ref[0].astype(jnp.float32)
    for i in range(1, parts_ref.shape[0]):
        pre = pre + parts_ref[i].astype(jnp.float32)
    normed = pre * lax.rsqrt(jnp.mean(pre * pre, axis=1, keepdims=True) + EPS)
    hidden = (silu(normed)).astype(jnp.bfloat16)
    rows = hidden.shape[0]
    cls = lax.broadcasted_iota(jnp.int32, (rows, LANES), 1) % CLASSES

    def within(value, combine):
        step = 1
        while step < CLASSES:
            ahead = pltpu.roll(value, step, 1)
            wrapped = pltpu.roll(value, LANES - CLASSES + step, 1)
            value = combine(value, jnp.where(cls >= step, ahead, wrapped))
            step *= 2
        return value

    total = jnp.zeros((rows, LANES), jnp.float32)
    every = jnp.dot(hidden, w_out_ref[...], preferred_element_type=jnp.float32)
    wants = jnp.dot(picked_ref[...], var_ref[...], preferred_element_type=jnp.float32)
    for start in range(0, LAT, LANES):
        logits = every[:, start : start + LANES]
        powers = jnp.exp(logits - within(logits, jnp.maximum))
        probs = 0.99 * (powers / within(powers, jnp.add)) + 0.01 / CLASSES
        want = wants[:, start : start + LANES]
        total = total + jnp.where(cls.astype(jnp.float32) == want, jnp.log(probs), 0.0)
    summed = jnp.where(mask_ref[...] > 0, jnp.sum(total, axis=1, keepdims=True), 0.0)
    lanes = lax.broadcasted_iota(jnp.int32, (rows, LANES), 1)
    diagonal = lax.broadcasted_iota(jnp.int32, (rows, LANES), 0) == lanes
    line = jnp.sum(jnp.where(diagonal, summed, 0.0), axis=0, keepdims=True)
    log_ref[...] = jnp.broadcast_to(line[None], log_ref.shape)


def tail_call(parts, w_out, picked, mask):
    tensor_n, rows = parts.shape[:2]
    lane = jnp.arange(LAT, dtype=jnp.int32)
    var_of = (jnp.arange(STOCH, dtype=jnp.int32)[:, None] == lane[None, :] // CLASSES).astype(jnp.bfloat16)
    vmem = pl.BlockSpec(memory_space=pltpu.VMEM)
    return pl.pallas_call(
        tail_kernel,
        in_specs=[vmem] * 5,
        out_specs=vmem,
        out_shape=jax.ShapeDtypeStruct((tensor_n, 8, LANES), jnp.float32),
        compiler_params=pltpu.CompilerParams(vmem_limit_bytes=32 * MIB),
        cost_estimate=pl.CostEstimate(
            flops=2 * rows * UNITS * LAT, bytes_accessed=2 * w_out.size, transcendentals=4 * rows * LAT
        ),
        name="tail",
    )(parts, w_out, picked, var_of, mask)


def body(
    post_deter,
    post_sample,
    samples,
    actions,
    counts,
    w_stoch,
    w_action,
    w_gate,
    w_rec,
    w_prior_in,
    w_prior_out,
    n_dp,
):
    rows = post_deter.shape[0]
    depth = w_gate.shape[0]
    tensor_n = NX * NC
    share = rows // tensor_n
    me = lax.axis_index("tensor")
    place = jnp.stack([me // NC, me % NC, lax.axis_index("dp") % NY]).astype(jnp.int32)
    n_far = n_dp // NY // NEAR

    sent = split_call(w_gate, n_far).reshape(n_far * NY, depth, -1)
    held = lax.all_to_all(sent, "dp", 0, 0, axis_index_groups=far_groups(n_dp)).reshape(n_far * NY * depth, -1)
    gate = jnp.broadcast_to(held[None], (NEAR,) + held.shape)
    gate = lax.all_to_all(gate, "dp", 0, 0, axis_index_groups=near_groups(n_dp))

    mine = diagonal_gather(prep_call(w_stoch, w_action, post_sample.T, samples.transpose(0, 2, 1), actions), n_dp)
    other = core_swap(mine)
    features = features_call(rows, place, mine, other)
    sums = lax.all_to_all(gate_call(features, gate, n_far), "dp", 0, 0, axis_index_groups=y_groups(n_dp))

    w_out_late, _ = lax.optimization_barrier((w_prior_out, features))
    out_mine = x_gather(w_out_late)
    out_other = core_swap(out_mine)

    positions = jnp.arange(STEPS, dtype=jnp.int32)
    valid_mask = (positions[None, :] < counts[:, None]).reshape(rows)
    my_mask = lax.dynamic_slice_in_dim(valid_mask, me * share, share, 0).astype(jnp.float32)
    my_mask = jnp.concatenate([my_mask] * IMAG)[:, None]
    picked = lax.dynamic_slice_in_dim(samples, me * share, share, 1)
    picked = picked.reshape(IMAG * share, STOCH).astype(jnp.bfloat16)

    deter, partial = gru_call(post_deter, w_rec[0], w_prior_in, sums, tensor_n)
    parts = lax.all_to_all(partial.reshape(tensor_n, IMAG * share, UNITS), "tensor", 0, 0)
    logs = tail_call(parts, assemble_call(place, out_mine, out_other), picked, my_mask)
    logs = lax.all_to_all(logs, "tensor", 0, 0)[:, 0, : IMAG * share]
    log_prob = logs.reshape(tensor_n, IMAG, share).transpose(1, 0, 2).reshape(IMAG, rows)
    deter_out = jnp.where(valid_mask[:, None], deter, jnp.zeros_like(deter))
    return (deter_out, log_prob)


def solution(mesh):
    in_specs = (
        P("dp", "tensor"),
        P("dp", None),
        P(None, "dp", None),
        P(None, "dp"),
        P("dp"),
        P(None, "tensor"),
        P(None, "tensor"),
        P("dp", "tensor"),
        P("tensor", None, None),
        P("tensor", None),
        P(None, "tensor"),
    )
    out_specs = (P("dp", "tensor"), P(None, "dp"))
    whole = functools.partial(body, n_dp=mesh.shape["dp"])
    return jax.shard_map(whole, mesh=mesh, in_specs=in_specs, out_specs=out_specs, check_vma=False)
```

```python
import functools

import jax
import jax.numpy as jnp
from jax import lax
from jax.experimental import pallas as pl
from jax.experimental.pallas import tpu as pltpu
from jax.sharding import PartitionSpec as P

STOCH = 32
CLASSES = 32
LAT = STOCH * CLASSES
ACTIONS = 18
STEPS = 64
IMAG = 2
UNITS = 1024
NY = 4
NX = 4
NC = 2
LANES = 128
CODES = 80
EPS = 1e-06
MIB = 1024 * 1024


def y_groups(n_dp):
    return [[start + y for y in range(NY)] for start in range(0, n_dp, NY)]


def z_groups(n_dp):
    return [list(range(y, n_dp, NY)) for y in range(NY)]


def x_shift(value, step):
    count = NX * NC
    perm = [(i, (i + step * NC) % count) for i in range(count)]
    return lax.ppermute(value, "tensor", perm)


def core_swap(value):
    perm = [(i, i ^ 1) for i in range(NX * NC)]
    return lax.ppermute(value, "tensor", perm)


def tensor_gather(value):
    mine = jnp.stack([value] + [x_shift(value, step) for step in range(1, NX)])
    return mine, core_swap(mine)


def silu(value):
    half = 0.5 * value
    return half + half * jnp.tanh(half)


def sigmoid(value):
    return 0.5 + 0.5 * jnp.tanh(0.5 * value)


def prep_kernel(w_ref, latent_ref, samples_ref, actions_ref, out_ref):
    depth = w_ref.shape[0]
    part = w_ref.shape[1] // 3 // NY
    rows = out_ref.shape[2]
    line = lax.broadcasted_iota(jnp.int32, (CODES - IMAG * STOCH, rows), 0)
    acts = jnp.zeros((CODES - IMAG * STOCH, rows), jnp.float32)
    for k in range(IMAG):
        acts = jnp.where(line == k, actions_ref[k : k + 1].astype(jnp.float32), acts)
    codes = [latent_ref[...].astype(jnp.float32), samples_ref[0].astype(jnp.float32), acts]
    codes = jnp.concatenate(codes, axis=0).astype(jnp.bfloat16)
    for y in range(NY):
        for which in range(3):
            columns = w_ref[:, (which * NY + y) * part : (which * NY + y + 1) * part]
            out_ref[y, which // 2 * depth : (which // 2 + 1) * depth, which % 2 * part : (which % 2 + 1) * part] = columns
        out_ref[y, depth : 2 * depth, part:] = jnp.zeros((depth, rows - part), jnp.bfloat16)
        out_ref[y, 2 * depth :] = codes


def prep_call(w_gate, latent, samples, actions):
    depth = w_gate.shape[0]
    rows = latent.shape[1]
    vmem = pl.BlockSpec(memory_space=pltpu.VMEM)
    return pl.pallas_call(
        prep_kernel,
        in_specs=[vmem] * 4,
        out_specs=vmem,
        out_shape=jax.ShapeDtypeStruct((NY, 2 * depth + CODES, rows), jnp.bfloat16),
        compiler_params=pltpu.CompilerParams(vmem_limit_bytes=60 * MIB),
        cost_estimate=pl.CostEstimate(flops=0, bytes_accessed=NY * rows * 512, transcendentals=0),
        name="prep",
    )(w_gate, latent, samples, actions)


def copies_kernel(came_ref, out_hbm, one_ref, sems):
    depth = one_ref.shape[0] // NY
    part = one_ref.shape[1] // 3
    for y in range(NY):
        here = slice(y * depth, (y + 1) * depth)
        one_ref[here, : 2 * part] = came_ref[y, :depth, : 2 * part]
        one_ref[here, 2 * part :] = came_ref[y, depth : 2 * depth, :part]
    copies = [pltpu.make_async_copy(one_ref, out_hbm.at[z], sems.at[z]) for z in range(out_hbm.shape[0])]
    for copy in copies:
        copy.start()
    for copy in copies:
        copy.wait()


def copies_call(came, n_z, depth, width):
    return pl.pallas_call(
        copies_kernel,
        in_specs=[pl.BlockSpec(memory_space=pltpu.VMEM)],
        out_specs=pl.BlockSpec(memory_space=pltpu.HBM),
        out_shape=pltpu.HBM((n_z, NY * depth, width), jnp.bfloat16),
        scratch_shapes=[pltpu.VMEM((NY * depth, width), jnp.bfloat16), pltpu.SemaphoreType.DMA((n_z,))],
        compiler_params=pltpu.CompilerParams(vmem_limit_bytes=16 * MIB),
        cost_estimate=pl.CostEstimate(flops=0, bytes_accessed=4 * n_z * depth * width, transcendentals=0),
        name="copies",
    )(came)


def features_kernel(place_ref, came_ref, spread_ref, target_ref, mine_ref, other_ref, out_ref, w_ref):
    x, core = place_ref[0], place_ref[1]
    width = w_ref.shape[0]
    rows = out_ref.shape[1]

    @pl.when(pl.program_id(0) == 0)
    def _():
        for i in range(NX):
            base = lax.rem(x + NX - i, NX) * NC
            w_ref[:, pl.ds(pl.multiple_of((base + core) * LANES, LANES), LANES)] = mine_ref[i]
            w_ref[:, pl.ds(pl.multiple_of((base + 1 - core) * LANES, LANES), LANES)] = other_ref[i]

    codes = came_ref[came_ref.shape[0] - CODES :]
    spread = lax.dot_general(codes, spread_ref[...], (((0,), (0,)), ((), ())), preferred_element_type=jnp.float32)
    spread = jnp.concatenate([spread[:, :width], spread[:, width:]], axis=0)
    hot = jnp.where(spread == target_ref[...], 1.0, 0.0).astype(jnp.bfloat16)
    pre = jnp.dot(hot, w_ref[...], preferred_element_type=jnp.float32)
    scale = lax.rsqrt(jnp.mean(pre * pre, axis=1, keepdims=True) + EPS)
    features = silu(pre * scale).astype(jnp.bfloat16)
    for k in range(IMAG):
        out_ref[k] = features[k * rows : (k + 1) * rows]


def features_call(place, came, mine, other):
    rows = came.shape[2]
    width = mine.shape[1]
    lane = jnp.arange(width, dtype=jnp.int32)
    is_lat = lane < LAT
    target = jnp.where(is_lat, lane % CLASSES, lane - LAT).astype(jnp.float32)[None, :]
    source = [jnp.where(is_lat, k * STOCH + lane // CLASSES, IMAG * STOCH + k) for k in range(IMAG)]
    source = jnp.concatenate(source)
    spread = (jnp.arange(CODES, dtype=jnp.int32)[:, None] == source[None, :]).astype(jnp.bfloat16)
    return pl.pallas_call(
        features_kernel,
        grid=(NY,),
        in_specs=[
            pl.BlockSpec(memory_space=pltpu.SMEM),
            pl.BlockSpec((None,) + came.shape[1:], lambda b: (b, 0, 0)),
            pl.BlockSpec(spread.shape, lambda b: (0, 0)),
            pl.BlockSpec((1, width), lambda b: (0, 0)),
            pl.BlockSpec((NX, width, LANES), lambda b: (0, 0, 0)),
            pl.BlockSpec((NX, width, LANES), lambda b: (0, 0, 0)),
        ],
        out_specs=pl.BlockSpec((None, IMAG, rows, UNITS), lambda b: (b, 0, 0, 0)),
        out_shape=pltpu.HBM((NY, IMAG, rows, UNITS), jnp.bfloat16),
        scratch_shapes=[pltpu.VMEM((width, UNITS), jnp.bfloat16)],
        compiler_params=pltpu.CompilerParams(vmem_limit_bytes=32 * MIB),
        cost_estimate=pl.CostEstimate(
            flops=2 * IMAG * NY * rows * width * (UNITS + LANES),
            bytes_accessed=IMAG * NY * rows * UNITS * 2 + width * UNITS * 2,
            transcendentals=IMAG * NY * rows * UNITS,
        ),
        name="features",
    )(place, came, spread, target, mine, other)


def gru_kernel(
    deter_hbm, w_rec_hbm, w_in_hbm, f_ref, new_ref, prior_hbm, deter_ref, w_rec_ref, w_in_ref, mid_ref, prior_ref, sems
):
    rows, bw = deter_ref.shape
    part = bw // NY
    pairs = [(deter_hbm, deter_ref), (w_rec_hbm, w_rec_ref), (w_in_hbm, w_in_ref)]
    pairs += [(prior_ref.at[:, k], prior_hbm.at[:, k]) for k in range(IMAG)]
    copies = [pltpu.make_async_copy(src, dst, sems.at[i]) for i, (src, dst) in enumerate(pairs)]
    for copy in copies[:3]:
        copy.start()
    copies[0].wait()
    copies[1].wait()
    for k in range(IMAG):
        old_ref = deter_ref if k == 0 else mid_ref
        next_ref = new_ref if k == IMAG - 1 else mid_ref
        old = old_ref[...]
        rec = jnp.dot(old, w_rec_ref[...], preferred_element_type=jnp.float32)
        for q in range(NY):

            def gate(which):
                mine = f_ref[q, k, :, which * part : (which + 1) * part].astype(jnp.float32)
                return rec[:, which * bw + q * part : which * bw + (q + 1) * part] + mine

            reset = sigmoid(gate(0))
            candidate = jnp.tanh(reset * gate(1))
            update = sigmoid(gate(2) - 1.0)
            before = old[:, q * part : (q + 1) * part].astype(jnp.float32)
            fresh = update * candidate + (1.0 - update) * before
            next_ref[:, q * part : (q + 1) * part] = fresh.astype(jnp.bfloat16)
        if k == 0:
            copies[2].wait()
        prior = jnp.dot(next_ref[...], w_in_ref[...], preferred_element_type=jnp.float32).astype(jnp.bfloat16)
        share = prior_ref.shape[2]
        for j in range(prior_ref.shape[0]):
            prior_ref[j, k] = prior[j * share : (j + 1) * share]
        copies[3 + k].start()
    for k in range(IMAG):
        copies[3 + k].wait()


def gru_call(deter, w_rec, w_in, sums, tensor_n):
    rows, bw = deter.shape
    hbm, vmem = pl.BlockSpec(memory_space=pltpu.HBM), pl.BlockSpec(memory_space=pltpu.VMEM)
    prior = (tensor_n, IMAG, rows // tensor_n, w_in.shape[1])
    return pl.pallas_call(
        gru_kernel,
        in_specs=[hbm] * 3 + [vmem],
        out_specs=[vmem, hbm],
        out_shape=[jax.ShapeDtypeStruct((rows, bw), jnp.bfloat16), pltpu.HBM(prior, jnp.bfloat16)],
        scratch_shapes=[
            pltpu.VMEM(deter.shape, jnp.bfloat16),
            pltpu.VMEM(w_rec.shape, jnp.bfloat16),
            pltpu.VMEM(w_in.shape, jnp.bfloat16),
            pltpu.VMEM((rows, bw), jnp.bfloat16),
            pltpu.VMEM(prior, jnp.bfloat16),
            pltpu.SemaphoreType.DMA((3 + IMAG,)),
        ],
        compiler_params=pltpu.CompilerParams(vmem_limit_bytes=24 * MIB),
        cost_estimate=pl.CostEstimate(
            flops=2 * IMAG * rows * bw * (3 * bw + w_in.shape[1]),
            bytes_accessed=2 * (w_rec.size + w_in.size) + 24 * rows * bw,
            transcendentals=6 * rows * bw,
        ),
        name="gru",
    )(*[pltpu.with_memory_space_constraint(value, pltpu.HBM) for value in (deter, w_rec, w_in)], sums)


def tail_kernel(me_ref, parts_ref, mine_ref, other_ref, picked_ref, var_ref, mask_ref, log_ref):
    pre = parts_ref[0].astype(jnp.float32)
    for i in range(1, parts_ref.shape[0]):
        pre = pre + parts_ref[i].astype(jnp.float32)
    normed = pre * lax.rsqrt(jnp.mean(pre * pre, axis=1, keepdims=True) + EPS)
    hidden = (silu(normed)).astype(jnp.bfloat16)
    rows = hidden.shape[0]
    cls = lax.broadcasted_iota(jnp.int32, (NX * NC * rows, LANES), 1) % CLASSES

    def within(value, combine):
        step = 1
        while step < CLASSES:
            ahead = pltpu.roll(value, step, 1)
            wrapped = pltpu.roll(value, LANES - CLASSES + step, 1)
            value = combine(value, jnp.where(cls >= step, ahead, wrapped))
            step *= 2
        return value

    x, core = me_ref[0], me_ref[1]
    logits, wants = [], []
    for i in range(NX * NC):
        w_ref = mine_ref if i % NC == 0 else other_ref
        piece = lax.rem(x + NX - i // NC, NX) * NC + (core if i % NC == 0 else 1 - core)
        here = pl.ds(pl.multiple_of(piece * LANES, LANES), LANES)
        logits.append(jnp.dot(hidden, w_ref[i // NC], preferred_element_type=jnp.float32))
        wants.append(jnp.dot(picked_ref[...], var_ref[:, here], preferred_element_type=jnp.float32))
    logits, wants = jnp.concatenate(logits, axis=0), jnp.concatenate(wants, axis=0)
    powers = jnp.exp(logits - within(logits, jnp.maximum))
    probs = 0.99 * (powers / within(powers, jnp.add)) + 0.01 / CLASSES
    terms = jnp.where(cls.astype(jnp.float32) == wants, jnp.log(probs), 0.0)
    total = terms[:rows]
    for i in range(1, NX * NC):
        total = total + terms[i * rows : (i + 1) * rows]
    summed = jnp.where(mask_ref[...] > 0, jnp.sum(total, axis=1, keepdims=True), 0.0)
    lanes = lax.broadcasted_iota(jnp.int32, (rows, LANES), 1)
    diagonal = lax.broadcasted_iota(jnp.int32, (rows, LANES), 0) == lanes
    line = jnp.sum(jnp.where(diagonal, summed, 0.0), axis=0, keepdims=True)
    log_ref[...] = jnp.broadcast_to(line[None], log_ref.shape)


def tail_call(place, parts, mine, other, picked, mask):
    tensor_n, rows = parts.shape[:2]
    lane = jnp.arange(LAT, dtype=jnp.int32)
    var_of = (jnp.arange(STOCH, dtype=jnp.int32)[:, None] == lane[None, :] // CLASSES).astype(jnp.bfloat16)
    vmem = pl.BlockSpec(memory_space=pltpu.VMEM)
    return pl.pallas_call(
        tail_kernel,
        in_specs=[pl.BlockSpec(memory_space=pltpu.SMEM)] + [vmem] * 6,
        out_specs=vmem,
        out_shape=jax.ShapeDtypeStruct((tensor_n, 8, LANES), jnp.float32),
        compiler_params=pltpu.CompilerParams(vmem_limit_bytes=32 * MIB),
        cost_estimate=pl.CostEstimate(
            flops=2 * rows * UNITS * LAT, bytes_accessed=8 * mine.size, transcendentals=4 * rows * LAT
        ),
        name="tail",
    )(place, parts, mine, other, picked, var_of, mask)


def body(
    post_deter,
    post_sample,
    samples,
    actions,
    counts,
    w_stoch,
    w_action,
    w_gate,
    w_rec,
    w_prior_in,
    w_prior_out,
    n_dp,
):
    rows = post_deter.shape[0]
    depth = w_gate.shape[0]
    tensor_n = NX * NC
    share = rows // tensor_n
    me = lax.axis_index("tensor")
    place = jnp.stack([me // NC, me % NC]).astype(jnp.int32)

    sent = prep_call(w_gate, post_sample.T, samples.transpose(0, 2, 1), actions)
    came = lax.all_to_all(sent, "dp", 0, 0, axis_index_groups=y_groups(n_dp))
    held = copies_call(came, n_dp // NY, depth, w_gate.shape[1] // NY)
    gate = lax.all_to_all(held, "dp", 0, 0, axis_index_groups=z_groups(n_dp)).reshape(n_dp * depth, -1)

    action_rows = jnp.pad(w_action, ((0, LANES - ACTIONS), (0, 0)))
    mine, other = tensor_gather(jnp.concatenate([w_stoch, action_rows], axis=0))

    features = features_call(place, came, mine, other)
    total = jnp.dot(features.reshape(-1, UNITS), gate, preferred_element_type=jnp.float32).astype(jnp.bfloat16)
    total = total.reshape(NY, IMAG, rows, -1)
    sums = lax.all_to_all(total, "dp", 0, 0, axis_index_groups=y_groups(n_dp))

    w_out_late, _ = lax.optimization_barrier((w_prior_out, features))
    out_mine, out_other = tensor_gather(w_out_late)

    positions = jnp.arange(STEPS, dtype=jnp.int32)
    valid_mask = (positions[None, :] < counts[:, None]).reshape(rows)
    my_mask = lax.dynamic_slice_in_dim(valid_mask, me * share, share, 0).astype(jnp.float32)
    my_mask = jnp.concatenate([my_mask] * IMAG)[:, None]
    picked = lax.dynamic_slice_in_dim(samples, me * share, share, 1)
    picked = picked.reshape(IMAG * share, STOCH).astype(jnp.bfloat16)

    deter, partial = gru_call(post_deter, w_rec[0], w_prior_in, sums, tensor_n)
    parts = lax.all_to_all(partial.reshape(tensor_n, IMAG * share, UNITS), "tensor", 0, 0)
    logs = tail_call(place, parts, out_mine, out_other, picked, my_mask)
    logs = lax.all_to_all(logs, "tensor", 0, 0)[:, 0, : IMAG * share]
    log_prob = logs.reshape(tensor_n, IMAG, share).transpose(1, 0, 2).reshape(IMAG, rows)
    deter_out = jnp.where(valid_mask[:, None], deter, jnp.zeros_like(deter))
    return (deter_out, log_prob)


def solution(mesh):
    in_specs = (
        P("dp", "tensor"),
        P("dp", None),
        P(None, "dp", None),
        P(None, "dp"),
        P("dp"),
        P(None, "tensor"),
        P(None, "tensor"),
        P("dp", "tensor"),
        P("tensor", None, None),
        P("tensor", None),
        P(None, "tensor"),
    )
    out_specs = (P("dp", "tensor"), P(None, "dp"))
    whole = functools.partial(body, n_dp=mesh.shape["dp"])
    return jax.shard_map(whole, mesh=mesh, in_specs=in_specs, out_specs=out_specs, check_vma=False)
```

```python
import functools

import jax
import jax.numpy as jnp
from jax import lax
from jax.experimental import pallas as pl
from jax.experimental.pallas import tpu as pltpu
from jax.sharding import PartitionSpec as P

STOCH = 32
CLASSES = 32
LAT = STOCH * CLASSES
ACTIONS = 18
STEPS = 64
IMAG = 2
UNITS = 1024
NY = 4
NX = 4
NC = 2
LANES = 128
EMBED = LAT + LANES
NEAR = 4
CODES = 80
EPS = 1e-06
MIB = 1024 * 1024
FEATURES_WEIGHT = 12


def y_groups(n_dp):
    return [[start + y for y in range(NY)] for start in range(0, n_dp, NY)]


def far_groups(n_dp):
    n_far = n_dp // NY // NEAR
    return [[(far * NEAR + near) * NY + y for far in range(n_far) for y in range(NY)] for near in range(NEAR)]


def near_groups(n_dp):
    n_far = n_dp // NY // NEAR
    return [[(far * NEAR + near) * NY + y for near in range(NEAR)] for far in range(n_far) for y in range(NY)]


def step_perm(n_dp, along_y, steps):
    def index(z, y, x, core):
        return ((z * NY + y) * NX + x) * NC + core

    return [
        (index(z, y, x, core), index(z, (y + along_y * steps[core]) % NY, (x + steps[core]) % NX, core))
        for z in range(n_dp // NY)
        for y in range(NY)
        for x in range(NX)
        for core in range(NC)
    ]


def ring_gather(value, n_dp, along_y):
    axes = ("dp", "tensor")
    behind = lax.ppermute(value, axes, step_perm(n_dp, along_y, (1, 1)))
    ahead = lax.ppermute(value, axes, step_perm(n_dp, along_y, (-1, -1)))
    passed = jnp.where(lax.axis_index("tensor") % NC == 0, behind, ahead)
    across = lax.ppermute(passed, axes, step_perm(n_dp, along_y, (1, -1)))
    return jnp.stack([value, behind, across, ahead])


def core_swap(value):
    perm = [(i, i ^ 1) for i in range(NX * NC)]
    return lax.ppermute(value, "tensor", perm)


def silu(value):
    half = 0.5 * value
    return half + half * jnp.tanh(half)


def sigmoid(value):
    return 0.5 + 0.5 * jnp.tanh(0.5 * value)


def split_kernel(w_ref, out_ref):
    part = w_ref.shape[1] // 3 // NY
    for y in range(NY):
        for which in range(3):
            columns = w_ref[:, (which * NY + y) * part : (which * NY + y + 1) * part]
            for z in range(out_ref.shape[0]):
                out_ref[z, y, :, which * part : (which + 1) * part] = columns


def split_call(w_gate, n_z):
    depth, width = w_gate.shape
    vmem = pl.BlockSpec(memory_space=pltpu.VMEM)
    return pl.pallas_call(
        split_kernel,
        in_specs=[vmem],
        out_specs=vmem,
        out_shape=jax.ShapeDtypeStruct((n_z, NY, depth, width // NY), w_gate.dtype),
        compiler_params=pltpu.CompilerParams(vmem_limit_bytes=60 * MIB),
        cost_estimate=pl.CostEstimate(flops=0, bytes_accessed=2 * n_z * depth * width, transcendentals=0),
        name="split",
    )(w_gate)


def prep_kernel(w_stoch_ref, w_action_ref, latent_ref, samples_ref, actions_ref, out_ref):
    rows = latent_ref.shape[1]
    out_ref[:LAT] = w_stoch_ref[...]
    out_ref[LAT:EMBED] = jnp.zeros((EMBED - LAT, LANES), jnp.bfloat16)
    out_ref[LAT : LAT + ACTIONS] = w_action_ref[...]
    line = lax.broadcasted_iota(jnp.int32, (CODES - IMAG * STOCH, rows), 0)
    acts = jnp.zeros((CODES - IMAG * STOCH, rows), jnp.float32)
    for k in range(IMAG):
        acts = jnp.where(line == k, actions_ref[k : k + 1].astype(jnp.float32), acts)
    codes = [latent_ref[...].astype(jnp.float32), samples_ref[0].astype(jnp.float32), acts]
    codes = jnp.concatenate(codes, axis=0).astype(jnp.bfloat16)
    for i in range(rows // LANES):
        out_ref[EMBED + i * CODES : EMBED + (i + 1) * CODES] = codes[:, i * LANES : (i + 1) * LANES]


def prep_call(w_stoch, w_action, latent, samples, actions):
    rows = latent.shape[1]
    vmem = pl.BlockSpec(memory_space=pltpu.VMEM)
    return pl.pallas_call(
        prep_kernel,
        in_specs=[vmem] * 5,
        out_specs=vmem,
        out_shape=jax.ShapeDtypeStruct((EMBED + rows // LANES * CODES, LANES), jnp.bfloat16),
        compiler_params=pltpu.CompilerParams(vmem_limit_bytes=60 * MIB),
        cost_estimate=pl.CostEstimate(flops=0, bytes_accessed=2 * EMBED * LANES * 2, transcendentals=0),
        name="prep",
    )(w_stoch, w_action, latent, samples, actions)


def features_kernel(place_ref, spread_ref, target_ref, mine_ref, other_ref, out_ref, w_ref):
    x, core, y = place_ref[0], place_ref[1], place_ref[2]
    rows = out_ref.shape[1]

    @pl.when(pl.program_id(0) == 0)
    def _():
        for i in range(NX):
            base = lax.rem(x + NX - i, NX) * NC
            w_ref[:, pl.ds(pl.multiple_of((base + core) * LANES, LANES), LANES)] = mine_ref[i, :EMBED]
            w_ref[:, pl.ds(pl.multiple_of((base + 1 - core) * LANES, LANES), LANES)] = other_ref[i, :EMBED]

    source = lax.rem(y + NY - pl.program_id(0), NY)
    spread = []
    for k in range(IMAG):
        for half in range(rows // LANES):
            codes = mine_ref[source, EMBED + half * CODES : EMBED + (half + 1) * CODES]
            wide = spread_ref[:, k * EMBED : (k + 1) * EMBED]
            spread.append(
                lax.dot_general(codes, wide, (((0,), (0,)), ((), ())), preferred_element_type=jnp.float32)
            )
    spread = jnp.concatenate(spread, axis=0)
    hot = jnp.where(spread == target_ref[...], 1.0, 0.0).astype(jnp.bfloat16)
    pre = jnp.dot(hot, w_ref[...], preferred_element_type=jnp.float32)
    scale = lax.rsqrt(jnp.mean(pre * pre, axis=1, keepdims=True) + EPS)
    features = silu(pre * scale).astype(jnp.bfloat16)
    for k in range(IMAG):
        out_ref[k] = features[k * rows : (k + 1) * rows]


def features_call(rows, place, mine, other):
    lane = jnp.arange(EMBED, dtype=jnp.int32)
    is_lat = lane < LAT
    target = jnp.where(is_lat, lane % CLASSES, lane - LAT).astype(jnp.float32)[None, :]
    source = [jnp.where(is_lat, k * STOCH + lane // CLASSES, IMAG * STOCH + k) for k in range(IMAG)]
    source = jnp.concatenate(source)
    spread = (jnp.arange(CODES, dtype=jnp.int32)[:, None] == source[None, :]).astype(jnp.bfloat16)
    return pl.pallas_call(
        features_kernel,
        grid=(NY,),
        in_specs=[
            pl.BlockSpec(memory_space=pltpu.SMEM),
            pl.BlockSpec(spread.shape, lambda b: (0, 0)),
            pl.BlockSpec((1, EMBED), lambda b: (0, 0)),
            pl.BlockSpec(mine.shape, lambda b: (0, 0, 0)),
            pl.BlockSpec(other.shape, lambda b: (0, 0, 0)),
        ],
        out_specs=pl.BlockSpec((IMAG, None, rows, UNITS), lambda b: (0, b, 0, 0)),
        out_shape=pltpu.HBM((IMAG, NY, rows, UNITS), jnp.bfloat16),
        scratch_shapes=[pltpu.VMEM((EMBED, UNITS), jnp.bfloat16)],
        compiler_params=pltpu.CompilerParams(vmem_limit_bytes=32 * MIB),
        cost_estimate=pl.CostEstimate(
            flops=FEATURES_WEIGHT * IMAG * NY * rows * EMBED * (UNITS + LANES) // 5,
            bytes_accessed=IMAG * NY * rows * UNITS * 2 + EMBED * UNITS * 2,
            transcendentals=IMAG * NY * rows * UNITS,
        ),
        name="features",
    )(place, spread, target, mine, other)


def gate_kernel(n_far, features_ref, gate_ref, out_ref, w_ref):
    near, held = gate_ref.shape[:2]
    depth = held // n_far

    @pl.when(pl.program_id(0) == 0)
    def _():
        for i in range(near):
            for far in range(n_far):
                w_ref[(far * near + i) * depth : (far * near + i + 1) * depth] = gate_ref[i, far * depth : (far + 1) * depth]

    for k in range(IMAG):
        out_ref[k] = jnp.dot(features_ref[k], w_ref[...], preferred_element_type=jnp.float32).astype(jnp.bfloat16)


def gate_call(features, gate, n_far):
    rows = features.shape[2]
    width = gate.shape[2]
    return pl.pallas_call(
        functools.partial(gate_kernel, n_far),
        grid=(NY,),
        in_specs=[
            pl.BlockSpec((IMAG, None, rows, UNITS), lambda b: (0, b, 0, 0)),
            pl.BlockSpec(gate.shape, lambda b: (0, 0, 0)),
        ],
        out_specs=pl.BlockSpec((None, IMAG, rows, width), lambda b: (b, 0, 0, 0)),
        out_shape=jax.ShapeDtypeStruct((NY, IMAG, rows, width), jnp.bfloat16),
        scratch_shapes=[pltpu.VMEM((UNITS, width), jnp.bfloat16)],
        compiler_params=pltpu.CompilerParams(vmem_limit_bytes=32 * MIB),
        cost_estimate=pl.CostEstimate(
            flops=2 * IMAG * NY * rows * UNITS * width,
            bytes_accessed=IMAG * NY * rows * (UNITS + width) * 2 + UNITS * width * 2,
            transcendentals=0,
        ),
        name="gate",
    )(features, gate)


def gru_kernel(
    deter_hbm, w_rec_hbm, w_in_hbm, f_ref, new_ref, prior_hbm, deter_ref, w_rec_ref, w_in_ref, mid_ref, prior_ref, sems
):
    rows, bw = deter_ref.shape
    part = bw // NY
    pairs = [(deter_hbm, deter_ref), (w_rec_hbm, w_rec_ref), (w_in_hbm, w_in_ref)]
    pairs += [(prior_ref.at[:, k], prior_hbm.at[:, k]) for k in range(IMAG)]
    copies = [pltpu.make_async_copy(src, dst, sems.at[i]) for i, (src, dst) in enumerate(pairs)]
    for copy in copies[:3]:
        copy.start()
    copies[0].wait()
    copies[1].wait()
    for k in range(IMAG):
        old_ref = deter_ref if k == 0 else mid_ref
        next_ref = new_ref if k == IMAG - 1 else mid_ref
        old = old_ref[...]
        rec = jnp.dot(old, w_rec_ref[...], preferred_element_type=jnp.float32)
        for q in range(NY):

            def gate(which):
                mine = f_ref[q, k, :, which * part : (which + 1) * part].astype(jnp.float32)
                return rec[:, which * bw + q * part : which * bw + (q + 1) * part] + mine

            reset = sigmoid(gate(0))
            candidate = jnp.tanh(reset * gate(1))
            update = sigmoid(gate(2) - 1.0)
            before = old[:, q * part : (q + 1) * part].astype(jnp.float32)
            fresh = update * candidate + (1.0 - update) * before
            next_ref[:, q * part : (q + 1) * part] = fresh.astype(jnp.bfloat16)
        if k == 0:
            copies[2].wait()
        prior = jnp.dot(next_ref[...], w_in_ref[...], preferred_element_type=jnp.float32).astype(jnp.bfloat16)
        share = prior_ref.shape[2]
        for j in range(prior_ref.shape[0]):
            prior_ref[j, k] = prior[j * share : (j + 1) * share]
        copies[3 + k].start()
    for k in range(IMAG):
        copies[3 + k].wait()


def gru_call(deter, w_rec, w_in, sums, tensor_n):
    rows, bw = deter.shape
    hbm, vmem = pl.BlockSpec(memory_space=pltpu.HBM), pl.BlockSpec(memory_space=pltpu.VMEM)
    prior = (tensor_n, IMAG, rows // tensor_n, w_in.shape[1])
    return pl.pallas_call(
        gru_kernel,
        in_specs=[hbm] * 3 + [vmem],
        out_specs=[vmem, hbm],
        out_shape=[jax.ShapeDtypeStruct((rows, bw), jnp.bfloat16), pltpu.HBM(prior, jnp.bfloat16)],
        scratch_shapes=[
            pltpu.VMEM(deter.shape, jnp.bfloat16),
            pltpu.VMEM(w_rec.shape, jnp.bfloat16),
            pltpu.VMEM(w_in.shape, jnp.bfloat16),
            pltpu.VMEM((rows, bw), jnp.bfloat16),
            pltpu.VMEM(prior, jnp.bfloat16),
            pltpu.SemaphoreType.DMA((3 + IMAG,)),
        ],
        compiler_params=pltpu.CompilerParams(vmem_limit_bytes=24 * MIB),
        cost_estimate=pl.CostEstimate(
            flops=2 * IMAG * rows * bw * (3 * bw + w_in.shape[1]),
            bytes_accessed=2 * (w_rec.size + w_in.size) + 24 * rows * bw,
            transcendentals=6 * rows * bw,
        ),
        name="gru",
    )(*[pltpu.with_memory_space_constraint(value, pltpu.HBM) for value in (deter, w_rec, w_in)], sums)


def tail_kernel(me_ref, parts_ref, mine_hbm, other_hbm, picked_ref, var_ref, mask_ref, log_ref, w_ref, sems):
    copies = []
    for i in range(NX * NC):
        source = mine_hbm if i % NC == 0 else other_hbm
        copies.append(pltpu.make_async_copy(source.at[i // NC], w_ref.at[i], sems.at[i]))
        copies[i].start()
    pre = parts_ref[0].astype(jnp.float32)
    for i in range(1, parts_ref.shape[0]):
        pre = pre + parts_ref[i].astype(jnp.float32)
    normed = pre * lax.rsqrt(jnp.mean(pre * pre, axis=1, keepdims=True) + EPS)
    hidden = (silu(normed)).astype(jnp.bfloat16)
    rows = hidden.shape[0]
    cls = lax.broadcasted_iota(jnp.int32, (NX * NC * rows, LANES), 1) % CLASSES

    def within(value, combine):
        step = 1
        while step < CLASSES:
            ahead = pltpu.roll(value, step, 1)
            wrapped = pltpu.roll(value, LANES - CLASSES + step, 1)
            value = combine(value, jnp.where(cls >= step, ahead, wrapped))
            step *= 2
        return value

    x, core = me_ref[0], me_ref[1]
    logits, wants = [], []
    for i in range(NX * NC):
        piece = lax.rem(x + NX - i // NC, NX) * NC + (core if i % NC == 0 else 1 - core)
        here = pl.ds(pl.multiple_of(piece * LANES, LANES), LANES)
        copies[i].wait()
        logits.append(jnp.dot(hidden, w_ref[i], preferred_element_type=jnp.float32))
        wants.append(jnp.dot(picked_ref[...], var_ref[:, here], preferred_element_type=jnp.float32))
    logits, wants = jnp.concatenate(logits, axis=0), jnp.concatenate(wants, axis=0)
    powers = jnp.exp(logits - within(logits, jnp.maximum))
    probs = 0.99 * (powers / within(powers, jnp.add)) + 0.01 / CLASSES
    terms = jnp.where(cls.astype(jnp.float32) == wants, jnp.log(probs), 0.0)
    total = terms[:rows]
    for i in range(1, NX * NC):
        total = total + terms[i * rows : (i + 1) * rows]
    summed = jnp.where(mask_ref[...] > 0, jnp.sum(total, axis=1, keepdims=True), 0.0)
    lanes = lax.broadcasted_iota(jnp.int32, (rows, LANES), 1)
    diagonal = lax.broadcasted_iota(jnp.int32, (rows, LANES), 0) == lanes
    line = jnp.sum(jnp.where(diagonal, summed, 0.0), axis=0, keepdims=True)
    log_ref[...] = jnp.broadcast_to(line[None], log_ref.shape)


def tail_call(place, parts, mine, other, picked, mask):
    tensor_n, rows = parts.shape[:2]
    lane = jnp.arange(LAT, dtype=jnp.int32)
    var_of = (jnp.arange(STOCH, dtype=jnp.int32)[:, None] == lane[None, :] // CLASSES).astype(jnp.bfloat16)
    vmem, hbm = pl.BlockSpec(memory_space=pltpu.VMEM), pl.BlockSpec(memory_space=pltpu.HBM)
    mine, other = [pltpu.with_memory_space_constraint(value, pltpu.HBM) for value in (mine, other)]
    return pl.pallas_call(
        tail_kernel,
        in_specs=[pl.BlockSpec(memory_space=pltpu.SMEM), vmem, hbm, hbm, vmem, vmem, vmem],
        out_specs=vmem,
        out_shape=jax.ShapeDtypeStruct((tensor_n, 8, LANES), jnp.float32),
        scratch_shapes=[pltpu.VMEM((NX * NC,) + mine.shape[1:], jnp.bfloat16), pltpu.SemaphoreType.DMA((NX * NC,))],
        compiler_params=pltpu.CompilerParams(vmem_limit_bytes=32 * MIB),
        cost_estimate=pl.CostEstimate(
            flops=2 * rows * UNITS * LAT, bytes_accessed=8 * mine.size, transcendentals=4 * rows * LAT
        ),
        name="tail",
    )(place, parts, mine, other, picked, var_of, mask)


def body(
    post_deter,
    post_sample,
    samples,
    actions,
    counts,
    w_stoch,
    w_action,
    w_gate,
    w_rec,
    w_prior_in,
    w_prior_out,
    n_dp,
):
    rows = post_deter.shape[0]
    depth = w_gate.shape[0]
    tensor_n = NX * NC
    share = rows // tensor_n
    me = lax.axis_index("tensor")
    place = jnp.stack([me // NC, me % NC, lax.axis_index("dp") % NY]).astype(jnp.int32)
    n_far = n_dp // NY // NEAR

    sent = split_call(w_gate, n_far).reshape(n_far * NY, depth, -1)
    held = lax.all_to_all(sent, "dp", 0, 0, axis_index_groups=far_groups(n_dp)).reshape(n_far * NY * depth, -1)
    gate = jnp.broadcast_to(held[None], (NEAR,) + held.shape)
    gate = lax.all_to_all(gate, "dp", 0, 0, axis_index_groups=near_groups(n_dp))

    mine = ring_gather(prep_call(w_stoch, w_action, post_sample.T, samples.transpose(0, 2, 1), actions), n_dp, 1)
    other = core_swap(mine)
    features = features_call(rows, place, mine, other)
    sums = lax.all_to_all(gate_call(features, gate, n_far), "dp", 0, 0, axis_index_groups=y_groups(n_dp))

    w_out_late, _ = lax.optimization_barrier((w_prior_out, features))
    out_mine = ring_gather(w_out_late, n_dp, 0)
    out_other = core_swap(out_mine)

    positions = jnp.arange(STEPS, dtype=jnp.int32)
    valid_mask = (positions[None, :] < counts[:, None]).reshape(rows)
    my_mask = lax.dynamic_slice_in_dim(valid_mask, me * share, share, 0).astype(jnp.float32)
    my_mask = jnp.concatenate([my_mask] * IMAG)[:, None]
    picked = lax.dynamic_slice_in_dim(samples, me * share, share, 1)
    picked = picked.reshape(IMAG * share, STOCH).astype(jnp.bfloat16)

    deter, partial = gru_call(post_deter, w_rec[0], w_prior_in, sums, tensor_n)
    parts = lax.all_to_all(partial.reshape(tensor_n, IMAG * share, UNITS), "tensor", 0, 0)
    logs = tail_call(place, parts, out_mine, out_other, picked, my_mask)
    logs = lax.all_to_all(logs, "tensor", 0, 0)[:, 0, : IMAG * share]
    log_prob = logs.reshape(tensor_n, IMAG, share).transpose(1, 0, 2).reshape(IMAG, rows)
    deter_out = jnp.where(valid_mask[:, None], deter, jnp.zeros_like(deter))
    return (deter_out, log_prob)


def solution(mesh):
    in_specs = (
        P("dp", "tensor"),
        P("dp", None),
        P(None, "dp", None),
        P(None, "dp"),
        P("dp"),
        P(None, "tensor"),
        P(None, "tensor"),
        P("dp", "tensor"),
        P("tensor", None, None),
        P("tensor", None),
        P(None, "tensor"),
    )
    out_specs = (P("dp", "tensor"), P(None, "dp"))
    whole = functools.partial(body, n_dp=mesh.shape["dp"])
    return jax.shard_map(whole, mesh=mesh, in_specs=in_specs, out_specs=out_specs, check_vma=False)
```

```python
import functools

import jax
import jax.numpy as jnp
from jax import lax
from jax.experimental import pallas as pl
from jax.experimental.pallas import tpu as pltpu
from jax.sharding import PartitionSpec as P

STOCH = 32
CLASSES = 32
LAT = STOCH * CLASSES
ACTIONS = 18
STEPS = 64
IMAG = 2
UNITS = 1024
NY = 4
NX = 4
NC = 2
LANES = 128
NEAR = 4
CODES = 80
EPS = 1e-06
MIB = 1024 * 1024
FEATURES_WEIGHT = 12


def y_groups(n_dp):
    return [[start + y for y in range(NY)] for start in range(0, n_dp, NY)]


def far_groups(n_dp):
    n_far = n_dp // NY // NEAR
    return [[(far * NEAR + near) * NY + y for far in range(n_far)] for near in range(NEAR) for y in range(NY)]


def near_groups(n_dp):
    n_far = n_dp // NY // NEAR
    return [[(far * NEAR + near) * NY + y for near in range(NEAR)] for far in range(n_far) for y in range(NY)]


def x_shift(value, step):
    count = NX * NC
    perm = [(i, (i + step * NC) % count) for i in range(count)]
    return lax.ppermute(value, "tensor", perm)


def core_swap(value):
    perm = [(i, i ^ 1) for i in range(NX * NC)]
    return lax.ppermute(value, "tensor", perm)


def tensor_gather(value):
    mine = jnp.stack([value] + [x_shift(value, step) for step in range(1, NX)])
    return mine, core_swap(mine)


def silu(value):
    half = 0.5 * value
    return half + half * jnp.tanh(half)


def sigmoid(value):
    return 0.5 + 0.5 * jnp.tanh(0.5 * value)


def prep_kernel(w_ref, latent_ref, samples_ref, actions_ref, out_ref):
    depth = w_ref.shape[0]
    part = w_ref.shape[1] // 3 // NY
    rows = out_ref.shape[2]
    line = lax.broadcasted_iota(jnp.int32, (CODES - IMAG * STOCH, rows), 0)
    acts = jnp.zeros((CODES - IMAG * STOCH, rows), jnp.float32)
    for k in range(IMAG):
        acts = jnp.where(line == k, actions_ref[k : k + 1].astype(jnp.float32), acts)
    codes = [latent_ref[...].astype(jnp.float32), samples_ref[0].astype(jnp.float32), acts]
    codes = jnp.concatenate(codes, axis=0).astype(jnp.bfloat16)
    for y in range(NY):
        for which in range(3):
            columns = w_ref[:, (which * NY + y) * part : (which * NY + y + 1) * part]
            out_ref[y, which // 2 * depth : (which // 2 + 1) * depth, which % 2 * part : (which % 2 + 1) * part] = columns
        out_ref[y, depth : 2 * depth, part:] = jnp.zeros((depth, rows - part), jnp.bfloat16)
        out_ref[y, 2 * depth :] = codes


def prep_call(w_gate, latent, samples, actions):
    depth = w_gate.shape[0]
    rows = latent.shape[1]
    vmem = pl.BlockSpec(memory_space=pltpu.VMEM)
    return pl.pallas_call(
        prep_kernel,
        in_specs=[vmem] * 4,
        out_specs=vmem,
        out_shape=jax.ShapeDtypeStruct((NY, 2 * depth + CODES, rows), jnp.bfloat16),
        compiler_params=pltpu.CompilerParams(vmem_limit_bytes=60 * MIB),
        cost_estimate=pl.CostEstimate(flops=0, bytes_accessed=NY * rows * 512, transcendentals=0),
        name="prep",
    )(w_gate, latent, samples, actions)


def copies_kernel(came_ref, out_hbm, one_ref, sems):
    depth = one_ref.shape[0] // NY
    part = one_ref.shape[1] // 3
    for y in range(NY):
        here = slice(y * depth, (y + 1) * depth)
        one_ref[here, : 2 * part] = came_ref[y, :depth, : 2 * part]
        one_ref[here, 2 * part :] = came_ref[y, depth : 2 * depth, :part]
    copies = [pltpu.make_async_copy(one_ref, out_hbm.at[z], sems.at[z]) for z in range(out_hbm.shape[0])]
    for copy in copies:
        copy.start()
    for copy in copies:
        copy.wait()


def copies_call(came, n_z, depth, width):
    return pl.pallas_call(
        copies_kernel,
        in_specs=[pl.BlockSpec(memory_space=pltpu.VMEM)],
        out_specs=pl.BlockSpec(memory_space=pltpu.HBM),
        out_shape=pltpu.HBM((n_z, NY * depth, width), jnp.bfloat16),
        scratch_shapes=[pltpu.VMEM((NY * depth, width), jnp.bfloat16), pltpu.SemaphoreType.DMA((n_z,))],
        compiler_params=pltpu.CompilerParams(vmem_limit_bytes=16 * MIB),
        cost_estimate=pl.CostEstimate(flops=0, bytes_accessed=4 * n_z * depth * width, transcendentals=0),
        name="copies",
    )(came)


def features_kernel(place_ref, came_ref, spread_ref, target_ref, mine_ref, other_ref, out_ref, w_ref):
    x, core = place_ref[0], place_ref[1]
    width = w_ref.shape[0]
    rows = out_ref.shape[1]

    @pl.when(pl.program_id(0) == 0)
    def _():
        for i in range(NX):
            base = lax.rem(x + NX - i, NX) * NC
            w_ref[:, pl.ds(pl.multiple_of((base + core) * LANES, LANES), LANES)] = mine_ref[i]
            w_ref[:, pl.ds(pl.multiple_of((base + 1 - core) * LANES, LANES), LANES)] = other_ref[i]

    codes = came_ref[came_ref.shape[0] - CODES :]
    spread = lax.dot_general(codes, spread_ref[...], (((0,), (0,)), ((), ())), preferred_element_type=jnp.float32)
    spread = jnp.concatenate([spread[:, :width], spread[:, width:]], axis=0)
    hot = jnp.where(spread == target_ref[...], 1.0, 0.0).astype(jnp.bfloat16)
    pre = jnp.dot(hot, w_ref[...], preferred_element_type=jnp.float32)
    scale = lax.rsqrt(jnp.mean(pre * pre, axis=1, keepdims=True) + EPS)
    features = silu(pre * scale).astype(jnp.bfloat16)
    for k in range(IMAG):
        out_ref[k] = features[k * rows : (k + 1) * rows]


def features_call(place, came, mine, other):
    rows = came.shape[2]
    width = mine.shape[1]
    lane = jnp.arange(width, dtype=jnp.int32)
    is_lat = lane < LAT
    target = jnp.where(is_lat, lane % CLASSES, lane - LAT).astype(jnp.float32)[None, :]
    source = [jnp.where(is_lat, k * STOCH + lane // CLASSES, IMAG * STOCH + k) for k in range(IMAG)]
    source = jnp.concatenate(source)
    spread = (jnp.arange(CODES, dtype=jnp.int32)[:, None] == source[None, :]).astype(jnp.bfloat16)
    return pl.pallas_call(
        features_kernel,
        grid=(NY,),
        in_specs=[
            pl.BlockSpec(memory_space=pltpu.SMEM),
            pl.BlockSpec((None,) + came.shape[1:], lambda b: (b, 0, 0)),
            pl.BlockSpec(spread.shape, lambda b: (0, 0)),
            pl.BlockSpec((1, width), lambda b: (0, 0)),
            pl.BlockSpec((NX, width, LANES), lambda b: (0, 0, 0)),
            pl.BlockSpec((NX, width, LANES), lambda b: (0, 0, 0)),
        ],
        out_specs=pl.BlockSpec((IMAG, None, rows, UNITS), lambda b: (0, b, 0, 0)),
        out_shape=pltpu.HBM((IMAG, NY, rows, UNITS), jnp.bfloat16),
        scratch_shapes=[pltpu.VMEM((width, UNITS), jnp.bfloat16)],
        compiler_params=pltpu.CompilerParams(vmem_limit_bytes=32 * MIB),
        cost_estimate=pl.CostEstimate(
            flops=FEATURES_WEIGHT * IMAG * NY * rows * width * (UNITS + LANES) // 5,
            bytes_accessed=IMAG * NY * rows * UNITS * 2 + width * UNITS * 2,
            transcendentals=IMAG * NY * rows * UNITS,
        ),
        name="features",
    )(place, came, spread, target, mine, other)


def gate_kernel(n_far, features_ref, gate_ref, out_ref, w_ref):
    near, held = gate_ref.shape[:2]
    depth = held // n_far

    @pl.when(pl.program_id(0) == 0)
    def _():
        for i in range(near):
            for far in range(n_far):
                w_ref[(far * near + i) * depth : (far * near + i + 1) * depth] = gate_ref[i, far * depth : (far + 1) * depth]

    for k in range(IMAG):
        out_ref[k] = jnp.dot(features_ref[k], w_ref[...], preferred_element_type=jnp.float32).astype(jnp.bfloat16)


def gate_call(features, gate, n_far):
    rows = features.shape[2]
    width = gate.shape[2]
    return pl.pallas_call(
        functools.partial(gate_kernel, n_far),
        grid=(NY,),
        in_specs=[
            pl.BlockSpec((IMAG, None, rows, UNITS), lambda b: (0, b, 0, 0)),
            pl.BlockSpec(gate.shape, lambda b: (0, 0, 0)),
        ],
        out_specs=pl.BlockSpec((None, IMAG, rows, width), lambda b: (b, 0, 0, 0)),
        out_shape=jax.ShapeDtypeStruct((NY, IMAG, rows, width), jnp.bfloat16),
        scratch_shapes=[pltpu.VMEM((UNITS, width), jnp.bfloat16)],
        compiler_params=pltpu.CompilerParams(vmem_limit_bytes=32 * MIB),
        cost_estimate=pl.CostEstimate(
            flops=2 * IMAG * NY * rows * UNITS * width,
            bytes_accessed=IMAG * NY * rows * (UNITS + width) * 2 + UNITS * width * 2,
            transcendentals=0,
        ),
        name="gate",
    )(features, gate)


def gru_kernel(
    deter_hbm, w_rec_hbm, w_in_hbm, f_ref, new_ref, prior_hbm, deter_ref, w_rec_ref, w_in_ref, mid_ref, prior_ref, sems
):
    rows, bw = deter_ref.shape
    part = bw // NY
    pairs = [(deter_hbm, deter_ref), (w_rec_hbm, w_rec_ref), (w_in_hbm, w_in_ref)]
    pairs += [(prior_ref.at[:, k], prior_hbm.at[:, k]) for k in range(IMAG)]
    copies = [pltpu.make_async_copy(src, dst, sems.at[i]) for i, (src, dst) in enumerate(pairs)]
    for copy in copies[:3]:
        copy.start()
    copies[0].wait()
    copies[1].wait()
    for k in range(IMAG):
        old_ref = deter_ref if k == 0 else mid_ref
        next_ref = new_ref if k == IMAG - 1 else mid_ref
        old = old_ref[...]
        rec = jnp.dot(old, w_rec_ref[...], preferred_element_type=jnp.float32)
        for q in range(NY):

            def gate(which):
                mine = f_ref[q, k, :, which * part : (which + 1) * part].astype(jnp.float32)
                return rec[:, which * bw + q * part : which * bw + (q + 1) * part] + mine

            reset = sigmoid(gate(0))
            candidate = jnp.tanh(reset * gate(1))
            update = sigmoid(gate(2) - 1.0)
            before = old[:, q * part : (q + 1) * part].astype(jnp.float32)
            fresh = update * candidate + (1.0 - update) * before
            next_ref[:, q * part : (q + 1) * part] = fresh.astype(jnp.bfloat16)
        if k == 0:
            copies[2].wait()
        prior = jnp.dot(next_ref[...], w_in_ref[...], preferred_element_type=jnp.float32).astype(jnp.bfloat16)
        share = prior_ref.shape[2]
        for j in range(prior_ref.shape[0]):
            prior_ref[j, k] = prior[j * share : (j + 1) * share]
        copies[3 + k].start()
    for k in range(IMAG):
        copies[3 + k].wait()


def gru_call(deter, w_rec, w_in, sums, tensor_n):
    rows, bw = deter.shape
    hbm, vmem = pl.BlockSpec(memory_space=pltpu.HBM), pl.BlockSpec(memory_space=pltpu.VMEM)
    prior = (tensor_n, IMAG, rows // tensor_n, w_in.shape[1])
    return pl.pallas_call(
        gru_kernel,
        in_specs=[hbm] * 3 + [vmem],
        out_specs=[vmem, hbm],
        out_shape=[jax.ShapeDtypeStruct((rows, bw), jnp.bfloat16), pltpu.HBM(prior, jnp.bfloat16)],
        scratch_shapes=[
            pltpu.VMEM(deter.shape, jnp.bfloat16),
            pltpu.VMEM(w_rec.shape, jnp.bfloat16),
            pltpu.VMEM(w_in.shape, jnp.bfloat16),
            pltpu.VMEM((rows, bw), jnp.bfloat16),
            pltpu.VMEM(prior, jnp.bfloat16),
            pltpu.SemaphoreType.DMA((3 + IMAG,)),
        ],
        compiler_params=pltpu.CompilerParams(vmem_limit_bytes=24 * MIB),
        cost_estimate=pl.CostEstimate(
            flops=2 * IMAG * rows * bw * (3 * bw + w_in.shape[1]),
            bytes_accessed=2 * (w_rec.size + w_in.size) + 24 * rows * bw,
            transcendentals=6 * rows * bw,
        ),
        name="gru",
    )(*[pltpu.with_memory_space_constraint(value, pltpu.HBM) for value in (deter, w_rec, w_in)], sums)


def tail_kernel(me_ref, parts_ref, mine_ref, other_ref, picked_ref, var_ref, mask_ref, log_ref):
    pre = parts_ref[0].astype(jnp.float32)
    for i in range(1, parts_ref.shape[0]):
        pre = pre + parts_ref[i].astype(jnp.float32)
    normed = pre * lax.rsqrt(jnp.mean(pre * pre, axis=1, keepdims=True) + EPS)
    hidden = (silu(normed)).astype(jnp.bfloat16)
    rows = hidden.shape[0]
    cls = lax.broadcasted_iota(jnp.int32, (NX * NC * rows, LANES), 1) % CLASSES

    def within(value, combine):
        step = 1
        while step < CLASSES:
            ahead = pltpu.roll(value, step, 1)
            wrapped = pltpu.roll(value, LANES - CLASSES + step, 1)
            value = combine(value, jnp.where(cls >= step, ahead, wrapped))
            step *= 2
        return value

    x, core = me_ref[0], me_ref[1]
    logits, wants = [], []
    for i in range(NX * NC):
        w_ref = mine_ref if i % NC == 0 else other_ref
        piece = lax.rem(x + NX - i // NC, NX) * NC + (core if i % NC == 0 else 1 - core)
        here = pl.ds(pl.multiple_of(piece * LANES, LANES), LANES)
        logits.append(jnp.dot(hidden, w_ref[i // NC], preferred_element_type=jnp.float32))
        wants.append(jnp.dot(picked_ref[...], var_ref[:, here], preferred_element_type=jnp.float32))
    logits, wants = jnp.concatenate(logits, axis=0), jnp.concatenate(wants, axis=0)
    powers = jnp.exp(logits - within(logits, jnp.maximum))
    probs = 0.99 * (powers / within(powers, jnp.add)) + 0.01 / CLASSES
    terms = jnp.where(cls.astype(jnp.float32) == wants, jnp.log(probs), 0.0)
    total = terms[:rows]
    for i in range(1, NX * NC):
        total = total + terms[i * rows : (i + 1) * rows]
    summed = jnp.where(mask_ref[...] > 0, jnp.sum(total, axis=1, keepdims=True), 0.0)
    lanes = lax.broadcasted_iota(jnp.int32, (rows, LANES), 1)
    diagonal = lax.broadcasted_iota(jnp.int32, (rows, LANES), 0) == lanes
    line = jnp.sum(jnp.where(diagonal, summed, 0.0), axis=0, keepdims=True)
    log_ref[...] = jnp.broadcast_to(line[None], log_ref.shape)


def tail_call(place, parts, mine, other, picked, mask):
    tensor_n, rows = parts.shape[:2]
    lane = jnp.arange(LAT, dtype=jnp.int32)
    var_of = (jnp.arange(STOCH, dtype=jnp.int32)[:, None] == lane[None, :] // CLASSES).astype(jnp.bfloat16)
    vmem = pl.BlockSpec(memory_space=pltpu.VMEM)
    return pl.pallas_call(
        tail_kernel,
        in_specs=[pl.BlockSpec(memory_space=pltpu.SMEM)] + [vmem] * 6,
        out_specs=vmem,
        out_shape=jax.ShapeDtypeStruct((tensor_n, 8, LANES), jnp.float32),
        compiler_params=pltpu.CompilerParams(vmem_limit_bytes=32 * MIB),
        cost_estimate=pl.CostEstimate(
            flops=2 * rows * UNITS * LAT, bytes_accessed=8 * mine.size, transcendentals=4 * rows * LAT
        ),
        name="tail",
    )(place, parts, mine, other, picked, var_of, mask)


def body(
    post_deter,
    post_sample,
    samples,
    actions,
    counts,
    w_stoch,
    w_action,
    w_gate,
    w_rec,
    w_prior_in,
    w_prior_out,
    n_dp,
):
    rows = post_deter.shape[0]
    depth = w_gate.shape[0]
    tensor_n = NX * NC
    share = rows // tensor_n
    me = lax.axis_index("tensor")
    place = jnp.stack([me // NC, me % NC]).astype(jnp.int32)

    sent = prep_call(w_gate, post_sample.T, samples.transpose(0, 2, 1), actions)
    came = lax.all_to_all(sent, "dp", 0, 0, axis_index_groups=y_groups(n_dp))
    n_far = n_dp // NY // NEAR
    held = copies_call(came, n_far, depth, w_gate.shape[1] // NY)
    held = lax.all_to_all(held, "dp", 0, 0, axis_index_groups=far_groups(n_dp)).reshape(n_far * NY * depth, -1)
    gate = jnp.broadcast_to(held[None], (NEAR,) + held.shape)
    gate = lax.all_to_all(gate, "dp", 0, 0, axis_index_groups=near_groups(n_dp))

    action_rows = jnp.pad(w_action, ((0, LANES - ACTIONS), (0, 0)))
    mine, other = tensor_gather(jnp.concatenate([w_stoch, action_rows], axis=0))

    features = features_call(place, came, mine, other)
    sums = lax.all_to_all(gate_call(features, gate, n_far), "dp", 0, 0, axis_index_groups=y_groups(n_dp))

    w_out_late, _ = lax.optimization_barrier((w_prior_out, features))
    out_mine, out_other = tensor_gather(w_out_late)

    positions = jnp.arange(STEPS, dtype=jnp.int32)
    valid_mask = (positions[None, :] < counts[:, None]).reshape(rows)
    my_mask = lax.dynamic_slice_in_dim(valid_mask, me * share, share, 0).astype(jnp.float32)
    my_mask = jnp.concatenate([my_mask] * IMAG)[:, None]
    picked = lax.dynamic_slice_in_dim(samples, me * share, share, 1)
    picked = picked.reshape(IMAG * share, STOCH).astype(jnp.bfloat16)

    deter, partial = gru_call(post_deter, w_rec[0], w_prior_in, sums, tensor_n)
    parts = lax.all_to_all(partial.reshape(tensor_n, IMAG * share, UNITS), "tensor", 0, 0)
    logs = tail_call(place, parts, out_mine, out_other, picked, my_mask)
    logs = lax.all_to_all(logs, "tensor", 0, 0)[:, 0, : IMAG * share]
    log_prob = logs.reshape(tensor_n, IMAG, share).transpose(1, 0, 2).reshape(IMAG, rows)
    deter_out = jnp.where(valid_mask[:, None], deter, jnp.zeros_like(deter))
    return (deter_out, log_prob)


def solution(mesh):
    in_specs = (
        P("dp", "tensor"),
        P("dp", None),
        P(None, "dp", None),
        P(None, "dp"),
        P("dp"),
        P(None, "tensor"),
        P(None, "tensor"),
        P("dp", "tensor"),
        P("tensor", None, None),
        P("tensor", None),
        P(None, "tensor"),
    )
    out_specs = (P("dp", "tensor"), P(None, "dp"))
    whole = functools.partial(body, n_dp=mesh.shape["dp"])
    return jax.shard_map(whole, mesh=mesh, in_specs=in_specs, out_specs=out_specs, check_vma=False)
```

```python
import functools

import jax
import jax.numpy as jnp
from jax import lax
from jax.experimental import pallas as pl
from jax.experimental.pallas import tpu as pltpu
from jax.sharding import PartitionSpec as P

STOCH = 32
CLASSES = 32
LAT = STOCH * CLASSES
ACTIONS = 18
STEPS = 64
IMAG = 2
UNITS = 1024
NY = 4
NX = 4
NC = 2
LANES = 128
CODES = 80
EPS = 1e-06
MIB = 1024 * 1024


def y_groups(n_dp):
    return [[start + y for y in range(NY)] for start in range(0, n_dp, NY)]


def z_groups(n_dp):
    return [list(range(y, n_dp, NY)) for y in range(NY)]


def x_shift(value, step):
    count = NX * NC
    perm = [(i, (i + step * NC) % count) for i in range(count)]
    return lax.ppermute(value, "tensor", perm)


def core_swap(value):
    perm = [(i, i ^ 1) for i in range(NX * NC)]
    return lax.ppermute(value, "tensor", perm)


def tensor_gather(value):
    mine = jnp.stack([value] + [x_shift(value, step) for step in range(1, NX)])
    return mine, core_swap(mine)


def silu(value):
    half = 0.5 * value
    return half + half * jnp.tanh(half)


def sigmoid(value):
    return 0.5 + 0.5 * jnp.tanh(0.5 * value)


def prep_kernel(w_ref, latent_ref, samples_ref, actions_ref, out_ref):
    depth = w_ref.shape[0]
    part = w_ref.shape[1] // 3 // NY
    rows = out_ref.shape[2]
    line = lax.broadcasted_iota(jnp.int32, (CODES - IMAG * STOCH, rows), 0)
    acts = jnp.zeros((CODES - IMAG * STOCH, rows), jnp.float32)
    for k in range(IMAG):
        acts = jnp.where(line == k, actions_ref[k : k + 1].astype(jnp.float32), acts)
    codes = [latent_ref[...].astype(jnp.float32), samples_ref[0].astype(jnp.float32), acts]
    codes = jnp.concatenate(codes, axis=0).astype(jnp.bfloat16)
    for y in range(NY):
        for which in range(3):
            columns = w_ref[:, (which * NY + y) * part : (which * NY + y + 1) * part]
            out_ref[y, which // 2 * depth : (which // 2 + 1) * depth, which % 2 * part : (which % 2 + 1) * part] = columns
        out_ref[y, depth : 2 * depth, part:] = jnp.zeros((depth, rows - part), jnp.bfloat16)
        out_ref[y, 2 * depth :] = codes


def prep_call(w_gate, latent, samples, actions):
    depth = w_gate.shape[0]
    rows = latent.shape[1]
    vmem = pl.BlockSpec(memory_space=pltpu.VMEM)
    return pl.pallas_call(
        prep_kernel,
        in_specs=[vmem] * 4,
        out_specs=vmem,
        out_shape=jax.ShapeDtypeStruct((NY, 2 * depth + CODES, rows), jnp.bfloat16),
        compiler_params=pltpu.CompilerParams(vmem_limit_bytes=60 * MIB),
        cost_estimate=pl.CostEstimate(flops=0, bytes_accessed=NY * rows * 512, transcendentals=0),
        name="prep",
    )(w_gate, latent, samples, actions)


def copies_kernel(came_ref, out_hbm, one_ref, sems):
    depth = one_ref.shape[0] // NY
    part = one_ref.shape[1] // 3
    for y in range(NY):
        here = slice(y * depth, (y + 1) * depth)
        one_ref[here, : 2 * part] = came_ref[y, :depth, : 2 * part]
        one_ref[here, 2 * part :] = came_ref[y, depth : 2 * depth, :part]
    copies = [pltpu.make_async_copy(one_ref, out_hbm.at[z], sems.at[z]) for z in range(out_hbm.shape[0])]
    for copy in copies:
        copy.start()
    for copy in copies:
        copy.wait()


def copies_call(came, n_z, depth, width):
    return pl.pallas_call(
        copies_kernel,
        in_specs=[pl.BlockSpec(memory_space=pltpu.VMEM)],
        out_specs=pl.BlockSpec(memory_space=pltpu.HBM),
        out_shape=pltpu.HBM((n_z, NY * depth, width), jnp.bfloat16),
        scratch_shapes=[pltpu.VMEM((NY * depth, width), jnp.bfloat16), pltpu.SemaphoreType.DMA((n_z,))],
        compiler_params=pltpu.CompilerParams(vmem_limit_bytes=16 * MIB),
        cost_estimate=pl.CostEstimate(flops=0, bytes_accessed=4 * n_z * depth * width, transcendentals=0),
        name="copies",
    )(came)


def features_kernel(place_ref, came_ref, spread_ref, target_ref, mine_ref, other_ref, out_ref, w_ref):
    x, core = place_ref[0], place_ref[1]
    width = w_ref.shape[0]
    rows = out_ref.shape[1]

    @pl.when(pl.program_id(0) == 0)
    def _():
        for i in range(NX):
            base = lax.rem(x + NX - i, NX) * NC
            w_ref[:, pl.ds(pl.multiple_of((base + core) * LANES, LANES), LANES)] = mine_ref[i]
            w_ref[:, pl.ds(pl.multiple_of((base + 1 - core) * LANES, LANES), LANES)] = other_ref[i]

    codes = came_ref[came_ref.shape[0] - CODES :]
    spread = lax.dot_general(codes, spread_ref[...], (((0,), (0,)), ((), ())), preferred_element_type=jnp.float32)
    spread = jnp.concatenate([spread[:, :width], spread[:, width:]], axis=0)
    hot = jnp.where(spread == target_ref[...], 1.0, 0.0).astype(jnp.bfloat16)
    pre = jnp.dot(hot, w_ref[...], preferred_element_type=jnp.float32)
    scale = lax.rsqrt(jnp.mean(pre * pre, axis=1, keepdims=True) + EPS)
    features = silu(pre * scale).astype(jnp.bfloat16)
    for k in range(IMAG):
        out_ref[k] = features[k * rows : (k + 1) * rows]


def features_call(place, came, mine, other):
    rows = came.shape[2]
    width = mine.shape[1]
    lane = jnp.arange(width, dtype=jnp.int32)
    is_lat = lane < LAT
    target = jnp.where(is_lat, lane % CLASSES, lane - LAT).astype(jnp.float32)[None, :]
    source = [jnp.where(is_lat, k * STOCH + lane // CLASSES, IMAG * STOCH + k) for k in range(IMAG)]
    source = jnp.concatenate(source)
    spread = (jnp.arange(CODES, dtype=jnp.int32)[:, None] == source[None, :]).astype(jnp.bfloat16)
    return pl.pallas_call(
        features_kernel,
        grid=(NY,),
        in_specs=[
            pl.BlockSpec(memory_space=pltpu.SMEM),
            pl.BlockSpec((None,) + came.shape[1:], lambda b: (b, 0, 0)),
            pl.BlockSpec(spread.shape, lambda b: (0, 0)),
            pl.BlockSpec((1, width), lambda b: (0, 0)),
            pl.BlockSpec((NX, width, LANES), lambda b: (0, 0, 0)),
            pl.BlockSpec((NX, width, LANES), lambda b: (0, 0, 0)),
        ],
        out_specs=pl.BlockSpec((None, IMAG, rows, UNITS), lambda b: (b, 0, 0, 0)),
        out_shape=pltpu.HBM((NY, IMAG, rows, UNITS), jnp.bfloat16),
        scratch_shapes=[pltpu.VMEM((width, UNITS), jnp.bfloat16)],
        compiler_params=pltpu.CompilerParams(vmem_limit_bytes=32 * MIB),
        cost_estimate=pl.CostEstimate(
            flops=2 * IMAG * NY * rows * width * (UNITS + LANES),
            bytes_accessed=IMAG * NY * rows * UNITS * 2 + width * UNITS * 2,
            transcendentals=IMAG * NY * rows * UNITS,
        ),
        name="features",
    )(place, came, spread, target, mine, other)


def gru_kernel(
    deter_hbm, w_rec_hbm, w_in_hbm, f_ref, new_ref, prior_hbm, deter_ref, w_rec_ref, w_in_ref, mid_ref, prior_ref, sems
):
    rows, bw = deter_ref.shape
    part = bw // NY
    half = bw // 2
    pairs = [(deter_hbm, deter_ref)]
    pairs += [(w_rec_hbm.at[pl.ds(i * half, half)], w_rec_ref.at[pl.ds(i * half, half)]) for i in range(2)]
    pairs += [(w_in_hbm, w_in_ref)]
    pairs += [(prior_ref.at[:, k], prior_hbm.at[:, k]) for k in range(IMAG)]
    copies = [pltpu.make_async_copy(src, dst, sems.at[i]) for i, (src, dst) in enumerate(pairs)]
    for copy in copies[:4]:
        copy.start()
    copies[0].wait()
    for k in range(IMAG):
        old_ref = deter_ref if k == 0 else mid_ref
        next_ref = new_ref if k == IMAG - 1 else mid_ref
        old = old_ref[...]
        if k == 0:
            copies[1].wait()
            rec = jnp.dot(old[:, :half], w_rec_ref[:half], preferred_element_type=jnp.float32)
            copies[2].wait()
            rec = rec + jnp.dot(old[:, half:], w_rec_ref[half:], preferred_element_type=jnp.float32)
        else:
            rec = jnp.dot(old, w_rec_ref[...], preferred_element_type=jnp.float32)
        for q in range(NY):

            def gate(which):
                mine = f_ref[q, k, :, which * part : (which + 1) * part].astype(jnp.float32)
                return rec[:, which * bw + q * part : which * bw + (q + 1) * part] + mine

            reset = sigmoid(gate(0))
            candidate = jnp.tanh(reset * gate(1))
            update = sigmoid(gate(2) - 1.0)
            before = old[:, q * part : (q + 1) * part].astype(jnp.float32)
            fresh = update * candidate + (1.0 - update) * before
            next_ref[:, q * part : (q + 1) * part] = fresh.astype(jnp.bfloat16)
        if k == 0:
            copies[3].wait()
        prior = jnp.dot(next_ref[...], w_in_ref[...], preferred_element_type=jnp.float32).astype(jnp.bfloat16)
        share = prior_ref.shape[2]
        for j in range(prior_ref.shape[0]):
            prior_ref[j, k] = prior[j * share : (j + 1) * share]
        copies[4 + k].start()
    for k in range(IMAG):
        copies[4 + k].wait()


def gru_call(deter, w_rec, w_in, sums, tensor_n):
    rows, bw = deter.shape
    hbm, vmem = pl.BlockSpec(memory_space=pltpu.HBM), pl.BlockSpec(memory_space=pltpu.VMEM)
    prior = (tensor_n, IMAG, rows // tensor_n, w_in.shape[1])
    return pl.pallas_call(
        gru_kernel,
        in_specs=[hbm] * 3 + [vmem],
        out_specs=[vmem, hbm],
        out_shape=[jax.ShapeDtypeStruct((rows, bw), jnp.bfloat16), pltpu.HBM(prior, jnp.bfloat16)],
        scratch_shapes=[
            pltpu.VMEM(deter.shape, jnp.bfloat16),
            pltpu.VMEM(w_rec.shape, jnp.bfloat16),
            pltpu.VMEM(w_in.shape, jnp.bfloat16),
            pltpu.VMEM((rows, bw), jnp.bfloat16),
            pltpu.VMEM(prior, jnp.bfloat16),
            pltpu.SemaphoreType.DMA((4 + IMAG,)),
        ],
        compiler_params=pltpu.CompilerParams(vmem_limit_bytes=24 * MIB),
        cost_estimate=pl.CostEstimate(
            flops=2 * IMAG * rows * bw * (3 * bw + w_in.shape[1]),
            bytes_accessed=2 * (w_rec.size + w_in.size) + 24 * rows * bw,
            transcendentals=6 * rows * bw,
        ),
        name="gru",
    )(*[pltpu.with_memory_space_constraint(value, pltpu.HBM) for value in (deter, w_rec, w_in)], sums)


def tail_kernel(me_ref, parts_ref, mine_ref, other_ref, picked_ref, var_ref, mask_ref, log_ref):
    pre = parts_ref[0].astype(jnp.float32)
    for i in range(1, parts_ref.shape[0]):
        pre = pre + parts_ref[i].astype(jnp.float32)
    normed = pre * lax.rsqrt(jnp.mean(pre * pre, axis=1, keepdims=True) + EPS)
    hidden = (silu(normed)).astype(jnp.bfloat16)
    rows = hidden.shape[0]
    cls = lax.broadcasted_iota(jnp.int32, (NX * NC * rows, LANES), 1) % CLASSES

    def within(value, combine):
        step = 1
        while step < CLASSES:
            ahead = pltpu.roll(value, step, 1)
            wrapped = pltpu.roll(value, LANES - CLASSES + step, 1)
            value = combine(value, jnp.where(cls >= step, ahead, wrapped))
            step *= 2
        return value

    x, core = me_ref[0], me_ref[1]
    logits, wants = [], []
    for i in range(NX):
        w_pair = jnp.concatenate([mine_ref[i], other_ref[i]], axis=1)
        pair = jnp.dot(hidden, w_pair, preferred_element_type=jnp.float32)
        base = lax.rem(x + NX - i, NX) * NC
        for half, piece in enumerate((base + core, base + 1 - core)):
            here = pl.ds(pl.multiple_of(piece * LANES, LANES), LANES)
            logits.append(pair[:, half * LANES : (half + 1) * LANES])
            wants.append(jnp.dot(picked_ref[...], var_ref[:, here], preferred_element_type=jnp.float32))
    logits, wants = jnp.concatenate(logits, axis=0), jnp.concatenate(wants, axis=0)
    powers = jnp.exp(logits - within(logits, jnp.maximum))
    probs = 0.99 * (powers / within(powers, jnp.add)) + 0.01 / CLASSES
    terms = jnp.where(cls.astype(jnp.float32) == wants, jnp.log(probs), 0.0)
    total = terms[:rows]
    for i in range(1, NX * NC):
        total = total + terms[i * rows : (i + 1) * rows]
    summed = jnp.where(mask_ref[...] > 0, jnp.sum(total, axis=1, keepdims=True), 0.0)
    lanes = lax.broadcasted_iota(jnp.int32, (rows, LANES), 1)
    diagonal = lax.broadcasted_iota(jnp.int32, (rows, LANES), 0) == lanes
    line = jnp.sum(jnp.where(diagonal, summed, 0.0), axis=0, keepdims=True)
    log_ref[...] = jnp.broadcast_to(line[None], log_ref.shape)


def tail_call(place, parts, mine, other, picked, mask):
    tensor_n, rows = parts.shape[:2]
    lane = jnp.arange(LAT, dtype=jnp.int32)
    var_of = (jnp.arange(STOCH, dtype=jnp.int32)[:, None] == lane[None, :] // CLASSES).astype(jnp.bfloat16)
    vmem = pl.BlockSpec(memory_space=pltpu.VMEM)
    return pl.pallas_call(
        tail_kernel,
        in_specs=[pl.BlockSpec(memory_space=pltpu.SMEM)] + [vmem] * 6,
        out_specs=vmem,
        out_shape=jax.ShapeDtypeStruct((tensor_n, 8, LANES), jnp.float32),
        compiler_params=pltpu.CompilerParams(vmem_limit_bytes=32 * MIB),
        cost_estimate=pl.CostEstimate(
            flops=2 * rows * UNITS * LAT, bytes_accessed=8 * mine.size, transcendentals=4 * rows * LAT
        ),
        name="tail",
    )(place, parts, mine, other, picked, var_of, mask)


def body(
    post_deter,
    post_sample,
    samples,
    actions,
    counts,
    w_stoch,
    w_action,
    w_gate,
    w_rec,
    w_prior_in,
    w_prior_out,
    n_dp,
):
    rows = post_deter.shape[0]
    depth = w_gate.shape[0]
    tensor_n = NX * NC
    share = rows // tensor_n
    me = lax.axis_index("tensor")
    place = jnp.stack([me // NC, me % NC]).astype(jnp.int32)

    sent = prep_call(w_gate, post_sample.T, samples.transpose(0, 2, 1), actions)
    came = lax.all_to_all(sent, "dp", 0, 0, axis_index_groups=y_groups(n_dp))
    held = copies_call(came, n_dp // NY, depth, w_gate.shape[1] // NY)
    gate = lax.all_to_all(held, "dp", 0, 0, axis_index_groups=z_groups(n_dp)).reshape(n_dp * depth, -1)

    action_rows = jnp.pad(w_action, ((0, LANES - ACTIONS), (0, 0)))
    mine, other = tensor_gather(jnp.concatenate([w_stoch, action_rows], axis=0))

    features = features_call(place, came, mine, other)
    total = jnp.dot(features.reshape(-1, UNITS), gate, preferred_element_type=jnp.float32).astype(jnp.bfloat16)
    total = total.reshape(NY, IMAG, rows, -1)
    sums = lax.all_to_all(total, "dp", 0, 0, axis_index_groups=y_groups(n_dp))

    w_out_late, _ = lax.optimization_barrier((w_prior_out, features))
    out_mine, out_other = tensor_gather(w_out_late)

    positions = jnp.arange(STEPS, dtype=jnp.int32)
    valid_mask = (positions[None, :] < counts[:, None]).reshape(rows)
    my_mask = lax.dynamic_slice_in_dim(valid_mask, me * share, share, 0).astype(jnp.float32)
    my_mask = jnp.concatenate([my_mask] * IMAG)[:, None]
    picked = lax.dynamic_slice_in_dim(samples, me * share, share, 1)
    picked = picked.reshape(IMAG * share, STOCH).astype(jnp.bfloat16)

    deter, partial = gru_call(post_deter, w_rec[0], w_prior_in, sums, tensor_n)
    parts = lax.all_to_all(partial.reshape(tensor_n, IMAG * share, UNITS), "tensor", 0, 0)
    logs = tail_call(place, parts, out_mine, out_other, picked, my_mask)
    logs = lax.all_to_all(logs, "tensor", 0, 0)[:, 0, : IMAG * share]
    log_prob = logs.reshape(tensor_n, IMAG, share).transpose(1, 0, 2).reshape(IMAG, rows)
    deter_out = jnp.where(valid_mask[:, None], deter, jnp.zeros_like(deter))
    return (deter_out, log_prob)


def solution(mesh):
    in_specs = (
        P("dp", "tensor"),
        P("dp", None),
        P(None, "dp", None),
        P(None, "dp"),
        P("dp"),
        P(None, "tensor"),
        P(None, "tensor"),
        P("dp", "tensor"),
        P("tensor", None, None),
        P("tensor", None),
        P(None, "tensor"),
    )
    out_specs = (P("dp", "tensor"), P(None, "dp"))
    whole = functools.partial(body, n_dp=mesh.shape["dp"])
    return jax.shard_map(whole, mesh=mesh, in_specs=in_specs, out_specs=out_specs, check_vma=False)
```

```python
import functools

import jax
import jax.numpy as jnp
from jax import lax
from jax.experimental import pallas as pl
from jax.experimental.pallas import tpu as pltpu
from jax.sharding import PartitionSpec as P

STOCH = 32
CLASSES = 32
LAT = STOCH * CLASSES
ACTIONS = 18
STEPS = 64
IMAG = 2
UNITS = 1024
NY = 4
NX = 4
NC = 2
LANES = 128
NEAR = 4
CODES = 80
EPS = 1e-06
MIB = 1024 * 1024
FEATURES_WEIGHT = 12


def y_groups(n_dp):
    return [[start + y for y in range(NY)] for start in range(0, n_dp, NY)]


def far_groups(n_dp):
    n_far = n_dp // NY // NEAR
    return [[(far * NEAR + near) * NY + y for far in range(n_far)] for near in range(NEAR) for y in range(NY)]


def near_groups(n_dp):
    n_far = n_dp // NY // NEAR
    return [[(far * NEAR + near) * NY + y for near in range(NEAR)] for far in range(n_far) for y in range(NY)]


def x_shift(value, step):
    count = NX * NC
    perm = [(i, (i + step * NC) % count) for i in range(count)]
    return lax.ppermute(value, "tensor", perm)


def core_swap(value):
    perm = [(i, i ^ 1) for i in range(NX * NC)]
    return lax.ppermute(value, "tensor", perm)


def tensor_gather(value):
    pieces = [value] + [x_shift(value, step) for step in range(1, NX)]
    mine = jnp.stack(pieces)
    return mine, core_swap(mine), pieces[1]


def silu(value):
    half = 0.5 * value
    return half + half * jnp.tanh(half)


def sigmoid(value):
    return 0.5 + 0.5 * jnp.tanh(0.5 * value)


def prep_kernel(w_ref, latent_ref, samples_ref, actions_ref, out_ref):
    depth = w_ref.shape[0]
    part = w_ref.shape[1] // 3 // NY
    rows = out_ref.shape[2]
    line = lax.broadcasted_iota(jnp.int32, (CODES - IMAG * STOCH, rows), 0)
    acts = jnp.zeros((CODES - IMAG * STOCH, rows), jnp.float32)
    for k in range(IMAG):
        acts = jnp.where(line == k, actions_ref[k : k + 1].astype(jnp.float32), acts)
    codes = [latent_ref[...].astype(jnp.float32), samples_ref[0].astype(jnp.float32), acts]
    codes = jnp.concatenate(codes, axis=0).astype(jnp.bfloat16)
    for y in range(NY):
        for which in range(3):
            columns = w_ref[:, (which * NY + y) * part : (which * NY + y + 1) * part]
            out_ref[y, which // 2 * depth : (which // 2 + 1) * depth, which % 2 * part : (which % 2 + 1) * part] = columns
        out_ref[y, depth : 2 * depth, part:] = jnp.zeros((depth, rows - part), jnp.bfloat16)
        out_ref[y, 2 * depth :] = codes


def prep_call(w_gate, latent, samples, actions):
    depth = w_gate.shape[0]
    rows = latent.shape[1]
    vmem = pl.BlockSpec(memory_space=pltpu.VMEM)
    return pl.pallas_call(
        prep_kernel,
        in_specs=[vmem] * 4,
        out_specs=vmem,
        out_shape=jax.ShapeDtypeStruct((NY, 2 * depth + CODES, rows), jnp.bfloat16),
        compiler_params=pltpu.CompilerParams(vmem_limit_bytes=60 * MIB),
        cost_estimate=pl.CostEstimate(flops=0, bytes_accessed=NY * rows * 512, transcendentals=0),
        name="prep",
    )(w_gate, latent, samples, actions)


def copies_kernel(came_ref, _, out_hbm, one_ref, sems):
    depth = one_ref.shape[0] // NY
    part = one_ref.shape[1] // 3
    for y in range(NY):
        here = slice(y * depth, (y + 1) * depth)
        one_ref[here, : 2 * part] = came_ref[y, :depth, : 2 * part]
        one_ref[here, 2 * part :] = came_ref[y, depth : 2 * depth, :part]
    copies = [pltpu.make_async_copy(one_ref, out_hbm.at[z], sems.at[z]) for z in range(out_hbm.shape[0])]
    for copy in copies:
        copy.start()
    for copy in copies:
        copy.wait()


def copies_call(came, early, n_z, depth, width):
    return pl.pallas_call(
        copies_kernel,
        in_specs=[pl.BlockSpec(memory_space=pltpu.VMEM), pl.BlockSpec(memory_space=pl.ANY)],
        out_specs=pl.BlockSpec(memory_space=pltpu.HBM),
        out_shape=pltpu.HBM((n_z, NY * depth, width), jnp.bfloat16),
        scratch_shapes=[pltpu.VMEM((NY * depth, width), jnp.bfloat16), pltpu.SemaphoreType.DMA((n_z,))],
        compiler_params=pltpu.CompilerParams(vmem_limit_bytes=16 * MIB),
        cost_estimate=pl.CostEstimate(flops=0, bytes_accessed=4 * n_z * depth * width, transcendentals=0),
        name="copies",
    )(came, early)


def features_kernel(place_ref, came_ref, spread_ref, target_ref, mine_ref, other_ref, out_ref, w_ref):
    x, core = place_ref[0], place_ref[1]
    width = w_ref.shape[0]
    rows = out_ref.shape[1]

    @pl.when(pl.program_id(0) == 0)
    def _():
        for i in range(NX):
            base = lax.rem(x + NX - i, NX) * NC
            w_ref[:, pl.ds(pl.multiple_of((base + core) * LANES, LANES), LANES)] = mine_ref[i]
            w_ref[:, pl.ds(pl.multiple_of((base + 1 - core) * LANES, LANES), LANES)] = other_ref[i]

    codes = came_ref[came_ref.shape[0] - CODES :]
    spread = lax.dot_general(codes, spread_ref[...], (((0,), (0,)), ((), ())), preferred_element_type=jnp.float32)
    spread = jnp.concatenate([spread[:, :width], spread[:, width:]], axis=0)
    hot = jnp.where(spread == target_ref[...], 1.0, 0.0).astype(jnp.bfloat16)
    pre = jnp.dot(hot, w_ref[...], preferred_element_type=jnp.float32)
    scale = lax.rsqrt(jnp.mean(pre * pre, axis=1, keepdims=True) + EPS)
    features = silu(pre * scale).astype(jnp.bfloat16)
    for k in range(IMAG):
        out_ref[k] = features[k * rows : (k + 1) * rows]


def features_call(place, came, mine, other):
    rows = came.shape[2]
    width = mine.shape[1]
    lane = jnp.arange(width, dtype=jnp.int32)
    is_lat = lane < LAT
    target = jnp.where(is_lat, lane % CLASSES, lane - LAT).astype(jnp.float32)[None, :]
    source = [jnp.where(is_lat, k * STOCH + lane // CLASSES, IMAG * STOCH + k) for k in range(IMAG)]
    source = jnp.concatenate(source)
    spread = (jnp.arange(CODES, dtype=jnp.int32)[:, None] == source[None, :]).astype(jnp.bfloat16)
    return pl.pallas_call(
        features_kernel,
        grid=(NY,),
        in_specs=[
            pl.BlockSpec(memory_space=pltpu.SMEM),
            pl.BlockSpec((None,) + came.shape[1:], lambda b: (b, 0, 0)),
            pl.BlockSpec(spread.shape, lambda b: (0, 0)),
            pl.BlockSpec((1, width), lambda b: (0, 0)),
            pl.BlockSpec((NX, width, LANES), lambda b: (0, 0, 0)),
            pl.BlockSpec((NX, width, LANES), lambda b: (0, 0, 0)),
        ],
        out_specs=pl.BlockSpec((IMAG, None, rows, UNITS), lambda b: (0, b, 0, 0)),
        out_shape=pltpu.HBM((IMAG, NY, rows, UNITS), jnp.bfloat16),
        scratch_shapes=[pltpu.VMEM((width, UNITS), jnp.bfloat16)],
        compiler_params=pltpu.CompilerParams(vmem_limit_bytes=32 * MIB),
        cost_estimate=pl.CostEstimate(
            flops=FEATURES_WEIGHT * IMAG * NY * rows * width * (UNITS + LANES) // 5,
            bytes_accessed=IMAG * NY * rows * UNITS * 2 + width * UNITS * 2,
            transcendentals=IMAG * NY * rows * UNITS,
        ),
        name="features",
    )(place, came, spread, target, mine, other)


def gate_kernel(n_far, features_ref, gate_ref, out_ref, w_ref):
    near, held = gate_ref.shape[:2]
    depth = held // n_far

    @pl.when(pl.program_id(0) == 0)
    def _():
        for i in range(near):
            for far in range(n_far):
                w_ref[(far * near + i) * depth : (far * near + i + 1) * depth] = gate_ref[i, far * depth : (far + 1) * depth]

    for k in range(IMAG):
        out_ref[k] = jnp.dot(features_ref[k], w_ref[...], preferred_element_type=jnp.float32).astype(jnp.bfloat16)


def gate_call(features, gate, n_far):
    rows = features.shape[2]
    width = gate.shape[2]
    return pl.pallas_call(
        functools.partial(gate_kernel, n_far),
        grid=(NY,),
        in_specs=[
            pl.BlockSpec((IMAG, None, rows, UNITS), lambda b: (0, b, 0, 0)),
            pl.BlockSpec(gate.shape, lambda b: (0, 0, 0)),
        ],
        out_specs=pl.BlockSpec((None, IMAG, rows, width), lambda b: (b, 0, 0, 0)),
        out_shape=jax.ShapeDtypeStruct((NY, IMAG, rows, width), jnp.bfloat16),
        scratch_shapes=[pltpu.VMEM((UNITS, width), jnp.bfloat16)],
        compiler_params=pltpu.CompilerParams(vmem_limit_bytes=32 * MIB),
        cost_estimate=pl.CostEstimate(
            flops=2 * IMAG * NY * rows * UNITS * width,
            bytes_accessed=IMAG * NY * rows * (UNITS + width) * 2 + UNITS * width * 2,
            transcendentals=0,
        ),
        name="gate",
    )(features, gate)


def gru_kernel(
    deter_hbm, w_rec_hbm, w_in_hbm, f_ref, new_ref, prior_hbm, deter_ref, w_rec_ref, w_in_ref, mid_ref, prior_ref, sems
):
    rows, bw = deter_ref.shape
    part = bw // NY
    pairs = [(deter_hbm, deter_ref), (w_rec_hbm, w_rec_ref), (w_in_hbm, w_in_ref)]
    pairs += [(prior_ref.at[:, k], prior_hbm.at[:, k]) for k in range(IMAG)]
    copies = [pltpu.make_async_copy(src, dst, sems.at[i]) for i, (src, dst) in enumerate(pairs)]
    for copy in copies[:3]:
        copy.start()
    copies[0].wait()
    copies[1].wait()
    for k in range(IMAG):
        old_ref = deter_ref if k == 0 else mid_ref
        next_ref = new_ref if k == IMAG - 1 else mid_ref
        old = old_ref[...]
        rec = jnp.dot(old, w_rec_ref[...], preferred_element_type=jnp.float32)
        for q in range(NY):

            def gate(which):
                mine = f_ref[q, k, :, which * part : (which + 1) * part].astype(jnp.float32)
                return rec[:, which * bw + q * part : which * bw + (q + 1) * part] + mine

            reset = sigmoid(gate(0))
            candidate = jnp.tanh(reset * gate(1))
            update = sigmoid(gate(2) - 1.0)
            before = old[:, q * part : (q + 1) * part].astype(jnp.float32)
            fresh = update * candidate + (1.0 - update) * before
            next_ref[:, q * part : (q + 1) * part] = fresh.astype(jnp.bfloat16)
        if k == 0:
            copies[2].wait()
        prior = jnp.dot(next_ref[...], w_in_ref[...], preferred_element_type=jnp.float32).astype(jnp.bfloat16)
        share = prior_ref.shape[2]
        for j in range(prior_ref.shape[0]):
            prior_ref[j, k] = prior[j * share : (j + 1) * share]
        copies[3 + k].start()
    for k in range(IMAG):
        copies[3 + k].wait()


def gru_call(deter, w_rec, w_in, sums, tensor_n):
    rows, bw = deter.shape
    hbm, vmem = pl.BlockSpec(memory_space=pltpu.HBM), pl.BlockSpec(memory_space=pltpu.VMEM)
    prior = (tensor_n, IMAG, rows // tensor_n, w_in.shape[1])
    return pl.pallas_call(
        gru_kernel,
        in_specs=[hbm] * 3 + [vmem],
        out_specs=[vmem, hbm],
        out_shape=[jax.ShapeDtypeStruct((rows, bw), jnp.bfloat16), pltpu.HBM(prior, jnp.bfloat16)],
        scratch_shapes=[
            pltpu.VMEM(deter.shape, jnp.bfloat16),
            pltpu.VMEM(w_rec.shape, jnp.bfloat16),
            pltpu.VMEM(w_in.shape, jnp.bfloat16),
            pltpu.VMEM((rows, bw), jnp.bfloat16),
            pltpu.VMEM(prior, jnp.bfloat16),
            pltpu.SemaphoreType.DMA((3 + IMAG,)),
        ],
        compiler_params=pltpu.CompilerParams(vmem_limit_bytes=24 * MIB),
        cost_estimate=pl.CostEstimate(
            flops=2 * IMAG * rows * bw * (3 * bw + w_in.shape[1]),
            bytes_accessed=2 * (w_rec.size + w_in.size) + 24 * rows * bw,
            transcendentals=6 * rows * bw,
        ),
        name="gru",
    )(*[pltpu.with_memory_space_constraint(value, pltpu.HBM) for value in (deter, w_rec, w_in)], sums)


def tail_kernel(me_ref, parts_ref, mine_ref, other_ref, picked_ref, var_ref, mask_ref, log_ref):
    pre = parts_ref[0].astype(jnp.float32)
    for i in range(1, parts_ref.shape[0]):
        pre = pre + parts_ref[i].astype(jnp.float32)
    normed = pre * lax.rsqrt(jnp.mean(pre * pre, axis=1, keepdims=True) + EPS)
    hidden = (silu(normed)).astype(jnp.bfloat16)
    rows = hidden.shape[0]
    cls = lax.broadcasted_iota(jnp.int32, (NX * NC * rows, LANES), 1) % CLASSES

    def within(value, combine):
        step = 1
        while step < CLASSES:
            ahead = pltpu.roll(value, step, 1)
            wrapped = pltpu.roll(value, LANES - CLASSES + step, 1)
            value = combine(value, jnp.where(cls >= step, ahead, wrapped))
            step *= 2
        return value

    x, core = me_ref[0], me_ref[1]
    logits, wants = [], []
    for i in range(NX * NC):
        w_ref = mine_ref if i % NC == 0 else other_ref
        piece = lax.rem(x + NX - i // NC, NX) * NC + (core if i % NC == 0 else 1 - core)
        here = pl.ds(pl.multiple_of(piece * LANES, LANES), LANES)
        logits.append(jnp.dot(hidden, w_ref[i // NC], preferred_element_type=jnp.float32))
        wants.append(jnp.dot(picked_ref[...], var_ref[:, here], preferred_element_type=jnp.float32))
    logits, wants = jnp.concatenate(logits, axis=0), jnp.concatenate(wants, axis=0)
    powers = jnp.exp(logits - within(logits, jnp.maximum))
    probs = 0.99 * (powers / within(powers, jnp.add)) + 0.01 / CLASSES
    terms = jnp.where(cls.astype(jnp.float32) == wants, jnp.log(probs), 0.0)
    total = terms[:rows]
    for i in range(1, NX * NC):
        total = total + terms[i * rows : (i + 1) * rows]
    summed = jnp.where(mask_ref[...] > 0, jnp.sum(total, axis=1, keepdims=True), 0.0)
    lanes = lax.broadcasted_iota(jnp.int32, (rows, LANES), 1)
    diagonal = lax.broadcasted_iota(jnp.int32, (rows, LANES), 0) == lanes
    line = jnp.sum(jnp.where(diagonal, summed, 0.0), axis=0, keepdims=True)
    log_ref[...] = jnp.broadcast_to(line[None], log_ref.shape)


def tail_call(place, parts, mine, other, picked, mask):
    tensor_n, rows = parts.shape[:2]
    lane = jnp.arange(LAT, dtype=jnp.int32)
    var_of = (jnp.arange(STOCH, dtype=jnp.int32)[:, None] == lane[None, :] // CLASSES).astype(jnp.bfloat16)
    vmem = pl.BlockSpec(memory_space=pltpu.VMEM)
    return pl.pallas_call(
        tail_kernel,
        in_specs=[pl.BlockSpec(memory_space=pltpu.SMEM)] + [vmem] * 6,
        out_specs=vmem,
        out_shape=jax.ShapeDtypeStruct((tensor_n, 8, LANES), jnp.float32),
        compiler_params=pltpu.CompilerParams(vmem_limit_bytes=32 * MIB),
        cost_estimate=pl.CostEstimate(
            flops=2 * rows * UNITS * LAT, bytes_accessed=8 * mine.size, transcendentals=4 * rows * LAT
        ),
        name="tail",
    )(place, parts, mine, other, picked, var_of, mask)


def body(
    post_deter,
    post_sample,
    samples,
    actions,
    counts,
    w_stoch,
    w_action,
    w_gate,
    w_rec,
    w_prior_in,
    w_prior_out,
    n_dp,
):
    rows = post_deter.shape[0]
    depth = w_gate.shape[0]
    tensor_n = NX * NC
    share = rows // tensor_n
    me = lax.axis_index("tensor")
    place = jnp.stack([me // NC, me % NC]).astype(jnp.int32)

    sent = prep_call(w_gate, post_sample.T, samples.transpose(0, 2, 1), actions)
    came = lax.all_to_all(sent, "dp", 0, 0, axis_index_groups=y_groups(n_dp))
    action_rows = jnp.pad(w_action, ((0, LANES - ACTIONS), (0, 0)))
    mine, other, early = tensor_gather(jnp.concatenate([w_stoch, action_rows], axis=0))

    n_far = n_dp // NY // NEAR
    held = copies_call(came, early, n_far, depth, w_gate.shape[1] // NY)
    held = lax.all_to_all(held, "dp", 0, 0, axis_index_groups=far_groups(n_dp)).reshape(n_far * NY * depth, -1)
    gate = jnp.broadcast_to(held[None], (NEAR,) + held.shape)
    gate = lax.all_to_all(gate, "dp", 0, 0, axis_index_groups=near_groups(n_dp))

    features = features_call(place, came, mine, other)
    sums = lax.all_to_all(gate_call(features, gate, n_far), "dp", 0, 0, axis_index_groups=y_groups(n_dp))

    w_out_late, _ = lax.optimization_barrier((w_prior_out, features))
    out_mine, out_other, _ = tensor_gather(w_out_late)

    positions = jnp.arange(STEPS, dtype=jnp.int32)
    valid_mask = (positions[None, :] < counts[:, None]).reshape(rows)
    my_mask = lax.dynamic_slice_in_dim(valid_mask, me * share, share, 0).astype(jnp.float32)
    my_mask = jnp.concatenate([my_mask] * IMAG)[:, None]
    picked = lax.dynamic_slice_in_dim(samples, me * share, share, 1)
    picked = picked.reshape(IMAG * share, STOCH).astype(jnp.bfloat16)

    deter, partial = gru_call(post_deter, w_rec[0], w_prior_in, sums, tensor_n)
    parts = lax.all_to_all(partial.reshape(tensor_n, IMAG * share, UNITS), "tensor", 0, 0)
    logs = tail_call(place, parts, out_mine, out_other, picked, my_mask)
    logs = lax.all_to_all(logs, "tensor", 0, 0)[:, 0, : IMAG * share]
    log_prob = logs.reshape(tensor_n, IMAG, share).transpose(1, 0, 2).reshape(IMAG, rows)
    deter_out = jnp.where(valid_mask[:, None], deter, jnp.zeros_like(deter))
    return (deter_out, log_prob)


def solution(mesh):
    in_specs = (
        P("dp", "tensor"),
        P("dp", None),
        P(None, "dp", None),
        P(None, "dp"),
        P("dp"),
        P(None, "tensor"),
        P(None, "tensor"),
        P("dp", "tensor"),
        P("tensor", None, None),
        P("tensor", None),
        P(None, "tensor"),
    )
    out_specs = (P("dp", "tensor"), P(None, "dp"))
    whole = functools.partial(body, n_dp=mesh.shape["dp"])
    return jax.shard_map(whole, mesh=mesh, in_specs=in_specs, out_specs=out_specs, check_vma=False)
```

```python
import functools

import jax
import jax.numpy as jnp
from jax import lax
from jax.experimental import pallas as pl
from jax.experimental.pallas import tpu as pltpu
from jax.sharding import PartitionSpec as P

STOCH = 32
CLASSES = 32
LAT = STOCH * CLASSES
ACTIONS = 18
STEPS = 64
IMAG = 2
UNITS = 1024
NY = 4
NX = 4
NC = 2
LANES = 128
CODES = 80
EPS = 1e-06
MIB = 1024 * 1024


def y_groups(n_dp):
    return [[start + y for y in range(NY)] for start in range(0, n_dp, NY)]


def z_groups(n_dp):
    return [list(range(y, n_dp, NY)) for y in range(NY)]


def x_shift(value, step):
    count = NX * NC
    perm = [(i, (i + step * NC) % count) for i in range(count)]
    return lax.ppermute(value, "tensor", perm)


def core_swap(value):
    perm = [(i, i ^ 1) for i in range(NX * NC)]
    return lax.ppermute(value, "tensor", perm)


def tensor_gather(value):
    mine = jnp.stack([value] + [x_shift(value, step) for step in range(1, NX)])
    return mine, core_swap(mine)


def silu(value):
    half = 0.5 * value
    return half + half * jnp.tanh(half)


def sigmoid(value):
    return 0.5 + 0.5 * jnp.tanh(0.5 * value)


def prep_kernel(w_ref, latent_ref, samples_ref, actions_ref, out_ref):
    depth = w_ref.shape[0]
    part = w_ref.shape[1] // 3 // NY
    rows = out_ref.shape[2]
    line = lax.broadcasted_iota(jnp.int32, (CODES - IMAG * STOCH, rows), 0)
    acts = jnp.zeros((CODES - IMAG * STOCH, rows), jnp.float32)
    for k in range(IMAG):
        acts = jnp.where(line == k, actions_ref[k : k + 1].astype(jnp.float32), acts)
    codes = [latent_ref[...].astype(jnp.float32), samples_ref[0].astype(jnp.float32), acts]
    codes = jnp.concatenate(codes, axis=0).astype(jnp.bfloat16)
    for y in range(NY):
        for which in range(3):
            columns = w_ref[:, (which * NY + y) * part : (which * NY + y + 1) * part]
            out_ref[y, which // 2 * depth : (which // 2 + 1) * depth, which % 2 * part : (which % 2 + 1) * part] = columns
        out_ref[y, depth : 2 * depth, part:] = jnp.zeros((depth, rows - part), jnp.bfloat16)
        out_ref[y, 2 * depth :] = codes


def prep_call(w_gate, latent, samples, actions):
    depth = w_gate.shape[0]
    rows = latent.shape[1]
    vmem = pl.BlockSpec(memory_space=pltpu.VMEM)
    return pl.pallas_call(
        prep_kernel,
        in_specs=[vmem] * 4,
        out_specs=vmem,
        out_shape=jax.ShapeDtypeStruct((NY, 2 * depth + CODES, rows), jnp.bfloat16),
        compiler_params=pltpu.CompilerParams(vmem_limit_bytes=60 * MIB),
        cost_estimate=pl.CostEstimate(flops=0, bytes_accessed=NY * rows * 512, transcendentals=0),
        name="prep",
    )(w_gate, latent, samples, actions)


def copies_kernel(came_ref, out_hbm, one_ref, sems):
    depth = one_ref.shape[0] // NY
    part = one_ref.shape[1] // 3
    for y in range(NY):
        here = slice(y * depth, (y + 1) * depth)
        one_ref[here, : 2 * part] = came_ref[y, :depth, : 2 * part]
        one_ref[here, 2 * part :] = came_ref[y, depth : 2 * depth, :part]
    copies = [pltpu.make_async_copy(one_ref, out_hbm.at[z], sems.at[z]) for z in range(out_hbm.shape[0])]
    for copy in copies:
        copy.start()
    for copy in copies:
        copy.wait()


def copies_call(came, n_z, depth, width):
    return pl.pallas_call(
        copies_kernel,
        in_specs=[pl.BlockSpec(memory_space=pltpu.VMEM)],
        out_specs=pl.BlockSpec(memory_space=pltpu.HBM),
        out_shape=pltpu.HBM((n_z, NY * depth, width), jnp.bfloat16),
        scratch_shapes=[pltpu.VMEM((NY * depth, width), jnp.bfloat16), pltpu.SemaphoreType.DMA((n_z,))],
        compiler_params=pltpu.CompilerParams(vmem_limit_bytes=16 * MIB),
        cost_estimate=pl.CostEstimate(flops=0, bytes_accessed=4 * n_z * depth * width, transcendentals=0),
        name="copies",
    )(came)


def features_kernel(place_ref, came_ref, spread_ref, target_ref, mine_ref, other_ref, out_ref, w_ref):
    x, core = place_ref[0], place_ref[1]
    width = w_ref.shape[0]
    rows = out_ref.shape[1]

    @pl.when(pl.program_id(0) == 0)
    def _():
        for i in range(NX):
            base = lax.rem(x + NX - i, NX) * NC
            w_ref[:, pl.ds(pl.multiple_of((base + core) * LANES, LANES), LANES)] = mine_ref[i]
            w_ref[:, pl.ds(pl.multiple_of((base + 1 - core) * LANES, LANES), LANES)] = other_ref[i]

    codes = came_ref[came_ref.shape[0] - CODES :]
    spread = lax.dot_general(codes, spread_ref[...], (((0,), (0,)), ((), ())), preferred_element_type=jnp.float32)
    spread = jnp.concatenate([spread[:, :width], spread[:, width:]], axis=0)
    hot = jnp.where(spread == target_ref[...], 1.0, 0.0).astype(jnp.bfloat16)
    pre = jnp.dot(hot, w_ref[...], preferred_element_type=jnp.float32)
    scale = lax.rsqrt(jnp.mean(pre * pre, axis=1, keepdims=True) + EPS)
    features = silu(pre * scale).astype(jnp.bfloat16)
    for k in range(IMAG):
        out_ref[k] = features[k * rows : (k + 1) * rows]


def features_call(place, came, mine, other):
    rows = came.shape[2]
    width = mine.shape[1]
    lane = jnp.arange(width, dtype=jnp.int32)
    is_lat = lane < LAT
    target = jnp.where(is_lat, lane % CLASSES, lane - LAT).astype(jnp.float32)[None, :]
    source = [jnp.where(is_lat, k * STOCH + lane // CLASSES, IMAG * STOCH + k) for k in range(IMAG)]
    source = jnp.concatenate(source)
    spread = (jnp.arange(CODES, dtype=jnp.int32)[:, None] == source[None, :]).astype(jnp.bfloat16)
    return pl.pallas_call(
        features_kernel,
        grid=(NY,),
        in_specs=[
            pl.BlockSpec(memory_space=pltpu.SMEM),
            pl.BlockSpec((None,) + came.shape[1:], lambda b: (b, 0, 0)),
            pl.BlockSpec(spread.shape, lambda b: (0, 0)),
            pl.BlockSpec((1, width), lambda b: (0, 0)),
            pl.BlockSpec((NX, width, LANES), lambda b: (0, 0, 0)),
            pl.BlockSpec((NX, width, LANES), lambda b: (0, 0, 0)),
        ],
        out_specs=pl.BlockSpec((None, IMAG, rows, UNITS), lambda b: (b, 0, 0, 0)),
        out_shape=pltpu.HBM((NY, IMAG, rows, UNITS), jnp.bfloat16),
        scratch_shapes=[pltpu.VMEM((width, UNITS), jnp.bfloat16)],
        compiler_params=pltpu.CompilerParams(vmem_limit_bytes=32 * MIB),
        cost_estimate=pl.CostEstimate(
            flops=2 * IMAG * NY * rows * width * (UNITS + LANES),
            bytes_accessed=IMAG * NY * rows * UNITS * 2 + width * UNITS * 2,
            transcendentals=IMAG * NY * rows * UNITS,
        ),
        name="features",
    )(place, came, spread, target, mine, other)


def gru_kernel(
    me_ref, deter_hbm, w_rec_hbm, w_in_hbm, f_ref, new_ref, keep_hbm, send_hbm, deter_ref, w_rec_ref, w_in_ref, mid_ref, prior_ref, sems
):
    rows, bw = deter_ref.shape
    part = bw // NY
    pairs = [(deter_hbm, deter_ref), (w_rec_hbm, w_rec_ref), (w_in_hbm, w_in_ref)]
    pairs += [(prior_ref.at[i, :, k], out.at[:, k]) for k in range(IMAG) for i, out in enumerate((keep_hbm, send_hbm))]
    copies = [pltpu.make_async_copy(src, dst, sems.at[i]) for i, (src, dst) in enumerate(pairs)]
    for copy in copies[:3]:
        copy.start()
    copies[0].wait()
    copies[1].wait()
    for k in range(IMAG):
        old_ref = deter_ref if k == 0 else mid_ref
        next_ref = new_ref if k == IMAG - 1 else mid_ref
        old = old_ref[...]
        rec = jnp.dot(old, w_rec_ref[...], preferred_element_type=jnp.float32)
        for q in range(NY):

            def gate(which):
                mine = f_ref[q, k, :, which * part : (which + 1) * part].astype(jnp.float32)
                return rec[:, which * bw + q * part : which * bw + (q + 1) * part] + mine

            reset = sigmoid(gate(0))
            candidate = jnp.tanh(reset * gate(1))
            update = sigmoid(gate(2) - 1.0)
            before = old[:, q * part : (q + 1) * part].astype(jnp.float32)
            fresh = update * candidate + (1.0 - update) * before
            next_ref[:, q * part : (q + 1) * part] = fresh.astype(jnp.bfloat16)
        if k == 0:
            copies[2].wait()
        prior = jnp.dot(next_ref[...], w_in_ref[...], preferred_element_type=jnp.float32).astype(jnp.bfloat16)
        share = prior_ref.shape[3]
        for j in range(NX * NC):
            other = lax.rem(me_ref[1] + j % NC, NC)
            prior_ref[other, j // NC, k] = prior[j * share : (j + 1) * share]
        for i in range(NC):
            copies[3 + NC * k + i].start()
    for copy in copies[3:]:
        copy.wait()


def gru_call(place, deter, w_rec, w_in, sums):
    rows, bw = deter.shape
    hbm, vmem = pl.BlockSpec(memory_space=pltpu.HBM), pl.BlockSpec(memory_space=pltpu.VMEM)
    prior = (NX, IMAG, rows // (NX * NC), w_in.shape[1])
    return pl.pallas_call(
        gru_kernel,
        in_specs=[pl.BlockSpec(memory_space=pltpu.SMEM)] + [hbm] * 3 + [vmem],
        out_specs=[vmem, hbm, hbm],
        out_shape=[jax.ShapeDtypeStruct((rows, bw), jnp.bfloat16), pltpu.HBM(prior, jnp.bfloat16), pltpu.HBM(prior, jnp.bfloat16)],
        scratch_shapes=[
            pltpu.VMEM(deter.shape, jnp.bfloat16),
            pltpu.VMEM(w_rec.shape, jnp.bfloat16),
            pltpu.VMEM(w_in.shape, jnp.bfloat16),
            pltpu.VMEM((rows, bw), jnp.bfloat16),
            pltpu.VMEM((NC,) + prior, jnp.bfloat16),
            pltpu.SemaphoreType.DMA((3 + NC * IMAG,)),
        ],
        compiler_params=pltpu.CompilerParams(vmem_limit_bytes=24 * MIB),
        cost_estimate=pl.CostEstimate(
            flops=2 * IMAG * rows * bw * (3 * bw + w_in.shape[1]),
            bytes_accessed=2 * (w_rec.size + w_in.size) + 24 * rows * bw,
            transcendentals=6 * rows * bw,
        ),
        name="gru",
    )(place, *[pltpu.with_memory_space_constraint(value, pltpu.HBM) for value in (deter, w_rec, w_in)], sums)


def tail_kernel(me_ref, parts_ref, mine_ref, other_ref, picked_ref, var_ref, mask_ref, log_ref):
    pre = parts_ref[0].astype(jnp.float32)
    for i in range(1, parts_ref.shape[0]):
        pre = pre + parts_ref[i].astype(jnp.float32)
    normed = pre * lax.rsqrt(jnp.mean(pre * pre, axis=1, keepdims=True) + EPS)
    hidden = (silu(normed)).astype(jnp.bfloat16)
    rows = hidden.shape[0]
    cls = lax.broadcasted_iota(jnp.int32, (NX * NC * rows, LANES), 1) % CLASSES

    def within(value, combine):
        step = 1
        while step < CLASSES:
            ahead = pltpu.roll(value, step, 1)
            wrapped = pltpu.roll(value, LANES - CLASSES + step, 1)
            value = combine(value, jnp.where(cls >= step, ahead, wrapped))
            step *= 2
        return value

    x, core = me_ref[0], me_ref[1]
    logits, wants = [], []
    for i in range(NX * NC):
        w_ref = mine_ref if i % NC == 0 else other_ref
        piece = lax.rem(x + NX - i // NC, NX) * NC + (core if i % NC == 0 else 1 - core)
        here = pl.ds(pl.multiple_of(piece * LANES, LANES), LANES)
        logits.append(jnp.dot(hidden, w_ref[i // NC], preferred_element_type=jnp.float32))
        wants.append(jnp.dot(picked_ref[...], var_ref[:, here], preferred_element_type=jnp.float32))
    logits, wants = jnp.concatenate(logits, axis=0), jnp.concatenate(wants, axis=0)
    powers = jnp.exp(logits - within(logits, jnp.maximum))
    probs = 0.99 * (powers / within(powers, jnp.add)) + 0.01 / CLASSES
    terms = jnp.where(cls.astype(jnp.float32) == wants, jnp.log(probs), 0.0)
    total = terms[:rows]
    for i in range(1, NX * NC):
        total = total + terms[i * rows : (i + 1) * rows]
    summed = jnp.where(mask_ref[...] > 0, jnp.sum(total, axis=1, keepdims=True), 0.0)
    lanes = lax.broadcasted_iota(jnp.int32, (rows, LANES), 1)
    diagonal = lax.broadcasted_iota(jnp.int32, (rows, LANES), 0) == lanes
    line = jnp.sum(jnp.where(diagonal, summed, 0.0), axis=0, keepdims=True)
    log_ref[...] = jnp.broadcast_to(line[None], log_ref.shape)


def tail_call(place, parts, mine, other, picked, mask):
    rows = parts.shape[1]
    lane = jnp.arange(LAT, dtype=jnp.int32)
    var_of = (jnp.arange(STOCH, dtype=jnp.int32)[:, None] == lane[None, :] // CLASSES).astype(jnp.bfloat16)
    vmem = pl.BlockSpec(memory_space=pltpu.VMEM)
    return pl.pallas_call(
        tail_kernel,
        in_specs=[pl.BlockSpec(memory_space=pltpu.SMEM)] + [vmem] * 6,
        out_specs=vmem,
        out_shape=jax.ShapeDtypeStruct((NX * NC, 8, LANES), jnp.float32),
        compiler_params=pltpu.CompilerParams(vmem_limit_bytes=32 * MIB),
        cost_estimate=pl.CostEstimate(
            flops=2 * rows * UNITS * LAT, bytes_accessed=8 * mine.size, transcendentals=4 * rows * LAT
        ),
        name="tail",
    )(place, parts, mine, other, picked, var_of, mask)


def body(
    post_deter,
    post_sample,
    samples,
    actions,
    counts,
    w_stoch,
    w_action,
    w_gate,
    w_rec,
    w_prior_in,
    w_prior_out,
    n_dp,
):
    rows = post_deter.shape[0]
    depth = w_gate.shape[0]
    tensor_n = NX * NC
    share = rows // tensor_n
    me = lax.axis_index("tensor")
    place = jnp.stack([me // NC, me % NC]).astype(jnp.int32)

    sent = prep_call(w_gate, post_sample.T, samples.transpose(0, 2, 1), actions)
    came = lax.all_to_all(sent, "dp", 0, 0, axis_index_groups=y_groups(n_dp))
    held = copies_call(came, n_dp // NY, depth, w_gate.shape[1] // NY)
    gate = lax.all_to_all(held, "dp", 0, 0, axis_index_groups=z_groups(n_dp)).reshape(n_dp * depth, -1)

    action_rows = jnp.pad(w_action, ((0, LANES - ACTIONS), (0, 0)))
    mine, other = tensor_gather(jnp.concatenate([w_stoch, action_rows], axis=0))

    features = features_call(place, came, mine, other)
    total = jnp.dot(features.reshape(-1, UNITS), gate, preferred_element_type=jnp.float32).astype(jnp.bfloat16)
    total = total.reshape(NY, IMAG, rows, -1)
    sums = lax.all_to_all(total, "dp", 0, 0, axis_index_groups=y_groups(n_dp))

    w_out_late, _ = lax.optimization_barrier((w_prior_out, features))
    out_mine, out_other = tensor_gather(w_out_late)

    positions = jnp.arange(STEPS, dtype=jnp.int32)
    valid_mask = (positions[None, :] < counts[:, None]).reshape(rows)
    my_mask = lax.dynamic_slice_in_dim(valid_mask, me * share, share, 0).astype(jnp.float32)
    my_mask = jnp.concatenate([my_mask] * IMAG)[:, None]
    picked = lax.dynamic_slice_in_dim(samples, me * share, share, 1)
    picked = picked.reshape(IMAG * share, STOCH).astype(jnp.bfloat16)

    deter, keep, send = gru_call(place, post_deter, w_rec[0], w_prior_in, sums)
    pair = (keep.astype(jnp.float32) + core_swap(send).astype(jnp.float32)).astype(jnp.bfloat16)
    x_groups = [list(range(core, tensor_n, NC)) for core in range(NC)]
    parts = lax.all_to_all(pair.reshape(NX, IMAG * share, UNITS), "tensor", 0, 0, axis_index_groups=x_groups)
    logs = tail_call(place, parts, out_mine, out_other, picked, my_mask)
    logs = lax.all_to_all(logs, "tensor", 0, 0)[:, 0, : IMAG * share]
    log_prob = logs.reshape(tensor_n, IMAG, share).transpose(1, 0, 2).reshape(IMAG, rows)
    deter_out = jnp.where(valid_mask[:, None], deter, jnp.zeros_like(deter))
    return (deter_out, log_prob)


def solution(mesh):
    in_specs = (
        P("dp", "tensor"),
        P("dp", None),
        P(None, "dp", None),
        P(None, "dp"),
        P("dp"),
        P(None, "tensor"),
        P(None, "tensor"),
        P("dp", "tensor"),
        P("tensor", None, None),
        P("tensor", None),
        P(None, "tensor"),
    )
    out_specs = (P("dp", "tensor"), P(None, "dp"))
    whole = functools.partial(body, n_dp=mesh.shape["dp"])
    return jax.shard_map(whole, mesh=mesh, in_specs=in_specs, out_specs=out_specs, check_vma=False)
```
